512 devices in a mesh: zonal: 64 (over x_hi, z, core), merid: 8 (over y, x_lo).
Axes of the slice: x: 4 (x_hi: 2, x_lo: 2; x = x_hi * 2 + x_lo), y: 4, z: 16, core: 2. Of those that a mesh axis runs over, the one named last changes fastest.
Arguments:
- zonal_current_speed: float32 [3, 1024, 8192], P(None, 'merid', 'zonal'), may hold values from -6 to 6
- meridional_current_speed: float32 [3, 1024, 8192], P(None, 'merid', 'zonal'), may hold values from -6 to 6
- thermal_anomaly: float32 [3, 1024, 8192], P(None, 'merid', 'zonal'), may hold values from -6 to 6
- saltiness_anomaly: float32 [3, 1024, 8192], P(None, 'merid', 'zonal'), may hold values from -6 to 6
- zonal_cell_width: float32 [1024, 8192], P('merid', 'zonal'), may hold values from 0.7 to 1.4
- meridional_cell_width: float32 [1024, 8192], P('merid', 'zonal'), may hold values from 0.7 to 1.4
- planetary_rotation_factor: float32 [1024, 8192], P('merid', 'zonal'), may hold values from -1.5 to 1.5
- cell_wet_indicator: int32 [3, 1024, 8192], P(None, 'merid', 'zonal'), may hold values from 0 to 1, as said below
- zonal_edge_wet_indicator: int32 [3, 1024, 8192], P(None, 'merid', 'zonal'), may hold values from 0 to 1, as said below
- meridional_edge_wet_indicator: int32 [3, 1024, 8192], P(None, 'merid', 'zonal'), may hold values from 0 to 1, as said below
- hinge_displacement: int32 [4], replicated, may hold values from 0 to 1
Outputs:
- zonal_out: float32 [3, 1024, 8192], P(None, 'merid', 'zonal')
- merid_out: float32 [3, 1024, 8192], P(None, 'merid', 'zonal')
- temperature_out: float32 [3, 1024, 8192], P(None, 'merid', 'zonal')
- salinity_out: float32 [3, 1024, 8192], P(None, 'merid', 'zonal')
The draws below stay inside these ranges and needn't reach their ends.
Inputs may be any that keep to these rules, and one draw needn't show every extreme that they name: `cell_wet_indicator`: 1 where a cell is sea at that level; a column that is sea at a level is sea at every level above it. `zonal_edge_wet_indicator`: 1 where the cell and its eastern neighbour (periodic) are both sea. `meridional_edge_wet_indicator`: 1 where the cell and its northern neighbour are both sea; on the northernmost row, where the cell is sea.
All inputs are finite; a program needn't handle non-finite values.
Results may differ from the reference program's by a relative error of at most 0.00002.
Values sent between devices are 32-bit elements; how exact they have to be, the bound alone decides.
A program may use at most 128 MiB of HBM per device.

```python
import math
import jax
import jax.numpy as jnp

VERTICAL_COUNT = 3
STEPS = 4
PARALLEL_COUNT = 8192
MERIDIAN_COUNT = 1024


def sea_levels(key):
    depth = jax.random.randint(key, (MERIDIAN_COUNT, PARALLEL_COUNT), 0, VERTICAL_COUNT + 1)
    levels = jnp.arange(VERTICAL_COUNT).reshape(VERTICAL_COUNT, 1, 1)
    return (levels < depth[None, :, :]).astype(jnp.int32)


def draw_cell_wet_indicator(key, part):
    wetness = sea_levels(key)
    return wetness


def draw_zonal_edge_wet_indicator(key, part):
    wetness = sea_levels(key)
    return (wetness * jnp.roll(wetness, -1, axis=2)).astype(jnp.int32)


def draw_meridional_edge_wet_indicator(key, part):
    wetness = sea_levels(key)
    upward = jnp.concatenate([wetness[:, 1:, :], wetness[:, -1:, :]], axis=1)
    return (wetness * upward).astype(jnp.int32)


def draw_hinge_displacement(key, part):
    key = jax.random.fold_in(key, 7)
    leading = jax.random.randint(key, (1,), 0, 2)
    others = jax.random.randint(jax.random.fold_in(key, 1), (2,), 0, 2)
    return jnp.concatenate([leading, 1 - leading, others]).astype(jnp.int32)


def block_levels(own_key, extent, cuts, smallest, top_value):
    factor_of = 1.0
    for axis_at, shards_of in cuts:
        heights = jax.random.uniform(jax.random.fold_in(jax.random.fold_in(own_key, 6), axis_at), (shards_of,), jnp.float32, smallest / len(cuts), top_value / len(cuts))
        factor_of = factor_of * jnp.repeat(jnp.exp(heights), extent[axis_at] // shards_of).reshape((-1,) + (1,) * (len(extent) - 1 - axis_at))
    return factor_of


def normal_values(stream_key, shape, deviation, reach, cuts=(), held_as=jnp.bfloat16):
    gain = block_levels(stream_key, shape, cuts, -0.22, 0.18) if cuts else 1.0
    entries = jax.random.normal(stream_key, shape, jnp.float32) * deviation * gain
    return jnp.minimum(jnp.maximum(entries, -reach), reach).astype(held_as)


def setup_inputs(seed: int = 0) -> dict:
    arg_keys = jax.random.split(jax.random.key(seed), 12)
    return {
        "zonal_current_speed": normal_values(arg_keys[0], (VERTICAL_COUNT, MERIDIAN_COUNT, PARALLEL_COUNT), 1.0, 6.0, ((1, 8), (2, 64)), jnp.float32),
        "meridional_current_speed": normal_values(arg_keys[1], (VERTICAL_COUNT, MERIDIAN_COUNT, PARALLEL_COUNT), 1.0, 6.0, ((1, 8), (2, 64)), jnp.float32),
        "thermal_anomaly": normal_values(arg_keys[2], (VERTICAL_COUNT, MERIDIAN_COUNT, PARALLEL_COUNT), 1.0, 6.0, ((1, 8), (2, 64)), jnp.float32),
        "saltiness_anomaly": normal_values(arg_keys[3], (VERTICAL_COUNT, MERIDIAN_COUNT, PARALLEL_COUNT), 1.0, 6.0, ((1, 8), (2, 64)), jnp.float32),
        "zonal_cell_width": jnp.clip(jnp.exp(math.log(1.4) - 0.6931472 * jax.random.uniform(arg_keys[4], (MERIDIAN_COUNT, PARALLEL_COUNT), jnp.float32) ** block_levels(arg_keys[4], (MERIDIAN_COUNT, PARALLEL_COUNT), ((0, 8), (1, 64)), -0.2, 0.2)), 0.7, 1.4),
        "meridional_cell_width": jnp.clip(jnp.exp(math.log(1.4) - 0.6931472 * jax.random.uniform(arg_keys[5], (MERIDIAN_COUNT, PARALLEL_COUNT), jnp.float32) ** block_levels(arg_keys[5], (MERIDIAN_COUNT, PARALLEL_COUNT), ((0, 8), (1, 64)), -0.2, 0.2)), 0.7, 1.4),
        "planetary_rotation_factor": jnp.clip(jax.random.uniform(arg_keys[6], (MERIDIAN_COUNT, PARALLEL_COUNT), jnp.float32, -1.5, 1.5) * block_levels(arg_keys[6], (MERIDIAN_COUNT, PARALLEL_COUNT), ((0, 8), (1, 64)), -0.4, 0.0), -1.5, 1.5),
        "cell_wet_indicator": draw_cell_wet_indicator(jax.random.fold_in(arg_keys[11], 71), 0),
        "zonal_edge_wet_indicator": draw_zonal_edge_wet_indicator(jax.random.fold_in(arg_keys[11], 71), 0),
        "meridional_edge_wet_indicator": draw_meridional_edge_wet_indicator(jax.random.fold_in(arg_keys[11], 71), 0),
        "hinge_displacement": draw_hinge_displacement(jax.random.fold_in(arg_keys[11], 71), 0),
    }


TIME_STEP = 0.25
VISCOSITY = 0.25
DIFFUSIVITY = 0.25


def water_column_weight(thermal_anomaly, saltiness_anomaly):
    gravity_density_term = 0.5 * thermal_anomaly - 0.4 * saltiness_anomaly
    return jnp.cumsum(gravity_density_term, axis=0) - 0.5 * gravity_density_term


def momentum_fluxes(evolving_state_quantities, eastern, western, northern, southern, zonal_cell_width, meridional_cell_width, planetary_rotation_factor, zonal_float, merid_float):
    zonal_vel = evolving_state_quantities[0]
    merid_vel = evolving_state_quantities[1]
    pressure_here = water_column_weight(evolving_state_quantities[2], evolving_state_quantities[3])

    def laplace(which_field):
        middle = evolving_state_quantities[which_field]
        return (eastern[which_field] - 2.0 * middle + western[which_field]) / zonal_cell_width ** 2 + (northern[which_field] - 2.0 * middle + southern[which_field]) / meridional_cell_width ** 2

    zonal_new = zonal_float * (zonal_vel + TIME_STEP * (planetary_rotation_factor * 0.5 * (merid_vel + southern[1]) - (water_column_weight(eastern[2], eastern[3]) - pressure_here) / zonal_cell_width + VISCOSITY * laplace(0)))
    merid_new = merid_float * (merid_vel + TIME_STEP * (-planetary_rotation_factor * 0.5 * (zonal_vel + western[0]) - (water_column_weight(northern[2], northern[3]) - pressure_here) / meridional_cell_width + VISCOSITY * laplace(1)))
    tracers = evolving_state_quantities[2:]
    flux_east = zonal_float * meridional_cell_width * (zonal_new * 0.5 * (tracers + eastern[2:]) - DIFFUSIVITY * (eastern[2:] - tracers) / zonal_cell_width)
    flux_north = merid_float * zonal_cell_width * (merid_new * 0.5 * (tracers + northern[2:]) - DIFFUSIVITY * (northern[2:] - tracers) / meridional_cell_width)
    return zonal_new, merid_new, flux_east, flux_north


def reference(zonal_current_speed, meridional_current_speed, thermal_anomaly, saltiness_anomaly, zonal_cell_width, meridional_cell_width, planetary_rotation_factor, cell_wet_indicator, zonal_edge_wet_indicator, meridional_edge_wet_indicator, hinge_displacement):
    cell_float = cell_wet_indicator.astype(jnp.float32)
    zonal_float = zonal_edge_wet_indicator.astype(jnp.float32)
    merid_float = meridional_edge_wet_indicator.astype(jnp.float32)
    scalar_wet_indicators = jnp.stack([zonal_float, merid_float, cell_float, cell_float])
    evolving_state_quantities = jnp.stack([zonal_current_speed, meridional_current_speed, thermal_anomaly, saltiness_anomaly]) * scalar_wet_indicators
    offsets = hinge_displacement.reshape(4, 1, 1)
    breadth = evolving_state_quantities.shape[3]
    columns = (breadth - 1 - jnp.arange(breadth, dtype=jnp.int32).reshape(1, 1, breadth) + offsets) % breadth
    columns = jnp.broadcast_to(columns, (4, VERTICAL_COUNT, breadth)).astype(jnp.int32)
    field_signs = jnp.array([-1.0, -1.0, 1.0, 1.0], jnp.float32).reshape(4, 1, 1)
    for substep in range(STEPS):
        source_rows = jnp.where(offsets == 0, evolving_state_quantities[:, :, -1, :], evolving_state_quantities[:, :, -2, :])
        ghost_row = field_signs * jnp.take_along_axis(source_rows, columns, axis=2)
        northern = jnp.concatenate([evolving_state_quantities[:, :, 1:, :], ghost_row[:, :, None, :]], axis=2)
        southern = jnp.concatenate([jnp.zeros_like(evolving_state_quantities[:, :, :1, :]), evolving_state_quantities[:, :, :-1, :]], axis=2)
        eastern = jnp.roll(evolving_state_quantities, -1, axis=3)
        western = jnp.roll(evolving_state_quantities, 1, axis=3)
        zonal_new, merid_new, flux_east, flux_north = momentum_fluxes(evolving_state_quantities, eastern, western, northern, southern, zonal_cell_width, meridional_cell_width, planetary_rotation_factor, zonal_float, merid_float)
        flux_west = jnp.roll(flux_east, 1, axis=3)
        flux_south = jnp.concatenate([jnp.zeros_like(flux_north[:, :, :1, :]), flux_north[:, :, :-1, :]], axis=2)
        tracers = cell_float * (evolving_state_quantities[2:] - TIME_STEP * (flux_east - flux_west + flux_north - flux_south) / (zonal_cell_width * meridional_cell_width))
        evolving_state_quantities = jnp.concatenate([zonal_new[None], merid_new[None], tracers], axis=0)
    return evolving_state_quantities[0], evolving_state_quantities[1], evolving_state_quantities[2], evolving_state_quantities[3]
```

```python
import jax
import jax.numpy as jnp
from jax import lax
from jax.experimental import pallas as pl
from jax.experimental.pallas import tpu as pltpu
from jax.sharding import PartitionSpec as P

STEPS = 4
LEVELS = 3
TIME_STEP = 0.25
VISCOSITY = 0.25
DIFFUSIVITY = 0.25

MESH = pl.DeviceIdType.MESH

N = 128
OFF = 16
ROWS = 160
CHUNK = 32
WIDE = 5
SLIM = 4
GROUP = 42
WEST_OWN = WIDE
EAST_FIRST = WIDE + 9
EAST_HALO = EAST_FIRST + 9
CA, CB, CC, CF, CGX, CGY, CHX, CHY, CDX, CDY, CK = range(11)
SIGN = (-1.0, -1.0, 1.0, 1.0)


def turned(x, shift):
    if isinstance(shift, int):
        shift %= N
        if shift == 0:
            return x
    return pltpu.roll(x, shift, 1)


def lanes(shape):
    return lax.broadcasted_iota(jnp.int32, shape, 1)


def coefficients(hx, hy, f):
    rx = 1.0 / hx
    ry = 1.0 / hy
    a = (TIME_STEP * VISCOSITY) * rx * rx
    b = (TIME_STEP * VISCOSITY) * ry * ry
    return (
        a,
        b,
        1.0 - 2.0 * (a + b),
        (0.5 * TIME_STEP) * f,
        TIME_STEP * rx,
        TIME_STEP * ry,
        0.5 * hx,
        0.5 * hy,
        DIFFUSIVITY * hy * rx,
        DIFFUSIVITY * hx * ry,
        TIME_STEP * rx * ry,
    )


def weights(t, s, lane):
    half = [0.25 * a - 0.2 * b for a, b in zip(t, s)]
    if len(half) == 1:
        one = jnp.where(lane >= GROUP, turned(half[0], GROUP), 0.0)
        two = jnp.where(lane >= 2 * GROUP, turned(half[0], 2 * GROUP), 0.0)
        return [half[0] + 2.0 * (one + two)]
    out = [half[0]]
    for k in range(1, LEVELS):
        out.append(out[-1] + (half[k - 1] + half[k]))
    return out


def advance(load, coef, masks, keep, east, west, rows, levels):
    lane = lanes((rows, N))
    span = range(levels)
    t = [load(2, k, 0) for k in span]
    s = [load(3, k, 0) for k in span]
    tn = [load(2, k, 1) for k in span]
    sn = [load(3, k, 1) for k in span]
    p = weights(t, s, lane)
    pn = weights(tn, sn, lane)
    for k in span:
        u, v = load(0, k, 0), load(1, k, 0)
        us, vs = load(0, k, -1), load(1, k, -1)
        uw = turned(u, west)
        mu, mv, mc = masks(k)
        un = mu * (
            coef(CC) * u
            + coef(CA) * (turned(u, east) + uw)
            + coef(CB) * (load(0, k, 1) + us)
            + coef(CF) * (v + vs)
            - coef(CGX) * (turned(p[k], east) - p[k])
        )
        vn = mv * (
            coef(CC) * v
            + coef(CA) * (turned(v, east) + turned(v, west))
            + coef(CB) * (load(1, k, 1) + vs)
            - coef(CF) * (u + uw)
            - coef(CGY) * (pn[k] - p[k])
        )
        keep(0, k, un)
        keep(1, k, vn)
        q, d = coef(CHY) * un, coef(CDX) * mu
        qp, qm = q + d, q - d
        r, e = coef(CHX) * vn, coef(CDY) * mv
        rp, rm = r + e, r - e
        scale = mc * coef(CK)
        for which, c, cn in ((2, t[k], tn[k]), (3, s[k], sn[k])):
            fe = qp * c + qm * turned(c, east)
            fn = rp * c + rm * cn
            below = keep(which + 2, k, fn)
            keep(which, k, c - scale * ((fe - turned(fe, west)) + (fn - below)))


def pack_wide(plane, rows):
    lane = lanes((rows, N))
    out = None
    for k in range(LEVELS):
        for g in range(8):
            first = GROUP * k + WIDE * g
            part = turned(plane(g, k), first - (N - WIDE))
            out = part if out is None else jnp.where(lane >= first, part, out)
    return out


def pack_slim(plane, rows):
    lane = lanes((rows, N))
    out = None
    for k in range(LEVELS):
        for g in range(8):
            first = GROUP * k + SLIM * g
            part = turned(plane(g, k), first)
            out = part if out is None else jnp.where(lane >= first, part, out)
    return out


def pack_own(plane, g, rows):
    lane = lanes((rows, N))
    out = None
    for k in range(LEVELS):
        x = plane(g, k)
        for first, column in ((GROUP * k + WEST_OWN, 0), (GROUP * k + EAST_FIRST, N - 9)):
            part = turned(x, first - column)
            out = part if out is None else jnp.where(lane >= first, part, out)
    return out


def merge_halo(own, wide, slim, g, rows):
    lane = lanes((rows, N))
    place = lane - jnp.where(lane >= 2 * GROUP, 2 * GROUP, jnp.where(lane >= GROUP, GROUP, 0))
    own = jnp.where(place < WIDE, turned(wide, -WIDE * g), own)
    east = (place >= EAST_HALO) & (place < EAST_HALO + SLIM)
    return jnp.where(east, turned(slim, EAST_HALO - SLIM * g), own)


def flipped(x):
    lane = lanes(x.shape)
    for bit in (64, 32, 16, 8, 4, 2, 1):
        if bit == 64:
            x = turned(x, 64)
        else:
            x = jnp.where((lane & bit) != 0, turned(x, bit), turned(x, -bit))
    return x


def kernel(
    hinge,
    u_ref,
    v_ref,
    t_ref,
    s_ref,
    hx_ref,
    hy_ref,
    f_ref,
    cell_ref,
    zonal_ref,
    merid_ref,
    u_out,
    v_out,
    t_out,
    s_out,
    main,
    edge,
    top_main,
    top_edge,
    flux_main,
    flux_edge,
    mask_main,
    mask_edge,
    mask_top_main,
    mask_top_edge,
    metric_main,
    metric_top,
    metric_edge,
    coef_main,
    coef_edge,
    coef_top_main,
    coef_top_edge,
    east_buf,
    west_buf,
    north_buf,
    south_buf,
    fold_tile,
    fold_west,
    fold_east,
    from_west,
    from_east,
    from_south,
    from_north,
    from_fold,
    from_corner,
    send_sem,
    recv_sem,
    local_sem,
):
    nz, nm = lax.axis_size("zonal"), lax.axis_size("merid")
    z, m = lax.axis_index("zonal"), lax.axis_index("merid")
    east_z, west_z = lax.rem(z + 1, nz), lax.rem(z + nz - 1, nz)
    fold_z = nz - 1 - z
    fold_up, fold_down = lax.rem(fold_z + 1, nz), lax.rem(fold_z + nz - 1, nz)
    top, bottom = m == nm - 1, m == 0
    inner = jnp.logical_not(top)
    raised = jnp.logical_not(bottom)

    def at(zz, mm):
        return {"zonal": zz, "merid": mm}

    barrier = pltpu.get_barrier_semaphore()

    def hail(zz, mm):
        pl.semaphore_signal(barrier, inc=1, device_id=at(zz, mm), device_id_type=MESH)

    hail(east_z, m)
    hail(west_z, m)

    @pl.when(raised)
    def _():
        for zz in (west_z, z, east_z):
            hail(zz, m - 1)

    @pl.when(inner)
    def _():
        for zz in (west_z, z, east_z):
            hail(zz, m + 1)

    @pl.when(top)
    def _():
        hail(fold_z, m)

        @pl.when(fold_up != z)
        def _():
            hail(fold_up, m)

        @pl.when(fold_down != z)
        def _():
            hail(fold_down, m)

    fields = (u_ref, v_ref, t_ref, s_ref)

    def fill(i, carry):
        here = pl.ds(pl.multiple_of(i * CHUNK, CHUNK), CHUNK)
        there = pl.ds(pl.multiple_of(OFF + i * CHUNK, 8), CHUNK)
        for k in range(LEVELS):
            mu = zonal_ref[k, here, :].astype(jnp.float32)
            mv = merid_ref[k, here, :].astype(jnp.float32)
            mc = cell_ref[k, here, :].astype(jnp.float32)
            mask_main[k, there, :] = mu
            mask_main[3 + k, there, :] = mv
            mask_main[6 + k, there, :] = mc
            for g, ref in enumerate(fields):
                main[0, 3 * g + k, there, :] = ref[k, here, :] * (mu, mv, mc, mc)[g]
        return carry

    lax.fori_loop(0, N // CHUNK, fill, 0)

    def plane_at(start, rows):
        def plane(g, k):
            if g < 4:
                return main[0, 3 * g + k, pl.ds(OFF + start, rows), :]
            if g == 4:
                return mask_main[6 + k, pl.ds(OFF + start, rows), :]
            return (hx_ref, hy_ref, f_ref)[g - 5][pl.ds(start, rows), :]

        return plane

    def number(g, k):
        return 3 * g + k if g < 5 else 15 + g - 5

    every = [(g, k) for g in range(5) for k in range(LEVELS)] + [(g, 0) for g in (5, 6, 7)]

    @pl.when(inner)
    def _():
        for g, k in every:
            i = number(g, k)
            north_buf[pl.ds(WIDE * i, WIDE), :] = plane_at(N - WIDE, WIDE)(g, k)

    @pl.when(top)
    def _():
        plane = plane_at(N - 8, 8)
        for g, k in every:
            i = number(g, k)
            tile = flipped(plane(g, k))
            fold_tile[i, :, :] = tile
            north_buf[pl.ds(WIDE * i, WIDE), :] = tile[8 - WIDE :, :]
            if g == 1:
                north_buf[pl.ds(90 + k, 1), :] = tile[2:3, :]

        def mirrored(g, k):
            return fold_tile[number(g, k)]

        fold_west[...] = pack_wide(mirrored, 8)
        fold_east[...] = pack_slim(mirrored, 8)

    def copy(src, dst, slot, zz, mm):
        return pltpu.make_async_remote_copy(
            src_ref=src,
            dst_ref=dst,
            send_sem=send_sem.at[slot],
            recv_sem=recv_sem.at[slot],
            device_id=at(zz, mm),
            device_id_type=MESH,
        )

    corner = lambda i: from_corner.at[i]
    low, high = pl.ds(0, 8), pl.ds(N - 8, 8)
    to_east = copy(east_buf, from_west, 0, east_z, m)
    to_west = copy(west_buf, from_east, 1, west_z, m)
    to_north = copy(north_buf, from_south, 2, z, m + 1)
    to_south = copy(south_buf, from_north, 3, z, m - 1)
    to_fold = copy(north_buf, from_fold, 4, fold_z, m)
    to_ne = copy(east_buf.at[high], corner(0), 5, east_z, m + 1)
    to_nw = copy(west_buf.at[high], corner(1), 6, west_z, m + 1)
    to_se = copy(east_buf.at[low], corner(2), 7, east_z, m - 1)
    to_sw = copy(west_buf.at[low], corner(3), 8, west_z, m - 1)
    to_fold_up = copy(fold_west, corner(2), 9, fold_up, m)
    to_fold_down = copy(fold_east, corner(3), 10, fold_down, m)
    keep_fold_up = pltpu.make_async_copy(fold_west, corner(2), local_sem.at[0])
    keep_fold_down = pltpu.make_async_copy(fold_east, corner(3), local_sem.at[1])

    same = jnp.where(fold_up == z, 1, 0) + jnp.where(fold_down == z, 1, 0)
    pl.semaphore_wait(barrier, 2 + jnp.where(bottom, 0, 3) + 3 - jnp.where(top, same, 0))

    @pl.when(top)
    def _():
        to_fold.start()

        @pl.when(fold_up != z)
        def _():
            to_fold_up.start()

        @pl.when(fold_up == z)
        def _():
            keep_fold_up.start()

        @pl.when(fold_down != z)
        def _():
            to_fold_down.start()

        @pl.when(fold_down == z)
        def _():
            keep_fold_down.start()

    @pl.when(inner)
    def _():
        to_north.start()

    def pack(i, carry):
        first = pl.multiple_of(i * CHUNK, CHUNK)
        plane = plane_at(first, CHUNK)
        east_buf[pl.ds(first, CHUNK), :] = pack_wide(plane, CHUNK)
        west_buf[pl.ds(first, CHUNK), :] = pack_slim(plane, CHUNK)
        return carry

    lax.fori_loop(0, N // CHUNK, pack, 0)
    to_east.start()
    to_west.start()

    @pl.when(inner)
    def _():
        to_ne.start()
        to_nw.start()

    for g, k in every:
        south_buf[pl.ds(SLIM * number(g, k), SLIM), :] = plane_at(0, SLIM)(g, k)

    @pl.when(raised)
    def _():
        to_south.start()
        to_se.start()
        to_sw.start()

    def prepare(i, carry):
        first = pl.multiple_of(i * CHUNK, CHUNK)
        here = pl.ds(first, CHUNK)
        there = pl.ds(pl.multiple_of(OFF + i * CHUNK, 8), CHUNK)
        for c, x in enumerate(coefficients(hx_ref[here, :], hy_ref[here, :], f_ref[here, :])):
            coef_main[c, there, :] = x
        plane = plane_at(first, CHUNK)
        for g in range(8):
            x = pack_own(plane, g, CHUNK)
            if g < 4:
                edge[0, g, there, :] = x
            elif g == 4:
                mask_edge[2, there, :] = x
            else:
                metric_edge[g - 5, there, :] = x
        return carry

    lax.fori_loop(0, N // CHUNK, prepare, 0)

    def step_rows(n, start, rows, state, flux, mask, coef, levels, align):
        def at_row(dj):
            first = OFF + start + dj
            if dj == 0 and align:
                first = pl.multiple_of(first, 8)
            return pl.ds(first, rows)

        def load(g, k, dj):
            return state[n, levels * g + k, at_row(dj), :]

        def keep(g, k, x):
            if g < 4:
                state[n + 1, levels * g + k, at_row(0), :] = x
                return None
            flux[n, levels * (g - 4) + k, at_row(0), :] = x
            return flux[n, levels * (g - 4) + k, at_row(-1), :]

        def masks(k):
            return [mask[levels * i + k, at_row(0), :] for i in range(3)]

        advance(load, lambda c: coef[c, at_row(0), :], masks, keep, N - 1, 1, rows, levels)

    def interior(n, carry):
        def chunk(i, inside):
            step_rows(n, i * CHUNK, CHUNK, main, flux_main, mask_main, coef_main, LEVELS, True)
            return inside

        return lax.fori_loop(0, N // CHUNK, chunk, carry)

    lax.fori_loop(0, STEPS, interior, 0)

    halo = pl.ds(OFF - 8, 8)

    @pl.when(raised)
    def _():
        to_north.wait_recv()
        to_ne.wait_recv()
        to_nw.wait_recv()
        last = pl.ds(OFF - WIDE, WIDE)
        for g, k in every:
            x = from_south[pl.ds(WIDE * number(g, k), WIDE), :]
            if g < 4:
                main[0, 3 * g + k, last, :] = x
            elif g == 4:
                mask_main[6 + k, last, :] = x
            else:
                metric_main[g - 5, pl.ds(8 - WIDE, WIDE), :] = x

    @pl.when(bottom)
    def _():
        zero = jnp.zeros((8, N), jnp.float32)
        for g, k in every:
            if g < 4:
                main[0, 3 * g + k, halo, :] = zero
            elif g == 4:
                mask_main[6 + k, halo, :] = zero
            else:
                metric_main[g - 5, :, :] = zero + 1.0
        for i in (0, 1):
            from_corner[i, :, :] = zero

    for k in range(LEVELS):
        mc = mask_main[6 + k, halo, :]
        mask_main[k, halo, :] = mc * turned(mc, N - 1)
        mask_main[3 + k, halo, :] = mc * mask_main[6 + k, pl.ds(OFF - 7, 8), :]
    for c, x in enumerate(coefficients(metric_main[0], metric_main[1], metric_main[2])):
        coef_main[c, halo, :] = x

    to_east.wait_recv()
    to_west.wait_recv()

    def edge_keep(g, rows, x, offset=0):
        if g < 4:
            edge[0, g, rows, :] = x
        elif g == 4:
            mask_edge[2, rows, :] = x
        else:
            metric_edge[g - 5, rows, :] = x

    def south_plane(g, k):
        if g < 4:
            return main[0, 3 * g + k, halo, :]
        if g == 4:
            return mask_main[6 + k, halo, :]
        return metric_main[g - 5, :, :]

    for g in range(8):
        x = pack_own(south_plane, g, 8)
        x = merge_halo(x, from_corner[0], from_corner[1], g, 8)
        if g in (5, 6):
            x = jnp.where(bottom, 1.0, x)
        edge_keep(g, halo, x)

    def unpack(i, carry):
        first = pl.multiple_of(i * CHUNK, CHUNK)
        there = pl.ds(pl.multiple_of(OFF + i * CHUNK, 8), CHUNK)
        wide = from_west[pl.ds(first, CHUNK), :]
        slim = from_east[pl.ds(first, CHUNK), :]
        for g in range(8):
            if g < 4:
                x = edge[0, g, there, :]
            elif g == 4:
                x = mask_edge[2, there, :]
            else:
                x = metric_edge[g - 5, there, :]
            edge_keep(g, there, merge_halo(x, wide, slim, g, CHUNK))
        return carry

    lax.fori_loop(0, N // CHUNK, unpack, 0)

    def edge_masks(start, rows):
        there = pl.ds(start, rows)
        mc = mask_edge[2, there, :]
        mask_edge[0, there, :] = mc * turned(mc, N - 1)
        mask_edge[1, there, :] = mc * mask_edge[2, pl.ds(start + 1, rows), :]

    def edge_ready(start, rows):
        there = pl.ds(start, rows)
        for c, x in enumerate(
            coefficients(metric_edge[0, there, :], metric_edge[1, there, :], metric_edge[2, there, :])
        ):
            coef_edge[c, there, :] = x

    edge_masks(OFF - 8, 8)
    edge_ready(OFF - 8, 8)

    def ready(i, carry):
        edge_masks(OFF + i * CHUNK, CHUNK)
        edge_ready(OFF + i * CHUNK, CHUNK)
        return carry

    lax.fori_loop(0, N // CHUNK, ready, 0)

    def south_side(n, carry):
        step_rows(n, n - WIDE, 8, main, flux_main, mask_main, coef_main, LEVELS, False)
        step_rows(n, -8, 8, edge, flux_edge, mask_edge, coef_edge, 1, True)

        def chunk(i, inside):
            step_rows(n, i * CHUNK, CHUNK, edge, flux_edge, mask_edge, coef_edge, 1, True)
            return inside

        return lax.fori_loop(0, N // CHUNK, chunk, carry)

    lax.fori_loop(0, STEPS, south_side, 0)

    strip = pl.ds(0, 8)
    for g, k in every:
        if g < 4:
            top_main[3 * g + k, strip, :] = jnp.zeros((8, N), jnp.float32)
        elif g == 4:
            mask_top_main[6 + k, strip, :] = jnp.zeros((8, N), jnp.float32)
        else:
            metric_top[g - 5, :, :] = jnp.ones((8, N), jnp.float32)

    def top_keep(g, k, first, x):
        rows = pl.ds(first, x.shape[0])
        if g < 4:
            top_main[3 * g + k, rows, :] = x
        elif g == 4:
            mask_top_main[6 + k, rows, :] = x
        else:
            metric_top[g - 5, pl.ds(first, x.shape[0]), :] = x

    @pl.when(inner)
    def _():
        to_south.wait_recv()
        to_se.wait_recv()
        to_sw.wait_recv()
        for g, k in every:
            top_keep(g, k, 0, from_north[pl.ds(SLIM * number(g, k), SLIM), :])

    @pl.when(top)
    def _():
        to_fold.wait_recv()

        @pl.when(fold_up != z)
        def _():
            to_fold_up.wait_recv()

        @pl.when(fold_up == z)
        def _():
            keep_fold_up.wait()

        @pl.when(fold_down != z)
        def _():
            to_fold_down.wait_recv()

        @pl.when(fold_down == z)
        def _():
            keep_fold_down.wait()

        for g, k in every:
            top_keep(g, k, 8 - WIDE, from_fold[pl.ds(WIDE * number(g, k), WIDE), :])
        for k in range(LEVELS):
            top_keep(1, k, 2, from_fold[pl.ds(90 + k, 1), :])

    east = jnp.where(top, 1, N - 1)
    west = jnp.where(top, N - 1, 1)

    def top_plane(g, k):
        if g < 4:
            return top_main[3 * g + k, strip, :]
        if g == 4:
            return mask_top_main[6 + k, strip, :]
        return metric_top[g - 5, :, :]

    edge_metric = []
    for g in range(8):
        x = merge_halo(pack_own(top_plane, g, 8), from_corner[2], from_corner[3], g, 8)
        if g < 4:
            top_edge[g, strip, :] = x
        elif g == 4:
            mask_top_edge[2, strip, :] = x
        else:
            edge_metric.append(x)
    for c, x in enumerate(coefficients(*edge_metric)):
        coef_top_edge[c, :, :] = x
    for c, x in enumerate(coefficients(metric_top[0], metric_top[1], metric_top[2])):
        coef_top_main[c, :, :] = x
    row = lax.broadcasted_iota(jnp.int32, (8, N), 0)
    mc = mask_edge[2, pl.ds(OFF + N - 8, 8), :]
    over = jnp.where(top, 1.0, pltpu.roll(mask_top_edge[2, strip, :], 7, 0))
    mask_edge[1, pl.ds(OFF + N - 8, 8), :] = mc * jnp.where(row == 7, over, pltpu.roll(mc, 7, 0))
    for mask, levels in ((mask_top_main, LEVELS), (mask_top_edge, 1)):
        for k in range(levels):
            mc = mask[2 * levels + k, strip, :]
            mask[k, strip, :] = mc * turned(mc, east)
            mask[levels + k, strip, :] = mc * jnp.where(row == 7, 1.0, pltpu.roll(mc, 7, 0))

    plain = [jnp.full((1, N), hinge[g], jnp.int32) == 0 for g in range(4)]

    first_row, last_row = row == 0, row == 7
    brim, under = pl.ds(OFF + N - 8, 8), pl.ds(OFF + N - 16, 8)

    def up(x):
        return pltpu.roll(x, 7, 0)

    def down(x):
        return pltpu.roll(x, 1, 0)

    kinds = (
        (LEVELS, main, flux_main, mask_main, mask_top_main, coef_main, coef_top_main),
        (1, edge, flux_edge, mask_edge, mask_top_edge, coef_edge, coef_top_edge),
    )

    def north_side(n, carry):
        after = []
        for (levels, state, flux, mask, mask_beyond, coef, coef_beyond), (below, beyond) in zip(
            kinds, carry
        ):
            new_below, new_beyond, fluxes = [None] * len(below), [None] * len(beyond), {}

            def load_below(g, k, dj):
                c, z = below[levels * g + k], beyond[levels * g + k]
                if dj == 0:
                    return c
                if dj < 0:
                    return jnp.where(first_row, down(state[n, levels * g + k, under, :]), down(c))
                ghost = SIGN[g] * jnp.where(plain[g], z, down(turned(z, 1)))
                return jnp.where(last_row, jnp.where(top, ghost, up(z)), up(c))

            def load_beyond(g, k, dj):
                c, z = below[levels * g + k], beyond[levels * g + k]
                if dj == 0:
                    return z
                if dj < 0:
                    return jnp.where(first_row, down(c), down(z))
                ghost = SIGN[g] * jnp.where(plain[g], c, down(turned(c, N - 1)))
                return jnp.where(last_row, ghost, up(z))

            def keep_below(g, k, x):
                if g < 4:
                    new_below[levels * g + k] = x
                    return None
                fluxes[g, k] = down(x)
                return jnp.where(
                    first_row, down(flux[n, levels * (g - 4) + k, under, :]), fluxes[g, k]
                )

            def keep_beyond(g, k, x):
                if g < 4:
                    new_beyond[levels * g + k] = x
                    return None
                return jnp.where(first_row, fluxes[g, k], down(x))

            def masks(k):
                return [mask[levels * i + k, brim, :] for i in range(3)]

            def masks_beyond(k):
                return [mask_beyond[levels * i + k, strip, :] for i in range(3)]

            advance(load_below, lambda c: coef[c, brim, :], masks, keep_below, N - 1, 1, 8, levels)
            advance(
                load_beyond, lambda c: coef_beyond[c], masks_beyond, keep_beyond, east, west, 8, levels
            )
            after.append((tuple(new_below), tuple(new_beyond)))
        return tuple(after)

    start = tuple(
        (
            tuple(state[0, i, brim, :] for i in range(4 * levels)),
            tuple(beyond[i, strip, :] for i in range(4 * levels)),
        )
        for levels, state, beyond in ((LEVELS, main, top_main), (1, edge, top_edge))
    )
    done = lax.fori_loop(0, STEPS, north_side, start)
    for state, (below, _) in zip((main, edge), done):
        for i, x in enumerate(below):
            state[STEPS, i, brim, :] = x

    def finish(i, carry):
        here = pl.ds(pl.multiple_of(i * CHUNK, CHUNK), CHUNK)
        there = pl.ds(pl.multiple_of(OFF + i * CHUNK, 8), CHUNK)
        lane = lanes((CHUNK, N))
        for g, ref in enumerate((u_out, v_out, t_out, s_out)):
            x = edge[STEPS, g, there, :]
            for k in range(LEVELS):
                y = main[STEPS, 3 * g + k, there, :]
                y = jnp.where(lane < WIDE, turned(x, -(GROUP * k + WEST_OWN)), y)
                sides = turned(x, N - SLIM - (GROUP * k + EAST_HALO - SLIM))
                ref[k, here, :] = jnp.where(lane >= N - SLIM, sides, y)
        return carry

    lax.fori_loop(0, N // CHUNK, finish, 0)

    to_east.wait_send()
    to_west.wait_send()

    @pl.when(inner)
    def _():
        for c in (to_north, to_ne, to_nw):
            c.wait_send()

    @pl.when(raised)
    def _():
        for c in (to_south, to_se, to_sw):
            c.wait_send()

    @pl.when(top)
    def _():
        to_fold.wait_send()

        @pl.when(fold_up != z)
        def _():
            to_fold_up.wait_send()

        @pl.when(fold_down != z)
        def _():
            to_fold_down.wait_send()


def per_device(u, v, t, s, hx, hy, f, cell, zonal, merid, hinge):
    def buf(*shape):
        return pltpu.VMEM(shape + (N,), jnp.float32)

    vmem = pl.BlockSpec(memory_space=pltpu.VMEM)
    shape = jax.ShapeDtypeStruct((LEVELS, N, N), jnp.float32)
    return pl.pallas_call(
        kernel,
        out_shape=(shape,) * 4,
        in_specs=[pl.BlockSpec(memory_space=pltpu.SMEM)] + [vmem] * 10,
        out_specs=(vmem,) * 4,
        scratch_shapes=[
            buf(5, 12, ROWS),
            buf(5, 4, ROWS),
            buf(12, 8),
            buf(4, 8),
            buf(4, 6, ROWS),
            buf(4, 2, ROWS),
            buf(9, ROWS),
            buf(3, ROWS),
            buf(9, 8),
            buf(3, 8),
            buf(3, 8),
            buf(3, 8),
            buf(3, ROWS),
            buf(11, ROWS),
            buf(11, ROWS),
            buf(11, 8),
            buf(11, 8),
            buf(N),
            buf(N),
            buf(96),
            buf(72),
            buf(18, 8),
            buf(8),
            buf(8),
            buf(N),
            buf(N),
            buf(96),
            buf(72),
            buf(96),
            buf(4, 8),
            pltpu.SemaphoreType.DMA((11,)),
            pltpu.SemaphoreType.DMA((11,)),
            pltpu.SemaphoreType.DMA((2,)),
        ],
        compiler_params=pltpu.CompilerParams(
            collective_id=0, has_side_effects=True, vmem_limit_bytes=48 * 1024 * 1024
        ),
        name="halo_steps",
    )(hinge, u, v, t, s, hx, hy, f, cell, zonal, merid)


def solution(mesh):
    field, plain = P(None, "merid", "zonal"), P("merid", "zonal")
    return jax.shard_map(
        per_device,
        mesh=mesh,
        in_specs=(field,) * 4 + (plain,) * 3 + (field,) * 3 + (P(),),
        out_specs=(field,) * 4,
        check_vma=False,
    )
```

```python
import jax
import jax.numpy as jnp
from jax import lax
from jax.experimental import pallas as pl
from jax.experimental.pallas import tpu as pltpu
from jax.sharding import PartitionSpec as P

STEPS = 4
LEVELS = 3
TIME_STEP = 0.25
VISCOSITY = 0.25
DIFFUSIVITY = 0.25

MESH = pl.DeviceIdType.MESH

N = 128
OFF = 16
ROWS = 160
CHUNK = 32
WIDE = 5
SLIM = 4
GROUP = 42
WEST_OWN = WIDE
EAST_FIRST = WIDE + 9
EAST_HALO = EAST_FIRST + 9
CA, CB, CC, CF, CGX, CGY, CHX, CHY, CDX, CDY, CK = range(11)
SIGN = (-1.0, -1.0, 1.0, 1.0)


def sweep(body, size):
    def step(i, carry):
        first = pl.multiple_of(i * size, 8)
        body(first, pl.ds(first, size), pl.ds(pl.multiple_of(OFF + first, 8), size))
        return carry

    lax.fori_loop(0, N // size, step, 0)


def turned(x, shift):
    if isinstance(shift, int):
        shift %= N
        if shift == 0:
            return x
    return pltpu.roll(x, shift, 1)


def lanes(shape):
    return lax.broadcasted_iota(jnp.int32, shape, 1)


def coefficients(hx, hy, f):
    rx = 1.0 / hx
    ry = 1.0 / hy
    a = (TIME_STEP * VISCOSITY) * rx * rx
    b = (TIME_STEP * VISCOSITY) * ry * ry
    return (
        a,
        b,
        1.0 - 2.0 * (a + b),
        (0.5 * TIME_STEP) * f,
        TIME_STEP * rx,
        TIME_STEP * ry,
        0.5 * hx,
        0.5 * hy,
        DIFFUSIVITY * hy * rx,
        DIFFUSIVITY * hx * ry,
        TIME_STEP * rx * ry,
    )


def weights(t, s, lane):
    half = [0.25 * a - 0.2 * b for a, b in zip(t, s)]
    if len(half) == 1:
        one = jnp.where(lane >= GROUP, turned(half[0], GROUP), 0.0)
        two = jnp.where(lane >= 2 * GROUP, turned(half[0], 2 * GROUP), 0.0)
        return [half[0] + 2.0 * (one + two)]
    out = [half[0]]
    for k in range(1, LEVELS):
        out.append(out[-1] + (half[k - 1] + half[k]))
    return out


def advance(load, coef, masks, keep, east, west, rows, levels):
    lane = lanes((rows, N))
    span = range(levels)
    t = [load(2, k, 0) for k in span]
    s = [load(3, k, 0) for k in span]
    tn = [load(2, k, 1) for k in span]
    sn = [load(3, k, 1) for k in span]
    p = weights(t, s, lane)
    pn = weights(tn, sn, lane)
    for k in span:
        u, v = load(0, k, 0), load(1, k, 0)
        us, vs = load(0, k, -1), load(1, k, -1)
        uw = turned(u, west)
        mu, mv, mc = masks(k)
        un = mu * (
            coef(CC) * u
            + coef(CA) * (turned(u, east) + uw)
            + coef(CB) * (load(0, k, 1) + us)
            + coef(CF) * (v + vs)
            - coef(CGX) * (turned(p[k], east) - p[k])
        )
        vn = mv * (
            coef(CC) * v
            + coef(CA) * (turned(v, east) + turned(v, west))
            + coef(CB) * (load(1, k, 1) + vs)
            - coef(CF) * (u + uw)
            - coef(CGY) * (pn[k] - p[k])
        )
        keep(0, k, un)
        keep(1, k, vn)
        q, d = coef(CHY) * un, coef(CDX) * mu
        qp, qm = q + d, q - d
        r, e = coef(CHX) * vn, coef(CDY) * mv
        rp, rm = r + e, r - e
        scale = mc * coef(CK)
        for which, c, cn in ((2, t[k], tn[k]), (3, s[k], sn[k])):
            fe = qp * c + qm * turned(c, east)
            fn = rp * c + rm * cn
            below = keep(which + 2, k, fn)
            keep(which, k, c - scale * ((fe - turned(fe, west)) + (fn - below)))


def pack_wide(plane, rows):
    lane = lanes((rows, N))
    out = None
    for k in range(LEVELS):
        for g in range(8):
            first = GROUP * k + WIDE * g
            part = turned(plane(g, k), first - (N - WIDE))
            out = part if out is None else jnp.where(lane >= first, part, out)
    return out


def pack_slim(plane, rows):
    lane = lanes((rows, N))
    out = None
    for k in range(LEVELS):
        for g in range(8):
            first = GROUP * k + SLIM * g
            part = turned(plane(g, k), first)
            out = part if out is None else jnp.where(lane >= first, part, out)
    return out


def pack_own(plane, g, rows):
    lane = lanes((rows, N))
    out = None
    for k in range(LEVELS):
        x = plane(g, k)
        for first, column in ((GROUP * k + WEST_OWN, 0), (GROUP * k + EAST_FIRST, N - 9)):
            part = turned(x, first - column)
            out = part if out is None else jnp.where(lane >= first, part, out)
    return out


def merge_halo(own, wide, slim, g, rows):
    lane = lanes((rows, N))
    place = lane - jnp.where(lane >= 2 * GROUP, 2 * GROUP, jnp.where(lane >= GROUP, GROUP, 0))
    own = jnp.where(place < WIDE, turned(wide, -WIDE * g), own)
    east = (place >= EAST_HALO) & (place < EAST_HALO + SLIM)
    return jnp.where(east, turned(slim, EAST_HALO - SLIM * g), own)


def flipped(x):
    lane = lanes(x.shape)
    for bit in (64, 32, 16, 8, 4, 2, 1):
        if bit == 64:
            x = turned(x, 64)
        else:
            x = jnp.where((lane & bit) != 0, turned(x, bit), turned(x, -bit))
    return x


def kernel(
    u_hbm,
    v_hbm,
    t_hbm,
    s_hbm,
    hx_hbm,
    hy_hbm,
    f_hbm,
    cell_hbm,
    zonal_hbm,
    merid_hbm,
    hinge_hbm,
    u_out,
    v_out,
    t_out,
    s_out,
    u_ref,
    v_ref,
    t_ref,
    s_ref,
    hx_ref,
    hy_ref,
    f_ref,
    cell_ref,
    zonal_ref,
    merid_ref,
    hinge,
    main,
    edge,
    top_main,
    top_edge,
    flux_main,
    flux_edge,
    mask_main,
    mask_edge,
    mask_top_main,
    mask_top_edge,
    metric_main,
    metric_top,
    metric_edge,
    coef_main,
    coef_edge,
    coef_top_main,
    coef_top_edge,
    east_buf,
    west_buf,
    north_buf,
    south_buf,
    fold_tile,
    fold_west,
    fold_east,
    from_west,
    from_east,
    from_south,
    from_north,
    from_fold,
    from_corner,
    send_sem,
    recv_sem,
    local_sem,
    load_sem,
):
    sources = (u_hbm, v_hbm, t_hbm, s_hbm, cell_hbm, zonal_hbm, merid_hbm, hx_hbm, hy_hbm, f_hbm, hinge_hbm)
    targets = (u_ref, v_ref, t_ref, s_ref, cell_ref, zonal_ref, merid_ref, hx_ref, hy_ref, f_ref, hinge)
    loads = [
        pltpu.make_async_copy(src, dst, load_sem.at[i])
        for i, (src, dst) in enumerate(zip(sources, targets))
    ]
    for c in loads:
        c.start()

    nz, nm = lax.axis_size("zonal"), lax.axis_size("merid")
    z, m = lax.axis_index("zonal"), lax.axis_index("merid")
    east_z, west_z = lax.rem(z + 1, nz), lax.rem(z + nz - 1, nz)
    fold_z = nz - 1 - z
    fold_up, fold_down = lax.rem(fold_z + 1, nz), lax.rem(fold_z + nz - 1, nz)
    top, bottom = m == nm - 1, m == 0
    inner = jnp.logical_not(top)
    raised = jnp.logical_not(bottom)

    def at(zz, mm):
        return {"zonal": zz, "merid": mm}

    barrier = pltpu.get_barrier_semaphore()

    def hail(zz, mm):
        pl.semaphore_signal(barrier, inc=1, device_id=at(zz, mm), device_id_type=MESH)

    hail(east_z, m)
    hail(west_z, m)

    @pl.when(raised)
    def _():
        for zz in (west_z, z, east_z):
            hail(zz, m - 1)

    @pl.when(inner)
    def _():
        for zz in (west_z, z, east_z):
            hail(zz, m + 1)

    @pl.when(top)
    def _():
        hail(fold_z, m)

        @pl.when(fold_up != z)
        def _():
            hail(fold_up, m)

        @pl.when(fold_down != z)
        def _():
            hail(fold_down, m)

    for c in loads:
        c.wait()
    fields = (u_ref, v_ref, t_ref, s_ref)

    def fill(first, here, there):
        for k in range(LEVELS):
            mu = zonal_ref[k, here, :].astype(jnp.float32)
            mv = merid_ref[k, here, :].astype(jnp.float32)
            mc = cell_ref[k, here, :].astype(jnp.float32)
            mask_main[k, there, :] = mu
            mask_main[3 + k, there, :] = mv
            mask_main[6 + k, there, :] = mc
            for g, ref in enumerate(fields):
                main[0, 3 * g + k, there, :] = ref[k, here, :] * (mu, mv, mc, mc)[g]

    sweep(fill, CHUNK)

    def plane_at(start, rows):
        def plane(g, k):
            if g < 4:
                return main[0, 3 * g + k, pl.ds(OFF + start, rows), :]
            if g == 4:
                return mask_main[6 + k, pl.ds(OFF + start, rows), :]
            return (hx_ref, hy_ref, f_ref)[g - 5][pl.ds(start, rows), :]

        return plane

    def number(g, k):
        return 3 * g + k if g < 5 else 15 + g - 5

    every = [(g, k) for g in range(5) for k in range(LEVELS)] + [(g, 0) for g in (5, 6, 7)]

    @pl.when(inner)
    def _():
        for g, k in every:
            i = number(g, k)
            north_buf[pl.ds(WIDE * i, WIDE), :] = plane_at(N - WIDE, WIDE)(g, k)

    @pl.when(top)
    def _():
        plane = plane_at(N - 8, 8)
        for g, k in every:
            i = number(g, k)
            tile = flipped(plane(g, k))
            fold_tile[i, :, :] = tile
            north_buf[pl.ds(WIDE * i, WIDE), :] = tile[8 - WIDE :, :]
            if g == 1:
                north_buf[pl.ds(90 + k, 1), :] = tile[2:3, :]

        def mirrored(g, k):
            return fold_tile[number(g, k)]

        fold_west[...] = pack_wide(mirrored, 8)
        fold_east[...] = pack_slim(mirrored, 8)

    def copy(src, dst, slot, zz, mm):
        return pltpu.make_async_remote_copy(
            src_ref=src,
            dst_ref=dst,
            send_sem=send_sem.at[slot],
            recv_sem=recv_sem.at[slot],
            device_id=at(zz, mm),
            device_id_type=MESH,
        )

    corner = lambda i: from_corner.at[i]
    low, high = pl.ds(0, 8), pl.ds(N - 8, 8)
    to_east = copy(east_buf, from_west, 0, east_z, m)
    to_west = copy(west_buf, from_east, 1, west_z, m)
    to_north = copy(north_buf, from_south, 2, z, m + 1)
    to_south = copy(south_buf, from_north, 3, z, m - 1)
    to_fold = copy(north_buf, from_fold, 4, fold_z, m)
    to_ne = copy(east_buf.at[high], corner(0), 5, east_z, m + 1)
    to_nw = copy(west_buf.at[high], corner(1), 6, west_z, m + 1)
    to_se = copy(east_buf.at[low], corner(2), 7, east_z, m - 1)
    to_sw = copy(west_buf.at[low], corner(3), 8, west_z, m - 1)
    to_fold_up = copy(fold_west, corner(2), 9, fold_up, m)
    to_fold_down = copy(fold_east, corner(3), 10, fold_down, m)
    keep_fold_up = pltpu.make_async_copy(fold_west, corner(2), local_sem.at[0])
    keep_fold_down = pltpu.make_async_copy(fold_east, corner(3), local_sem.at[1])

    same = jnp.where(fold_up == z, 1, 0) + jnp.where(fold_down == z, 1, 0)
    pl.semaphore_wait(barrier, 2 + jnp.where(bottom, 0, 3) + 3 - jnp.where(top, same, 0))

    @pl.when(top)
    def _():
        to_fold.start()

        @pl.when(fold_up != z)
        def _():
            to_fold_up.start()

        @pl.when(fold_up == z)
        def _():
            keep_fold_up.start()

        @pl.when(fold_down != z)
        def _():
            to_fold_down.start()

        @pl.when(fold_down == z)
        def _():
            keep_fold_down.start()

    @pl.when(inner)
    def _():
        to_north.start()

    def pack(first, here, there):
        plane = plane_at(first, CHUNK)
        east_buf[here, :] = pack_wide(plane, CHUNK)
        west_buf[here, :] = pack_slim(plane, CHUNK)

    sweep(pack, CHUNK)
    to_east.start()
    to_west.start()

    @pl.when(inner)
    def _():
        to_ne.start()
        to_nw.start()

    for g, k in every:
        south_buf[pl.ds(SLIM * number(g, k), SLIM), :] = plane_at(0, SLIM)(g, k)

    @pl.when(raised)
    def _():
        to_south.start()
        to_se.start()
        to_sw.start()

    def prepare(first, here, there):
        for c, x in enumerate(coefficients(hx_ref[here, :], hy_ref[here, :], f_ref[here, :])):
            coef_main[c, there, :] = x
        plane = plane_at(first, CHUNK)
        for g in range(8):
            x = pack_own(plane, g, CHUNK)
            if g < 4:
                edge[0, g, there, :] = x
            elif g == 4:
                mask_edge[2, there, :] = x
            else:
                metric_edge[g - 5, there, :] = x

    sweep(prepare, CHUNK)

    def step_rows(n, start, rows, state, flux, mask, coef, levels, align=True):
        def at_row(dj):
            first = OFF + start + dj
            if dj == 0 and align:
                first = pl.multiple_of(first, 8)
            return pl.ds(first, rows)

        def load(g, k, dj):
            return state[n, levels * g + k, at_row(dj), :]

        def keep(g, k, x):
            if g < 4:
                state[n + 1, levels * g + k, at_row(0), :] = x
                return None
            flux[n, levels * (g - 4) + k, at_row(0), :] = x
            return flux[n, levels * (g - 4) + k, at_row(-1), :]

        def masks(k):
            return [mask[levels * i + k, at_row(0), :] for i in range(3)]

        advance(load, lambda c: coef[c, at_row(0), :], masks, keep, N - 1, 1, rows, levels)

    def interior(n, carry):
        def chunk(i, inside):
            step_rows(n, i * CHUNK, CHUNK, main, flux_main, mask_main, coef_main, LEVELS)
            return inside

        return lax.fori_loop(0, N // CHUNK, chunk, carry)

    lax.fori_loop(0, STEPS, interior, 0)

    halo = pl.ds(OFF - 8, 8)

    @pl.when(raised)
    def _():
        to_north.wait_recv()
        to_ne.wait_recv()
        to_nw.wait_recv()
        last = pl.ds(OFF - WIDE, WIDE)
        for g, k in every:
            x = from_south[pl.ds(WIDE * number(g, k), WIDE), :]
            if g < 4:
                main[0, 3 * g + k, last, :] = x
            elif g == 4:
                mask_main[6 + k, last, :] = x
            else:
                metric_main[g - 5, pl.ds(8 - WIDE, WIDE), :] = x

    @pl.when(bottom)
    def _():
        zero = jnp.zeros((8, N), jnp.float32)
        for g, k in every:
            if g < 4:
                main[0, 3 * g + k, halo, :] = zero
            elif g == 4:
                mask_main[6 + k, halo, :] = zero
            else:
                metric_main[g - 5, :, :] = zero + 1.0
        for i in (0, 1):
            from_corner[i, :, :] = zero

    for k in range(LEVELS):
        mc = mask_main[6 + k, halo, :]
        mask_main[k, halo, :] = mc * turned(mc, N - 1)
        mask_main[3 + k, halo, :] = mc * mask_main[6 + k, pl.ds(OFF - 7, 8), :]
    for c, x in enumerate(coefficients(metric_main[0], metric_main[1], metric_main[2])):
        coef_main[c, halo, :] = x

    to_east.wait_recv()
    to_west.wait_recv()

    def edge_keep(g, rows, x, offset=0):
        if g < 4:
            edge[0, g, rows, :] = x
        elif g == 4:
            mask_edge[2, rows, :] = x
        else:
            metric_edge[g - 5, rows, :] = x

    def south_plane(g, k):
        if g < 4:
            return main[0, 3 * g + k, halo, :]
        if g == 4:
            return mask_main[6 + k, halo, :]
        return metric_main[g - 5, :, :]

    for g in range(8):
        x = pack_own(south_plane, g, 8)
        x = merge_halo(x, from_corner[0], from_corner[1], g, 8)
        if g in (5, 6):
            x = jnp.where(bottom, 1.0, x)
        edge_keep(g, halo, x)

    def unpack(first, here, there):
        wide = from_west[here, :]
        slim = from_east[here, :]
        for g in range(8):
            if g < 4:
                x = edge[0, g, there, :]
            elif g == 4:
                x = mask_edge[2, there, :]
            else:
                x = metric_edge[g - 5, there, :]
            edge_keep(g, there, merge_halo(x, wide, slim, g, CHUNK))

    sweep(unpack, CHUNK)

    def edge_masks(start, rows):
        there = pl.ds(start, rows)
        mc = mask_edge[2, there, :]
        mask_edge[0, there, :] = mc * turned(mc, N - 1)
        mask_edge[1, there, :] = mc * mask_edge[2, pl.ds(start + 1, rows), :]

    def edge_ready(start, rows):
        there = pl.ds(start, rows)
        for c, x in enumerate(
            coefficients(metric_edge[0, there, :], metric_edge[1, there, :], metric_edge[2, there, :])
        ):
            coef_edge[c, there, :] = x

    edge_masks(OFF - 8, 8)
    edge_ready(OFF - 8, 8)

    def ready(first, here, there):
        edge_masks(OFF + first, CHUNK)
        edge_ready(OFF + first, CHUNK)

    sweep(ready, CHUNK)

    def south_side(n, carry):
        step_rows(n, n - WIDE, 8, main, flux_main, mask_main, coef_main, LEVELS, False)
        step_rows(n, -8, 8, edge, flux_edge, mask_edge, coef_edge, 1)

        def chunk(i, inside):
            step_rows(n, i * CHUNK, CHUNK, edge, flux_edge, mask_edge, coef_edge, 1)
            return inside

        return lax.fori_loop(0, N // CHUNK, chunk, carry)

    lax.fori_loop(0, STEPS, south_side, 0)

    strip = pl.ds(0, 8)
    for g, k in every:
        if g < 4:
            top_main[3 * g + k, strip, :] = jnp.zeros((8, N), jnp.float32)
        elif g == 4:
            mask_top_main[6 + k, strip, :] = jnp.zeros((8, N), jnp.float32)
        else:
            metric_top[g - 5, :, :] = jnp.ones((8, N), jnp.float32)

    def top_keep(g, k, first, x):
        rows = pl.ds(first, x.shape[0])
        if g < 4:
            top_main[3 * g + k, rows, :] = x
        elif g == 4:
            mask_top_main[6 + k, rows, :] = x
        else:
            metric_top[g - 5, pl.ds(first, x.shape[0]), :] = x

    @pl.when(inner)
    def _():
        to_south.wait_recv()
        to_se.wait_recv()
        to_sw.wait_recv()
        for g, k in every:
            top_keep(g, k, 0, from_north[pl.ds(SLIM * number(g, k), SLIM), :])

    @pl.when(top)
    def _():
        to_fold.wait_recv()

        @pl.when(fold_up != z)
        def _():
            to_fold_up.wait_recv()

        @pl.when(fold_up == z)
        def _():
            keep_fold_up.wait()

        @pl.when(fold_down != z)
        def _():
            to_fold_down.wait_recv()

        @pl.when(fold_down == z)
        def _():
            keep_fold_down.wait()

        for g, k in every:
            top_keep(g, k, 8 - WIDE, from_fold[pl.ds(WIDE * number(g, k), WIDE), :])
        for k in range(LEVELS):
            top_keep(1, k, 2, from_fold[pl.ds(90 + k, 1), :])

    east = jnp.where(top, 1, N - 1)
    west = jnp.where(top, N - 1, 1)

    def top_plane(g, k):
        if g < 4:
            return top_main[3 * g + k, strip, :]
        if g == 4:
            return mask_top_main[6 + k, strip, :]
        return metric_top[g - 5, :, :]

    edge_metric = []
    for g in range(8):
        x = merge_halo(pack_own(top_plane, g, 8), from_corner[2], from_corner[3], g, 8)
        if g < 4:
            top_edge[g, strip, :] = x
        elif g == 4:
            mask_top_edge[2, strip, :] = x
        else:
            edge_metric.append(x)
    for c, x in enumerate(coefficients(*edge_metric)):
        coef_top_edge[c, :, :] = x
    for c, x in enumerate(coefficients(metric_top[0], metric_top[1], metric_top[2])):
        coef_top_main[c, :, :] = x
    row = lax.broadcasted_iota(jnp.int32, (8, N), 0)
    mc = mask_edge[2, pl.ds(OFF + N - 8, 8), :]
    over = jnp.where(top, 1.0, pltpu.roll(mask_top_edge[2, strip, :], 7, 0))
    mask_edge[1, pl.ds(OFF + N - 8, 8), :] = mc * jnp.where(row == 7, over, pltpu.roll(mc, 7, 0))
    for mask, levels in ((mask_top_main, LEVELS), (mask_top_edge, 1)):
        for k in range(levels):
            mc = mask[2 * levels + k, strip, :]
            mask[k, strip, :] = mc * turned(mc, east)
            mask[levels + k, strip, :] = mc * jnp.where(row == 7, 1.0, pltpu.roll(mc, 7, 0))

    plain = [jnp.full((1, N), hinge[g], jnp.int32) == 0 for g in range(4)]

    first_row, last_row = row == 0, row == 7
    brim, under = pl.ds(OFF + N - 8, 8), pl.ds(OFF + N - 16, 8)

    def up(x):
        return pltpu.roll(x, 7, 0)

    def down(x):
        return pltpu.roll(x, 1, 0)

    kinds = (
        (LEVELS, main, flux_main, mask_main, mask_top_main, coef_main, coef_top_main),
        (1, edge, flux_edge, mask_edge, mask_top_edge, coef_edge, coef_top_edge),
    )

    def north_side(n, carry):
        after = []
        for (levels, state, flux, mask, mask_beyond, coef, coef_beyond), (below, beyond) in zip(
            kinds, carry
        ):
            new_below, new_beyond, fluxes = [None] * len(below), [None] * len(beyond), {}

            def load_below(g, k, dj):
                c, z = below[levels * g + k], beyond[levels * g + k]
                if dj == 0:
                    return c
                if dj < 0:
                    return jnp.where(first_row, down(state[n, levels * g + k, under, :]), down(c))
                ghost = SIGN[g] * jnp.where(plain[g], z, down(turned(z, 1)))
                return jnp.where(last_row, jnp.where(top, ghost, up(z)), up(c))

            def load_beyond(g, k, dj):
                c, z = below[levels * g + k], beyond[levels * g + k]
                if dj == 0:
                    return z
                if dj < 0:
                    return jnp.where(first_row, down(c), down(z))
                ghost = SIGN[g] * jnp.where(plain[g], c, down(turned(c, N - 1)))
                return jnp.where(last_row, ghost, up(z))

            def keep_below(g, k, x):
                if g < 4:
                    new_below[levels * g + k] = x
                    return None
                fluxes[g, k] = down(x)
                return jnp.where(
                    first_row, down(flux[n, levels * (g - 4) + k, under, :]), fluxes[g, k]
                )

            def keep_beyond(g, k, x):
                if g < 4:
                    new_beyond[levels * g + k] = x
                    return None
                return jnp.where(first_row, fluxes[g, k], down(x))

            def masks(k):
                return [mask[levels * i + k, brim, :] for i in range(3)]

            def masks_beyond(k):
                return [mask_beyond[levels * i + k, strip, :] for i in range(3)]

            advance(load_below, lambda c: coef[c, brim, :], masks, keep_below, N - 1, 1, 8, levels)
            advance(
                load_beyond, lambda c: coef_beyond[c], masks_beyond, keep_beyond, east, west, 8, levels
            )
            after.append((tuple(new_below), tuple(new_beyond)))
        return tuple(after)

    start = tuple(
        (
            tuple(state[0, i, brim, :] for i in range(4 * levels)),
            tuple(beyond[i, strip, :] for i in range(4 * levels)),
        )
        for levels, state, beyond in ((LEVELS, main, top_main), (1, edge, top_edge))
    )
    done = lax.fori_loop(0, STEPS, north_side, start)
    for state, (below, _) in zip((main, edge), done):
        for i, x in enumerate(below):
            state[STEPS, i, brim, :] = x

    def finish(first, here, there):
        lane = lanes((CHUNK, N))
        for g, ref in enumerate((u_out, v_out, t_out, s_out)):
            x = edge[STEPS, g, there, :]
            for k in range(LEVELS):
                y = main[STEPS, 3 * g + k, there, :]
                y = jnp.where(lane < WIDE, turned(x, -(GROUP * k + WEST_OWN)), y)
                sides = turned(x, N - SLIM - (GROUP * k + EAST_HALO - SLIM))
                ref[k, here, :] = jnp.where(lane >= N - SLIM, sides, y)

    sweep(finish, CHUNK)

    to_east.wait_send()
    to_west.wait_send()

    @pl.when(inner)
    def _():
        for c in (to_north, to_ne, to_nw):
            c.wait_send()

    @pl.when(raised)
    def _():
        for c in (to_south, to_se, to_sw):
            c.wait_send()

    @pl.when(top)
    def _():
        to_fold.wait_send()

        @pl.when(fold_up != z)
        def _():
            to_fold_up.wait_send()

        @pl.when(fold_down != z)
        def _():
            to_fold_down.wait_send()


def deliver(*refs):
    for i in range(4):
        refs[4 + i][...] = refs[i][...]


def per_device(u, v, t, s, hx, hy, f, cell, zonal, merid, hinge):
    def buf(*shape):
        return pltpu.VMEM(shape + (N,), jnp.float32)

    vmem = pl.BlockSpec(memory_space=pltpu.VMEM)
    shape = jax.ShapeDtypeStruct((LEVELS, N, N), jnp.float32)
    results = pl.pallas_call(
        kernel,
        out_shape=(shape,) * 4,
        in_specs=[pl.BlockSpec(memory_space=pltpu.HBM)] * 11,
        out_specs=(vmem,) * 4,
        scratch_shapes=[buf(LEVELS, N)] * 4
        + [buf(N)] * 3
        + [pltpu.VMEM((LEVELS, N, N), jnp.int32)] * 3
        + [pltpu.SMEM((4,), jnp.int32)]
        + [
            buf(5, 12, ROWS),
            buf(5, 4, ROWS),
            buf(12, 8),
            buf(4, 8),
            buf(4, 6, ROWS),
            buf(4, 2, ROWS),
            buf(9, ROWS),
            buf(3, ROWS),
            buf(9, 8),
            buf(3, 8),
            buf(3, 8),
            buf(3, 8),
            buf(3, ROWS),
            buf(11, ROWS),
            buf(11, ROWS),
            buf(11, 8),
            buf(11, 8),
            buf(N),
            buf(N),
            buf(96),
            buf(72),
            buf(18, 8),
            buf(8),
            buf(8),
            buf(N),
            buf(N),
            buf(96),
            buf(72),
            buf(96),
            buf(4, 8),
            pltpu.SemaphoreType.DMA((11,)),
            pltpu.SemaphoreType.DMA((11,)),
            pltpu.SemaphoreType.DMA((2,)),
            pltpu.SemaphoreType.DMA((11,)),
        ],
        compiler_params=pltpu.CompilerParams(
            collective_id=0, has_side_effects=True, vmem_limit_bytes=60 * 1024 * 1024
        ),
        name="halo_steps",
    )(u, v, t, s, hx, hy, f, cell, zonal, merid, hinge)


    return pl.pallas_call(
        deliver,
        out_shape=(shape,) * 4,
        in_specs=[vmem] * 4,
        out_specs=(vmem,) * 4,
        name="deliver",
    )(*results)


def solution(mesh):
    field, plain = P(None, "merid", "zonal"), P("merid", "zonal")
    return jax.shard_map(
        per_device,
        mesh=mesh,
        in_specs=(field,) * 4 + (plain,) * 3 + (field,) * 3 + (P(),),
        out_specs=(field,) * 4,
        check_vma=False,
    )
```

```python
import jax
import jax.numpy as jnp
from jax import lax
from jax.experimental import pallas as pl
from jax.experimental.pallas import tpu as pltpu
from jax.sharding import PartitionSpec as P

STEPS = 4
LEVELS = 3
TIME_STEP = 0.25
VISCOSITY = 0.25
DIFFUSIVITY = 0.25

MESH = pl.DeviceIdType.MESH

N = 128
OFF = 16
ROWS = 160
CHUNK = 32
EDGE_ROWS = 128
FILL = PACK = PREPARE = UNPACK = READY = FINISH = 128
PARTS = 1
PIECE = N // PARTS
WIDE = 5
SLIM = 4
GROUP = 42
WEST_OWN = WIDE
EAST_FIRST = WIDE + 9
EAST_HALO = EAST_FIRST + 9
CA, CB, CC, CF, CGX, CGY, CHX, CHY, CDX, CDY, CK = range(11)
SIGN = (-1.0, -1.0, 1.0, 1.0)


def sweep(body, size):
    def step(i, carry):
        first = pl.multiple_of(i * size, 8)
        body(first, pl.ds(first, size), pl.ds(pl.multiple_of(OFF + first, 8), size))
        return carry

    lax.fori_loop(0, N // size, step, 0)


def turned(x, shift):
    if isinstance(shift, int):
        shift %= N
        if shift == 0:
            return x
    return pltpu.roll(x, shift, 1)


def lanes(shape):
    return lax.broadcasted_iota(jnp.int32, shape, 1)


def coefficients(hx, hy, f):
    rx = 1.0 / hx
    ry = 1.0 / hy
    a = (TIME_STEP * VISCOSITY) * rx * rx
    b = (TIME_STEP * VISCOSITY) * ry * ry
    return (
        a,
        b,
        1.0 - 2.0 * (a + b),
        (0.5 * TIME_STEP) * f,
        TIME_STEP * rx,
        TIME_STEP * ry,
        0.5 * hx,
        0.5 * hy,
        DIFFUSIVITY * hy * rx,
        DIFFUSIVITY * hx * ry,
        TIME_STEP * rx * ry,
    )


def weights(t, s, lane):
    half = [0.25 * a - 0.2 * b for a, b in zip(t, s)]
    if len(half) == 1:
        one = jnp.where(lane >= GROUP, turned(half[0], GROUP), 0.0)
        two = jnp.where(lane >= 2 * GROUP, turned(half[0], 2 * GROUP), 0.0)
        return [half[0] + 2.0 * (one + two)]
    out = [half[0]]
    for k in range(1, LEVELS):
        out.append(out[-1] + (half[k - 1] + half[k]))
    return out


def advance(load, coef, masks, keep, east, west, rows, levels):
    lane = lanes((rows, N))
    span = range(levels)
    t = [load(2, k, 0) for k in span]
    s = [load(3, k, 0) for k in span]
    tn = [load(2, k, 1) for k in span]
    sn = [load(3, k, 1) for k in span]
    p = weights(t, s, lane)
    pn = weights(tn, sn, lane)
    for k in span:
        u, v = load(0, k, 0), load(1, k, 0)
        us, vs = load(0, k, -1), load(1, k, -1)
        uw = turned(u, west)
        mu, mv, mc = masks(k)
        un = mu * (
            coef(CC) * u
            + coef(CA) * (turned(u, east) + uw)
            + coef(CB) * (load(0, k, 1) + us)
            + coef(CF) * (v + vs)
            - coef(CGX) * (turned(p[k], east) - p[k])
        )
        vn = mv * (
            coef(CC) * v
            + coef(CA) * (turned(v, east) + turned(v, west))
            + coef(CB) * (load(1, k, 1) + vs)
            - coef(CF) * (u + uw)
            - coef(CGY) * (pn[k] - p[k])
        )
        keep(0, k, un)
        keep(1, k, vn)
        q, d = coef(CHY) * un, coef(CDX) * mu
        qp, qm = q + d, q - d
        r, e = coef(CHX) * vn, coef(CDY) * mv
        rp, rm = r + e, r - e
        scale = mc * coef(CK)
        for which, c, cn in ((2, t[k], tn[k]), (3, s[k], sn[k])):
            fe = qp * c + qm * turned(c, east)
            fn = rp * c + rm * cn
            below = keep(which + 2, k, fn)
            keep(which, k, c - scale * ((fe - turned(fe, west)) + (fn - below)))


def pack_wide(plane, rows):
    lane = lanes((rows, N))
    out = None
    for k in range(LEVELS):
        for g in range(8):
            first = GROUP * k + WIDE * g
            part = turned(plane(g, k), first - (N - WIDE))
            out = part if out is None else jnp.where(lane >= first, part, out)
    return out


def pack_slim(plane, rows):
    lane = lanes((rows, N))
    out = None
    for k in range(LEVELS):
        for g in range(8):
            first = GROUP * k + SLIM * g
            part = turned(plane(g, k), first)
            out = part if out is None else jnp.where(lane >= first, part, out)
    return out


def pack_own(plane, g, rows):
    lane = lanes((rows, N))
    out = None
    for k in range(LEVELS):
        x = plane(g, k)
        for first, column in ((GROUP * k + WEST_OWN, 0), (GROUP * k + EAST_FIRST, N - 9)):
            part = turned(x, first - column)
            out = part if out is None else jnp.where(lane >= first, part, out)
    return out


def merge_halo(own, wide, slim, g, rows):
    lane = lanes((rows, N))
    place = lane - jnp.where(lane >= 2 * GROUP, 2 * GROUP, jnp.where(lane >= GROUP, GROUP, 0))
    own = jnp.where(place < WIDE, turned(wide, -WIDE * g), own)
    east = (place >= EAST_HALO) & (place < EAST_HALO + SLIM)
    return jnp.where(east, turned(slim, EAST_HALO - SLIM * g), own)


def flipped(x):
    lane = lanes(x.shape)
    for bit in (64, 32, 16, 8, 4, 2, 1):
        if bit == 64:
            x = turned(x, 64)
        else:
            x = jnp.where((lane & bit) != 0, turned(x, bit), turned(x, -bit))
    return x


def kernel(
    u_hbm,
    v_hbm,
    t_hbm,
    s_hbm,
    hx_hbm,
    hy_hbm,
    f_hbm,
    cell_hbm,
    zonal_hbm,
    merid_hbm,
    hinge_hbm,
    u_out,
    v_out,
    t_out,
    s_out,
    u_ref,
    v_ref,
    t_ref,
    s_ref,
    hx_ref,
    hy_ref,
    f_ref,
    cell_ref,
    zonal_ref,
    merid_ref,
    hinge,
    main,
    edge,
    top_main,
    top_edge,
    flux_main,
    flux_edge,
    mask_main,
    mask_edge,
    mask_top_main,
    mask_top_edge,
    metric_main,
    metric_top,
    metric_edge,
    coef_main,
    coef_edge,
    coef_top_main,
    coef_top_edge,
    east_buf,
    west_buf,
    north_buf,
    south_buf,
    fold_tile,
    fold_west,
    fold_east,
    from_west,
    from_east,
    from_south,
    from_north,
    from_fold,
    from_corner,
    send_sem,
    recv_sem,
    local_sem,
    load_sem,
):
    sources = (u_hbm, v_hbm, t_hbm, s_hbm, cell_hbm, zonal_hbm, merid_hbm, hx_hbm, hy_hbm, f_hbm, hinge_hbm)
    targets = (u_ref, v_ref, t_ref, s_ref, cell_ref, zonal_ref, merid_ref, hx_ref, hy_ref, f_ref, hinge)
    loads = [
        pltpu.make_async_copy(src, dst, load_sem.at[i])
        for i, (src, dst) in enumerate(zip(sources, targets))
    ]
    for c in loads:
        c.start()

    nz, nm = lax.axis_size("zonal"), lax.axis_size("merid")
    z, m = lax.axis_index("zonal"), lax.axis_index("merid")
    east_z, west_z = lax.rem(z + 1, nz), lax.rem(z + nz - 1, nz)
    fold_z = nz - 1 - z
    fold_up, fold_down = lax.rem(fold_z + 1, nz), lax.rem(fold_z + nz - 1, nz)
    top, bottom = m == nm - 1, m == 0
    inner = jnp.logical_not(top)
    raised = jnp.logical_not(bottom)

    def at(zz, mm):
        return {"zonal": zz, "merid": mm}

    barrier = pltpu.get_barrier_semaphore()

    def hail(zz, mm):
        pl.semaphore_signal(barrier, inc=1, device_id=at(zz, mm), device_id_type=MESH)

    hail(east_z, m)
    hail(west_z, m)

    @pl.when(raised)
    def _():
        for zz in (west_z, z, east_z):
            hail(zz, m - 1)

    @pl.when(inner)
    def _():
        for zz in (west_z, z, east_z):
            hail(zz, m + 1)

    @pl.when(top)
    def _():
        hail(fold_z, m)

        @pl.when(fold_up != z)
        def _():
            hail(fold_up, m)

        @pl.when(fold_down != z)
        def _():
            hail(fold_down, m)

    for c in loads:
        c.wait()
    fields = (u_ref, v_ref, t_ref, s_ref)

    def fill(first, here, there):
        for k in range(LEVELS):
            mu = zonal_ref[k, here, :].astype(jnp.float32)
            mv = merid_ref[k, here, :].astype(jnp.float32)
            mc = cell_ref[k, here, :].astype(jnp.float32)
            mask_main[k, there, :] = mu
            mask_main[3 + k, there, :] = mv
            mask_main[6 + k, there, :] = mc
            for g, ref in enumerate(fields):
                main[0, 3 * g + k, there, :] = ref[k, here, :] * (mu, mv, mc, mc)[g]

    sweep(fill, FILL)

    def plane_at(start, rows):
        def plane(g, k):
            if g < 4:
                return main[0, 3 * g + k, pl.ds(OFF + start, rows), :]
            if g == 4:
                return mask_main[6 + k, pl.ds(OFF + start, rows), :]
            return (hx_ref, hy_ref, f_ref)[g - 5][pl.ds(start, rows), :]

        return plane

    def number(g, k):
        return 3 * g + k if g < 5 else 15 + g - 5

    every = [(g, k) for g in range(5) for k in range(LEVELS)] + [(g, 0) for g in (5, 6, 7)]

    @pl.when(inner)
    def _():
        for g, k in every:
            i = number(g, k)
            north_buf[pl.ds(WIDE * i, WIDE), :] = plane_at(N - WIDE, WIDE)(g, k)

    @pl.when(top)
    def _():
        plane = plane_at(N - 8, 8)
        for g, k in every:
            i = number(g, k)
            tile = flipped(plane(g, k))
            fold_tile[i, :, :] = tile
            north_buf[pl.ds(WIDE * i, WIDE), :] = tile[8 - WIDE :, :]
            if g == 1:
                north_buf[pl.ds(90 + k, 1), :] = tile[2:3, :]

        def mirrored(g, k):
            return fold_tile[number(g, k)]

        fold_west[...] = pack_wide(mirrored, 8)
        fold_east[...] = pack_slim(mirrored, 8)

    def copy(src, dst, slot, zz, mm):
        return pltpu.make_async_remote_copy(
            src_ref=src,
            dst_ref=dst,
            send_sem=send_sem.at[slot],
            recv_sem=recv_sem.at[slot],
            device_id=at(zz, mm),
            device_id_type=MESH,
        )

    corner = lambda i: from_corner.at[i]
    low, high = pl.ds(0, 8), pl.ds(N - 8, 8)
    to_east, to_west = [], []
    for i in range(PARTS):
        piece = pl.ds(i * PIECE, PIECE)
        to_east.append(copy(east_buf.at[piece], from_west.at[piece], 11 + 2 * i, east_z, m))
        to_west.append(copy(west_buf.at[piece], from_east.at[piece], 12 + 2 * i, west_z, m))
    to_north = copy(north_buf, from_south, 2, z, m + 1)
    to_south = copy(south_buf, from_north, 3, z, m - 1)
    to_fold = copy(north_buf, from_fold, 4, fold_z, m)
    to_ne = copy(east_buf.at[high], corner(0), 5, east_z, m + 1)
    to_nw = copy(west_buf.at[high], corner(1), 6, west_z, m + 1)
    to_se = copy(east_buf.at[low], corner(2), 7, east_z, m - 1)
    to_sw = copy(west_buf.at[low], corner(3), 8, west_z, m - 1)
    to_fold_up = copy(fold_west, corner(2), 9, fold_up, m)
    to_fold_down = copy(fold_east, corner(3), 10, fold_down, m)
    keep_fold_up = pltpu.make_async_copy(fold_west, corner(2), local_sem.at[0])
    keep_fold_down = pltpu.make_async_copy(fold_east, corner(3), local_sem.at[1])

    same = jnp.where(fold_up == z, 1, 0) + jnp.where(fold_down == z, 1, 0)
    pl.semaphore_wait(barrier, 2 + jnp.where(bottom, 0, 3) + 3 - jnp.where(top, same, 0))

    @pl.when(top)
    def _():
        to_fold.start()

        @pl.when(fold_up != z)
        def _():
            to_fold_up.start()

        @pl.when(fold_up == z)
        def _():
            keep_fold_up.start()

        @pl.when(fold_down != z)
        def _():
            to_fold_down.start()

        @pl.when(fold_down == z)
        def _():
            keep_fold_down.start()

    @pl.when(inner)
    def _():
        to_north.start()

    for i in range(PARTS):
        plane = plane_at(i * PIECE, PIECE)
        east_buf[pl.ds(i * PIECE, PIECE), :] = pack_wide(plane, PIECE)
        to_east[i].start()
        west_buf[pl.ds(i * PIECE, PIECE), :] = pack_slim(plane, PIECE)
        to_west[i].start()

    @pl.when(inner)
    def _():
        to_ne.start()
        to_nw.start()

    for g, k in every:
        south_buf[pl.ds(SLIM * number(g, k), SLIM), :] = plane_at(0, SLIM)(g, k)

    @pl.when(raised)
    def _():
        to_south.start()
        to_se.start()
        to_sw.start()

    def prepare(first, here, there):
        for c, x in enumerate(coefficients(hx_ref[here, :], hy_ref[here, :], f_ref[here, :])):
            coef_main[c, there, :] = x
        plane = plane_at(first, PREPARE)
        for g in range(8):
            x = pack_own(plane, g, PREPARE)
            if g < 4:
                edge[0, g, there, :] = x
            elif g == 4:
                mask_edge[2, there, :] = x
            else:
                metric_edge[g - 5, there, :] = x

    sweep(prepare, PREPARE)

    def step_rows(n, start, rows, state, flux, mask, coef, levels, align=True):
        def at_row(dj):
            first = OFF + start + dj
            if dj == 0 and align:
                first = pl.multiple_of(first, 8)
            return pl.ds(first, rows)

        def load(g, k, dj):
            return state[n, levels * g + k, at_row(dj), :]

        def keep(g, k, x):
            if g < 4:
                state[n + 1, levels * g + k, at_row(0), :] = x
                return None
            flux[n, levels * (g - 4) + k, at_row(0), :] = x
            return flux[n, levels * (g - 4) + k, at_row(-1), :]

        def masks(k):
            return [mask[levels * i + k, at_row(0), :] for i in range(3)]

        advance(load, lambda c: coef[c, at_row(0), :], masks, keep, N - 1, 1, rows, levels)

    def interior(n, carry):
        def chunk(i, inside):
            step_rows(n, i * CHUNK, CHUNK, main, flux_main, mask_main, coef_main, LEVELS)
            return inside

        return lax.fori_loop(0, N // CHUNK, chunk, carry)

    lax.fori_loop(0, STEPS, interior, 0)

    halo = pl.ds(OFF - 8, 8)

    @pl.when(raised)
    def _():
        to_north.wait_recv()
        to_ne.wait_recv()
        to_nw.wait_recv()
        last = pl.ds(OFF - WIDE, WIDE)
        for g, k in every:
            x = from_south[pl.ds(WIDE * number(g, k), WIDE), :]
            if g < 4:
                main[0, 3 * g + k, last, :] = x
            elif g == 4:
                mask_main[6 + k, last, :] = x
            else:
                metric_main[g - 5, pl.ds(8 - WIDE, WIDE), :] = x

    @pl.when(bottom)
    def _():
        zero = jnp.zeros((8, N), jnp.float32)
        for g, k in every:
            if g < 4:
                main[0, 3 * g + k, halo, :] = zero
            elif g == 4:
                mask_main[6 + k, halo, :] = zero
            else:
                metric_main[g - 5, :, :] = zero + 1.0
        for i in (0, 1):
            from_corner[i, :, :] = zero

    for k in range(LEVELS):
        mc = mask_main[6 + k, halo, :]
        mask_main[k, halo, :] = mc * turned(mc, N - 1)
        mask_main[3 + k, halo, :] = mc * mask_main[6 + k, pl.ds(OFF - 7, 8), :]
    for c, x in enumerate(coefficients(metric_main[0], metric_main[1], metric_main[2])):
        coef_main[c, halo, :] = x

    for c in to_east + to_west:
        c.wait_recv()

    def edge_keep(g, rows, x, offset=0):
        if g < 4:
            edge[0, g, rows, :] = x
        elif g == 4:
            mask_edge[2, rows, :] = x
        else:
            metric_edge[g - 5, rows, :] = x

    def south_plane(g, k):
        if g < 4:
            return main[0, 3 * g + k, halo, :]
        if g == 4:
            return mask_main[6 + k, halo, :]
        return metric_main[g - 5, :, :]

    for g in range(8):
        x = pack_own(south_plane, g, 8)
        x = merge_halo(x, from_corner[0], from_corner[1], g, 8)
        if g in (5, 6):
            x = jnp.where(bottom, 1.0, x)
        edge_keep(g, halo, x)

    def unpack(first, here, there):
        wide = from_west[here, :]
        slim = from_east[here, :]
        for g in range(8):
            if g < 4:
                x = edge[0, g, there, :]
            elif g == 4:
                x = mask_edge[2, there, :]
            else:
                x = metric_edge[g - 5, there, :]
            edge_keep(g, there, merge_halo(x, wide, slim, g, UNPACK))

    sweep(unpack, UNPACK)

    def edge_masks(start, rows):
        there = pl.ds(start, rows)
        mc = mask_edge[2, there, :]
        mask_edge[0, there, :] = mc * turned(mc, N - 1)
        mask_edge[1, there, :] = mc * mask_edge[2, pl.ds(start + 1, rows), :]

    def edge_ready(start, rows):
        there = pl.ds(start, rows)
        for c, x in enumerate(
            coefficients(metric_edge[0, there, :], metric_edge[1, there, :], metric_edge[2, there, :])
        ):
            coef_edge[c, there, :] = x

    edge_masks(OFF - 8, 8)
    edge_ready(OFF - 8, 8)

    def ready(first, here, there):
        edge_masks(OFF + first, READY)
        edge_ready(OFF + first, READY)

    sweep(ready, READY)

    def south_side(n, carry):
        step_rows(n, n - WIDE, 8, main, flux_main, mask_main, coef_main, LEVELS, False)
        step_rows(n, -8, 8, edge, flux_edge, mask_edge, coef_edge, 1)

        def chunk(i, inside):
            step_rows(n, i * EDGE_ROWS, EDGE_ROWS, edge, flux_edge, mask_edge, coef_edge, 1)
            return inside

        return lax.fori_loop(0, N // EDGE_ROWS, chunk, carry)

    lax.fori_loop(0, STEPS, south_side, 0)

    strip = pl.ds(0, 8)
    for g, k in every:
        if g < 4:
            top_main[3 * g + k, strip, :] = jnp.zeros((8, N), jnp.float32)
        elif g == 4:
            mask_top_main[6 + k, strip, :] = jnp.zeros((8, N), jnp.float32)
        else:
            metric_top[g - 5, :, :] = jnp.ones((8, N), jnp.float32)

    def top_keep(g, k, first, x):
        rows = pl.ds(first, x.shape[0])
        if g < 4:
            top_main[3 * g + k, rows, :] = x
        elif g == 4:
            mask_top_main[6 + k, rows, :] = x
        else:
            metric_top[g - 5, pl.ds(first, x.shape[0]), :] = x

    @pl.when(inner)
    def _():
        to_south.wait_recv()
        to_se.wait_recv()
        to_sw.wait_recv()
        for g, k in every:
            top_keep(g, k, 0, from_north[pl.ds(SLIM * number(g, k), SLIM), :])

    @pl.when(top)
    def _():
        to_fold.wait_recv()

        @pl.when(fold_up != z)
        def _():
            to_fold_up.wait_recv()

        @pl.when(fold_up == z)
        def _():
            keep_fold_up.wait()

        @pl.when(fold_down != z)
        def _():
            to_fold_down.wait_recv()

        @pl.when(fold_down == z)
        def _():
            keep_fold_down.wait()

        for g, k in every:
            top_keep(g, k, 8 - WIDE, from_fold[pl.ds(WIDE * number(g, k), WIDE), :])
        for k in range(LEVELS):
            top_keep(1, k, 2, from_fold[pl.ds(90 + k, 1), :])

    east = jnp.where(top, 1, N - 1)
    west = jnp.where(top, N - 1, 1)

    def top_plane(g, k):
        if g < 4:
            return top_main[3 * g + k, strip, :]
        if g == 4:
            return mask_top_main[6 + k, strip, :]
        return metric_top[g - 5, :, :]

    edge_metric = []
    for g in range(8):
        x = merge_halo(pack_own(top_plane, g, 8), from_corner[2], from_corner[3], g, 8)
        if g < 4:
            top_edge[g, strip, :] = x
        elif g == 4:
            mask_top_edge[2, strip, :] = x
        else:
            edge_metric.append(x)
    for c, x in enumerate(coefficients(*edge_metric)):
        coef_top_edge[c, :, :] = x
    for c, x in enumerate(coefficients(metric_top[0], metric_top[1], metric_top[2])):
        coef_top_main[c, :, :] = x
    row = lax.broadcasted_iota(jnp.int32, (8, N), 0)
    mc = mask_edge[2, pl.ds(OFF + N - 8, 8), :]
    over = jnp.where(top, 1.0, pltpu.roll(mask_top_edge[2, strip, :], 7, 0))
    mask_edge[1, pl.ds(OFF + N - 8, 8), :] = mc * jnp.where(row == 7, over, pltpu.roll(mc, 7, 0))
    for mask, levels in ((mask_top_main, LEVELS), (mask_top_edge, 1)):
        for k in range(levels):
            mc = mask[2 * levels + k, strip, :]
            mask[k, strip, :] = mc * turned(mc, east)
            mask[levels + k, strip, :] = mc * jnp.where(row == 7, 1.0, pltpu.roll(mc, 7, 0))

    plain = [jnp.full((1, N), hinge[g], jnp.int32) == 0 for g in range(4)]

    first_row, last_row = row == 0, row == 7
    brim, under = pl.ds(OFF + N - 8, 8), pl.ds(OFF + N - 16, 8)

    def up(x):
        return pltpu.roll(x, 7, 0)

    def down(x):
        return pltpu.roll(x, 1, 0)

    kinds = (
        (LEVELS, main, flux_main, mask_main, mask_top_main, coef_main, coef_top_main),
        (1, edge, flux_edge, mask_edge, mask_top_edge, coef_edge, coef_top_edge),
    )

    def north_side(n, carry):
        after = []
        for (levels, state, flux, mask, mask_beyond, coef, coef_beyond), (below, beyond) in zip(
            kinds, carry
        ):
            new_below, new_beyond, fluxes = [None] * len(below), [None] * len(beyond), {}

            def load_below(g, k, dj):
                c, z = below[levels * g + k], beyond[levels * g + k]
                if dj == 0:
                    return c
                if dj < 0:
                    return jnp.where(first_row, down(state[n, levels * g + k, under, :]), down(c))
                ghost = SIGN[g] * jnp.where(plain[g], z, down(turned(z, 1)))
                return jnp.where(last_row, jnp.where(top, ghost, up(z)), up(c))

            def load_beyond(g, k, dj):
                c, z = below[levels * g + k], beyond[levels * g + k]
                if dj == 0:
                    return z
                if dj < 0:
                    return jnp.where(first_row, down(c), down(z))
                ghost = SIGN[g] * jnp.where(plain[g], c, down(turned(c, N - 1)))
                return jnp.where(last_row, ghost, up(z))

            def keep_below(g, k, x):
                if g < 4:
                    new_below[levels * g + k] = x
                    return None
                fluxes[g, k] = down(x)
                return jnp.where(
                    first_row, down(flux[n, levels * (g - 4) + k, under, :]), fluxes[g, k]
                )

            def keep_beyond(g, k, x):
                if g < 4:
                    new_beyond[levels * g + k] = x
                    return None
                return jnp.where(first_row, fluxes[g, k], down(x))

            def masks(k):
                return [mask[levels * i + k, brim, :] for i in range(3)]

            def masks_beyond(k):
                return [mask_beyond[levels * i + k, strip, :] for i in range(3)]

            advance(load_below, lambda c: coef[c, brim, :], masks, keep_below, N - 1, 1, 8, levels)
            advance(
                load_beyond, lambda c: coef_beyond[c], masks_beyond, keep_beyond, east, west, 8, levels
            )
            after.append((tuple(new_below), tuple(new_beyond)))
        return tuple(after)

    start = tuple(
        (
            tuple(state[0, i, brim, :] for i in range(4 * levels)),
            tuple(beyond[i, strip, :] for i in range(4 * levels)),
        )
        for levels, state, beyond in ((LEVELS, main, top_main), (1, edge, top_edge))
    )
    done = lax.fori_loop(0, STEPS, north_side, start)
    for state, (below, _) in zip((main, edge), done):
        for i, x in enumerate(below):
            state[STEPS, i, brim, :] = x

    def finish(first, here, there):
        lane = lanes((FINISH, N))
        for g, ref in enumerate((u_out, v_out, t_out, s_out)):
            x = edge[STEPS, g, there, :]
            for k in range(LEVELS):
                y = main[STEPS, 3 * g + k, there, :]
                y = jnp.where(lane < WIDE, turned(x, -(GROUP * k + WEST_OWN)), y)
                sides = turned(x, N - SLIM - (GROUP * k + EAST_HALO - SLIM))
                ref[k, here, :] = jnp.where(lane >= N - SLIM, sides, y)

    sweep(finish, FINISH)

    for c in to_east + to_west:
        c.wait_send()

    @pl.when(inner)
    def _():
        for c in (to_north, to_ne, to_nw):
            c.wait_send()

    @pl.when(raised)
    def _():
        for c in (to_south, to_se, to_sw):
            c.wait_send()

    @pl.when(top)
    def _():
        to_fold.wait_send()

        @pl.when(fold_up != z)
        def _():
            to_fold_up.wait_send()

        @pl.when(fold_down != z)
        def _():
            to_fold_down.wait_send()


def deliver(*refs):
    copies = [pltpu.make_async_copy(refs[i], refs[4 + i], refs[8].at[i]) for i in range(4)]
    for c in copies:
        c.start()
    for c in copies:
        c.wait()


def per_device(u, v, t, s, hx, hy, f, cell, zonal, merid, hinge):
    def buf(*shape):
        return pltpu.VMEM(shape + (N,), jnp.float32)

    vmem = pl.BlockSpec(memory_space=pltpu.VMEM)
    shape = jax.ShapeDtypeStruct((LEVELS, N, N), jnp.float32)
    results = pl.pallas_call(
        kernel,
        out_shape=(pltpu.VMEM((LEVELS, N, N), jnp.float32),) * 4,
        in_specs=[pl.BlockSpec(memory_space=pltpu.HBM)] * 11,
        out_specs=(vmem,) * 4,
        scratch_shapes=[buf(LEVELS, N)] * 4
        + [buf(N)] * 3
        + [pltpu.VMEM((LEVELS, N, N), jnp.int32)] * 3
        + [pltpu.SMEM((4,), jnp.int32)]
        + [
            buf(5, 12, ROWS),
            buf(5, 4, ROWS),
            buf(12, 8),
            buf(4, 8),
            buf(4, 6, ROWS),
            buf(4, 2, ROWS),
            buf(9, ROWS),
            buf(3, ROWS),
            buf(9, 8),
            buf(3, 8),
            buf(3, 8),
            buf(3, 8),
            buf(3, ROWS),
            buf(11, ROWS),
            buf(11, ROWS),
            buf(11, 8),
            buf(11, 8),
            buf(N),
            buf(N),
            buf(96),
            buf(72),
            buf(18, 8),
            buf(8),
            buf(8),
            buf(N),
            buf(N),
            buf(96),
            buf(72),
            buf(96),
            buf(4, 8),
            pltpu.SemaphoreType.DMA((11 + 2 * PARTS,)),
            pltpu.SemaphoreType.DMA((11 + 2 * PARTS,)),
            pltpu.SemaphoreType.DMA((2,)),
            pltpu.SemaphoreType.DMA((11,)),
        ],
        compiler_params=pltpu.CompilerParams(
            collective_id=0, has_side_effects=True, vmem_limit_bytes=60 * 1024 * 1024
        ),
        name="halo_steps",
    )(u, v, t, s, hx, hy, f, cell, zonal, merid, hinge)


    return pl.pallas_call(
        deliver,
        out_shape=(shape,) * 4,
        in_specs=[vmem] * 4,
        out_specs=(pl.BlockSpec(memory_space=pl.ANY),) * 4,
        scratch_shapes=[pltpu.SemaphoreType.DMA((4,))],
        name="deliver",
    )(*(pltpu.with_memory_space_constraint(r, pltpu.VMEM) for r in results))


def solution(mesh):
    field, plain = P(None, "merid", "zonal"), P("merid", "zonal")
    return jax.shard_map(
        per_device,
        mesh=mesh,
        in_specs=(field,) * 4 + (plain,) * 3 + (field,) * 3 + (P(),),
        out_specs=(field,) * 4,
        check_vma=False,
    )
```

```python
import jax
import jax.numpy as jnp
from jax import lax
from jax.experimental import pallas as pl
from jax.experimental.pallas import tpu as pltpu
from jax.sharding import PartitionSpec as P

STEPS = 4
LEVELS = 3
TIME_STEP = 0.25
VISCOSITY = 0.25
DIFFUSIVITY = 0.25

MESH = pl.DeviceIdType.MESH

N = 128
OFF = 16
ROWS = 160
CHUNK = 128
FILL = PACK = PREPARE = UNPACK = READY = 128
PARTS = 1
PIECE = N // PARTS
WIDE = 5
SLIM = 4
GROUP = 42
WEST_OWN = WIDE
EAST_FIRST = WIDE + 9
EAST_HALO = EAST_FIRST + 9
CA, CB, CC, CF, CGX, CGY, CHX, CHY, CDX, CDY, CK = range(11)
SIGN = (-1.0, -1.0, 1.0, 1.0)


def sweep(body, size):
    def step(i, carry):
        first = pl.multiple_of(i * size, 8)
        body(first, pl.ds(first, size), pl.ds(pl.multiple_of(OFF + first, 8), size))
        return carry

    lax.fori_loop(0, N // size, step, 0)


def turned(x, shift):
    if isinstance(shift, int):
        shift %= N
        if shift == 0:
            return x
    return pltpu.roll(x, shift, 1)


def lanes(shape):
    return lax.broadcasted_iota(jnp.int32, shape, 1)


def coefficients(hx, hy, f):
    rx = 1.0 / hx
    ry = 1.0 / hy
    a = (TIME_STEP * VISCOSITY) * rx * rx
    b = (TIME_STEP * VISCOSITY) * ry * ry
    return (
        a,
        b,
        1.0 - 2.0 * (a + b),
        (0.5 * TIME_STEP) * f,
        TIME_STEP * rx,
        TIME_STEP * ry,
        0.5 * hx,
        0.5 * hy,
        DIFFUSIVITY * hy * rx,
        DIFFUSIVITY * hx * ry,
        TIME_STEP * rx * ry,
    )


def weights(t, s, lane):
    half = [0.25 * a - 0.2 * b for a, b in zip(t, s)]
    if len(half) == 1:
        one = jnp.where(lane >= GROUP, turned(half[0], GROUP), 0.0)
        two = jnp.where(lane >= 2 * GROUP, turned(half[0], 2 * GROUP), 0.0)
        return [half[0] + 2.0 * (one + two)]
    out = [half[0]]
    for k in range(1, LEVELS):
        out.append(out[-1] + (half[k - 1] + half[k]))
    return out


def advance(load, coef, masks, keep, east, west, rows, levels):
    lane = lanes((rows, N))
    span = range(levels)
    t = [load(2, k, 0) for k in span]
    s = [load(3, k, 0) for k in span]
    tn = [load(2, k, 1) for k in span]
    sn = [load(3, k, 1) for k in span]
    p = weights(t, s, lane)
    pn = weights(tn, sn, lane)
    te = [turned(x, east) for x in t]
    se = [turned(x, east) for x in s]
    if levels == 1:
        dp = [turned(p[0], east) - p[0]]
    else:
        dp = weights([a - b for a, b in zip(te, t)], [a - b for a, b in zip(se, s)], lane)
    for k in span:
        u, v = load(0, k, 0), load(1, k, 0)
        us, vs = load(0, k, -1), load(1, k, -1)
        uw = turned(u, west)
        mu, mv, mc = masks(k)
        un = mu * (
            coef(CC) * u
            + coef(CA) * (turned(u, east) + uw)
            + coef(CB) * (load(0, k, 1) + us)
            + coef(CF) * (v + vs)
            - coef(CGX) * dp[k]
        )
        vn = mv * (
            coef(CC) * v
            + coef(CA) * (turned(v, east) + turned(v, west))
            + coef(CB) * (load(1, k, 1) + vs)
            - coef(CF) * (u + uw)
            - coef(CGY) * (pn[k] - p[k])
        )
        keep(0, k, un)
        keep(1, k, vn)
        q, d = coef(CHY) * un, coef(CDX) * mu
        qp, qm = q + d, q - d
        r, e = coef(CHX) * vn, coef(CDY) * mv
        rp, rm = r + e, r - e
        scale = mc * coef(CK)
        for which, c, ce, cn in ((2, t[k], te[k], tn[k]), (3, s[k], se[k], sn[k])):
            fe = qp * c + qm * ce
            fn = rp * c + rm * cn
            below = keep(which + 2, k, fn)
            keep(which, k, c - scale * ((fe - turned(fe, west)) + (fn - below)))


def pack_wide(plane, rows):
    lane = lanes((rows, N))
    out = None
    for k in range(LEVELS):
        for g in range(8):
            first = GROUP * k + WIDE * g
            part = turned(plane(g, k), first - (N - WIDE))
            out = part if out is None else jnp.where(lane >= first, part, out)
    return out


def pack_slim(plane, rows):
    lane = lanes((rows, N))
    out = None
    for k in range(LEVELS):
        for g in range(8):
            first = GROUP * k + SLIM * g
            part = turned(plane(g, k), first)
            out = part if out is None else jnp.where(lane >= first, part, out)
    return out


def pack_own(plane, g, rows):
    lane = lanes((rows, N))
    out = None
    for k in range(LEVELS):
        x = plane(g, k)
        for first, column in ((GROUP * k + WEST_OWN, 0), (GROUP * k + EAST_FIRST, N - 9)):
            part = turned(x, first - column)
            out = part if out is None else jnp.where(lane >= first, part, out)
    return out


def merge_halo(own, wide, slim, g, rows):
    lane = lanes((rows, N))
    place = lane - jnp.where(lane >= 2 * GROUP, 2 * GROUP, jnp.where(lane >= GROUP, GROUP, 0))
    own = jnp.where(place < WIDE, turned(wide, -WIDE * g), own)
    east = (place >= EAST_HALO) & (place < EAST_HALO + SLIM)
    return jnp.where(east, turned(slim, EAST_HALO - SLIM * g), own)


def flipped(x):
    lane = lanes(x.shape)
    for bit in (64, 32, 16, 8, 4, 2, 1):
        if bit == 64:
            x = turned(x, 64)
        else:
            x = jnp.where((lane & bit) != 0, turned(x, bit), turned(x, -bit))
    return x


def kernel(
    u_hbm,
    v_hbm,
    t_hbm,
    s_hbm,
    hx_hbm,
    hy_hbm,
    f_hbm,
    cell_hbm,
    zonal_hbm,
    merid_hbm,
    hinge_hbm,
    main_out,
    edge_out,
    u_ref,
    v_ref,
    t_ref,
    s_ref,
    hx_ref,
    hy_ref,
    f_ref,
    cell_ref,
    zonal_ref,
    merid_ref,
    hinge,
    main,
    edge,
    top_main,
    top_edge,
    flux_main,
    flux_edge,
    mask_main,
    mask_edge,
    mask_top_main,
    mask_top_edge,
    metric_main,
    metric_top,
    metric_edge,
    coef_main,
    coef_edge,
    coef_top_main,
    coef_top_edge,
    east_buf,
    west_buf,
    north_buf,
    south_buf,
    fold_tile,
    fold_west,
    fold_east,
    from_west,
    from_east,
    from_south,
    from_north,
    from_fold,
    from_corner,
    send_sem,
    recv_sem,
    local_sem,
    load_sem,
):
    sources = (u_hbm, v_hbm, t_hbm, s_hbm, cell_hbm, zonal_hbm, merid_hbm, hx_hbm, hy_hbm, f_hbm, hinge_hbm)
    targets = (u_ref, v_ref, t_ref, s_ref, cell_ref, zonal_ref, merid_ref, hx_ref, hy_ref, f_ref, hinge)
    loads = [
        pltpu.make_async_copy(src, dst, load_sem.at[i])
        for i, (src, dst) in enumerate(zip(sources, targets))
    ]
    for c in loads:
        c.start()

    nz, nm = lax.axis_size("zonal"), lax.axis_size("merid")
    z, m = lax.axis_index("zonal"), lax.axis_index("merid")
    east_z, west_z = lax.rem(z + 1, nz), lax.rem(z + nz - 1, nz)
    fold_z = nz - 1 - z
    fold_up, fold_down = lax.rem(fold_z + 1, nz), lax.rem(fold_z + nz - 1, nz)
    top, bottom = m == nm - 1, m == 0
    inner = jnp.logical_not(top)
    raised = jnp.logical_not(bottom)

    def at(zz, mm):
        return {"zonal": zz, "merid": mm}

    barrier = pltpu.get_barrier_semaphore()

    def hail(zz, mm):
        pl.semaphore_signal(barrier, inc=1, device_id=at(zz, mm), device_id_type=MESH)

    hail(east_z, m)
    hail(west_z, m)

    @pl.when(raised)
    def _():
        for zz in (west_z, z, east_z):
            hail(zz, m - 1)

    @pl.when(inner)
    def _():
        for zz in (west_z, z, east_z):
            hail(zz, m + 1)

    @pl.when(top)
    def _():
        hail(fold_z, m)

        @pl.when(fold_up != z)
        def _():
            hail(fold_up, m)

        @pl.when(fold_down != z)
        def _():
            hail(fold_down, m)

    for c in loads:
        c.wait()
    fields = (u_ref, v_ref, t_ref, s_ref)

    def fill(first, here, there):
        for k in range(LEVELS):
            mu = zonal_ref[k, here, :].astype(jnp.float32)
            mv = merid_ref[k, here, :].astype(jnp.float32)
            mc = cell_ref[k, here, :].astype(jnp.float32)
            mask_main[k, there, :] = mu
            mask_main[3 + k, there, :] = mv
            mask_main[6 + k, there, :] = mc
            for g, ref in enumerate(fields):
                main[0, 3 * g + k, there, :] = ref[k, here, :] * (mu, mv, mc, mc)[g]

    sweep(fill, FILL)

    def plane_at(start, rows):
        def plane(g, k):
            if g < 4:
                return main[0, 3 * g + k, pl.ds(OFF + start, rows), :]
            if g == 4:
                return mask_main[6 + k, pl.ds(OFF + start, rows), :]
            return (hx_ref, hy_ref, f_ref)[g - 5][pl.ds(start, rows), :]

        return plane

    def number(g, k):
        return 3 * g + k if g < 5 else 15 + g - 5

    every = [(g, k) for g in range(5) for k in range(LEVELS)] + [(g, 0) for g in (5, 6, 7)]

    @pl.when(inner)
    def _():
        for g, k in every:
            i = number(g, k)
            north_buf[pl.ds(WIDE * i, WIDE), :] = plane_at(N - WIDE, WIDE)(g, k)

    @pl.when(top)
    def _():
        plane = plane_at(N - 8, 8)
        for g, k in every:
            i = number(g, k)
            tile = flipped(plane(g, k))
            fold_tile[i, :, :] = tile
            north_buf[pl.ds(WIDE * i, WIDE), :] = tile[8 - WIDE :, :]
            if g == 1:
                north_buf[pl.ds(90 + k, 1), :] = tile[2:3, :]

        def mirrored(g, k):
            return fold_tile[number(g, k)]

        fold_west[...] = pack_wide(mirrored, 8)
        fold_east[...] = pack_slim(mirrored, 8)

    def copy(src, dst, slot, zz, mm):
        return pltpu.make_async_remote_copy(
            src_ref=src,
            dst_ref=dst,
            send_sem=send_sem.at[slot],
            recv_sem=recv_sem.at[slot],
            device_id=at(zz, mm),
            device_id_type=MESH,
        )

    corner = lambda i: from_corner.at[i]
    low, high = pl.ds(0, 8), pl.ds(N - 8, 8)
    to_east, to_west = [], []
    for i in range(PARTS):
        piece = pl.ds(i * PIECE, PIECE)
        to_east.append(copy(east_buf.at[piece], from_west.at[piece], 11 + 2 * i, east_z, m))
        to_west.append(copy(west_buf.at[piece], from_east.at[piece], 12 + 2 * i, west_z, m))
    to_north = copy(north_buf, from_south, 2, z, m + 1)
    to_south = copy(south_buf, from_north, 3, z, m - 1)
    to_fold = copy(north_buf, from_fold, 4, fold_z, m)
    to_ne = copy(east_buf.at[high], corner(0), 5, east_z, m + 1)
    to_nw = copy(west_buf.at[high], corner(1), 6, west_z, m + 1)
    to_se = copy(east_buf.at[low], corner(2), 7, east_z, m - 1)
    to_sw = copy(west_buf.at[low], corner(3), 8, west_z, m - 1)
    to_fold_up = copy(fold_west, corner(2), 9, fold_up, m)
    to_fold_down = copy(fold_east, corner(3), 10, fold_down, m)
    keep_fold_up = pltpu.make_async_copy(fold_west, corner(2), local_sem.at[0])
    keep_fold_down = pltpu.make_async_copy(fold_east, corner(3), local_sem.at[1])

    same = jnp.where(fold_up == z, 1, 0) + jnp.where(fold_down == z, 1, 0)
    pl.semaphore_wait(barrier, 2 + jnp.where(bottom, 0, 3) + 3 - jnp.where(top, same, 0))

    @pl.when(top)
    def _():
        to_fold.start()

        @pl.when(fold_up != z)
        def _():
            to_fold_up.start()

        @pl.when(fold_up == z)
        def _():
            keep_fold_up.start()

        @pl.when(fold_down != z)
        def _():
            to_fold_down.start()

        @pl.when(fold_down == z)
        def _():
            keep_fold_down.start()

    @pl.when(inner)
    def _():
        to_north.start()

    for g, k in every:
        south_buf[pl.ds(SLIM * number(g, k), SLIM), :] = plane_at(0, SLIM)(g, k)

    @pl.when(raised)
    def _():
        to_south.start()

    for i in range(PARTS):
        plane = plane_at(i * PIECE, PIECE)
        east_buf[pl.ds(i * PIECE, PIECE), :] = pack_wide(plane, PIECE)
        to_east[i].start()
        west_buf[pl.ds(i * PIECE, PIECE), :] = pack_slim(plane, PIECE)
        to_west[i].start()

    @pl.when(inner)
    def _():
        to_ne.start()
        to_nw.start()

    @pl.when(raised)
    def _():
        to_se.start()
        to_sw.start()

    def prepare(first, here, there):
        for c, x in enumerate(coefficients(hx_ref[here, :], hy_ref[here, :], f_ref[here, :])):
            coef_main[c, there, :] = x
        plane = plane_at(first, PREPARE)
        for g in range(8):
            x = pack_own(plane, g, PREPARE)
            if g < 4:
                edge[0, g, there, :] = x
            elif g == 4:
                mask_edge[2, there, :] = x
            else:
                metric_edge[g - 5, there, :] = x

    sweep(prepare, PREPARE)

    def step_rows(n, start, rows, state, flux, mask, coef, levels, align=True):
        def at_row(dj):
            first = OFF + start + dj
            if dj == 0 and align:
                first = pl.multiple_of(first, 8)
            return pl.ds(first, rows)

        def load(g, k, dj):
            return state[n, levels * g + k, at_row(dj), :]

        def keep(g, k, x):
            if g < 4:
                state[n + 1, levels * g + k, at_row(0), :] = x
                return None
            flux[n, levels * (g - 4) + k, at_row(0), :] = x
            return flux[n, levels * (g - 4) + k, at_row(-1), :]

        def masks(k):
            return [mask[levels * i + k, at_row(0), :] for i in range(3)]

        advance(load, lambda c: coef[c, at_row(0), :], masks, keep, N - 1, 1, rows, levels)

    def interior(n, carry):
        def chunk(i, inside):
            step_rows(n, i * CHUNK, CHUNK, main, flux_main, mask_main, coef_main, LEVELS)
            return inside

        return lax.fori_loop(0, N // CHUNK, chunk, carry)

    lax.fori_loop(0, STEPS, interior, 0)

    halo = pl.ds(OFF - 8, 8)

    @pl.when(raised)
    def _():
        to_north.wait_recv()
        to_ne.wait_recv()
        to_nw.wait_recv()
        last = pl.ds(OFF - WIDE, WIDE)
        for g, k in every:
            x = from_south[pl.ds(WIDE * number(g, k), WIDE), :]
            if g < 4:
                main[0, 3 * g + k, last, :] = x
            elif g == 4:
                mask_main[6 + k, last, :] = x
            else:
                metric_main[g - 5, pl.ds(8 - WIDE, WIDE), :] = x

    @pl.when(bottom)
    def _():
        zero = jnp.zeros((8, N), jnp.float32)
        for g, k in every:
            if g < 4:
                main[0, 3 * g + k, halo, :] = zero
            elif g == 4:
                mask_main[6 + k, halo, :] = zero
            else:
                metric_main[g - 5, :, :] = zero + 1.0
        for i in (0, 1):
            from_corner[i, :, :] = zero

    for k in range(LEVELS):
        mc = mask_main[6 + k, halo, :]
        mask_main[k, halo, :] = mc * turned(mc, N - 1)
        mask_main[3 + k, halo, :] = mc * mask_main[6 + k, pl.ds(OFF - 7, 8), :]
    for c, x in enumerate(coefficients(metric_main[0], metric_main[1], metric_main[2])):
        coef_main[c, halo, :] = x

    for c in to_east + to_west:
        c.wait_recv()

    def edge_keep(g, rows, x, offset=0):
        if g < 4:
            edge[0, g, rows, :] = x
        elif g == 4:
            mask_edge[2, rows, :] = x
        else:
            metric_edge[g - 5, rows, :] = x

    def south_plane(g, k):
        if g < 4:
            return main[0, 3 * g + k, halo, :]
        if g == 4:
            return mask_main[6 + k, halo, :]
        return metric_main[g - 5, :, :]

    for g in range(8):
        x = pack_own(south_plane, g, 8)
        x = merge_halo(x, from_corner[0], from_corner[1], g, 8)
        if g in (5, 6):
            x = jnp.where(bottom, 1.0, x)
        edge_keep(g, halo, x)

    def unpack(first, here, there):
        wide = from_west[here, :]
        slim = from_east[here, :]
        for g in range(8):
            if g < 4:
                x = edge[0, g, there, :]
            elif g == 4:
                x = mask_edge[2, there, :]
            else:
                x = metric_edge[g - 5, there, :]
            edge_keep(g, there, merge_halo(x, wide, slim, g, UNPACK))

    sweep(unpack, UNPACK)

    def edge_masks(start, rows):
        there = pl.ds(start, rows)
        mc = mask_edge[2, there, :]
        mask_edge[0, there, :] = mc * turned(mc, N - 1)
        mask_edge[1, there, :] = mc * mask_edge[2, pl.ds(start + 1, rows), :]

    def edge_ready(start, rows):
        there = pl.ds(start, rows)
        for c, x in enumerate(
            coefficients(metric_edge[0, there, :], metric_edge[1, there, :], metric_edge[2, there, :])
        ):
            coef_edge[c, there, :] = x

    edge_masks(OFF - 8, 8)
    edge_ready(OFF - 8, 8)

    def ready(first, here, there):
        edge_masks(OFF + first, READY)
        edge_ready(OFF + first, READY)

    sweep(ready, READY)

    strip = pl.ds(0, 8)
    for g, k in every:
        if g < 4:
            top_main[3 * g + k, strip, :] = jnp.zeros((8, N), jnp.float32)
        elif g == 4:
            mask_top_main[6 + k, strip, :] = jnp.zeros((8, N), jnp.float32)
        else:
            metric_top[g - 5, :, :] = jnp.ones((8, N), jnp.float32)

    def top_keep(g, k, first, x):
        rows = pl.ds(first, x.shape[0])
        if g < 4:
            top_main[3 * g + k, rows, :] = x
        elif g == 4:
            mask_top_main[6 + k, rows, :] = x
        else:
            metric_top[g - 5, pl.ds(first, x.shape[0]), :] = x

    @pl.when(inner)
    def _():
        to_south.wait_recv()
        to_se.wait_recv()
        to_sw.wait_recv()
        for g, k in every:
            top_keep(g, k, 0, from_north[pl.ds(SLIM * number(g, k), SLIM), :])

    @pl.when(top)
    def _():
        to_fold.wait_recv()

        @pl.when(fold_up != z)
        def _():
            to_fold_up.wait_recv()

        @pl.when(fold_up == z)
        def _():
            keep_fold_up.wait()

        @pl.when(fold_down != z)
        def _():
            to_fold_down.wait_recv()

        @pl.when(fold_down == z)
        def _():
            keep_fold_down.wait()

        for g, k in every:
            top_keep(g, k, 8 - WIDE, from_fold[pl.ds(WIDE * number(g, k), WIDE), :])
        for k in range(LEVELS):
            top_keep(1, k, 2, from_fold[pl.ds(90 + k, 1), :])

    east = jnp.where(top, 1, N - 1)
    west = jnp.where(top, N - 1, 1)

    def top_plane(g, k):
        if g < 4:
            return top_main[3 * g + k, strip, :]
        if g == 4:
            return mask_top_main[6 + k, strip, :]
        return metric_top[g - 5, :, :]

    edge_metric = []
    for g in range(8):
        x = merge_halo(pack_own(top_plane, g, 8), from_corner[2], from_corner[3], g, 8)
        if g < 4:
            top_edge[g, strip, :] = x
        elif g == 4:
            mask_top_edge[2, strip, :] = x
        else:
            edge_metric.append(x)
    for c, x in enumerate(coefficients(*edge_metric)):
        coef_top_edge[c, :, :] = x
    for c, x in enumerate(coefficients(metric_top[0], metric_top[1], metric_top[2])):
        coef_top_main[c, :, :] = x
    row = lax.broadcasted_iota(jnp.int32, (8, N), 0)
    mc = mask_edge[2, pl.ds(OFF + N - 8, 8), :]
    over = jnp.where(top, 1.0, pltpu.roll(mask_top_edge[2, strip, :], 7, 0))
    mask_edge[1, pl.ds(OFF + N - 8, 8), :] = mc * jnp.where(row == 7, over, pltpu.roll(mc, 7, 0))
    for mask, levels in ((mask_top_main, LEVELS), (mask_top_edge, 1)):
        for k in range(levels):
            mc = mask[2 * levels + k, strip, :]
            mask[k, strip, :] = mc * turned(mc, east)
            mask[levels + k, strip, :] = mc * jnp.where(row == 7, 1.0, pltpu.roll(mc, 7, 0))

    plain = [jnp.full((1, N), hinge[g], jnp.int32) == 0 for g in range(4)]

    first_row, last_row = row == 0, row == 7
    brim, under = pl.ds(OFF + N - 8, 8), pl.ds(OFF + N - 16, 8)

    def up(x):
        return pltpu.roll(x, 7, 0)

    def down(x):
        return pltpu.roll(x, 1, 0)

    kinds = (
        (LEVELS, main, flux_main, mask_main, mask_top_main, coef_main, coef_top_main),
        (1, edge, flux_edge, mask_edge, mask_top_edge, coef_edge, coef_top_edge),
    )

    def outer(n, carry):
        step_rows(n, n - WIDE, 8, main, flux_main, mask_main, coef_main, LEVELS, False)
        step_rows(n, -8, 8, edge, flux_edge, mask_edge, coef_edge, 1)
        step_rows(n, 0, N - 8, edge, flux_edge, mask_edge, coef_edge, 1)
        after = []
        for (levels, state, flux, mask, mask_beyond, coef, coef_beyond), (below, beyond) in zip(
            kinds, carry
        ):
            new_below, new_beyond, fluxes = [None] * len(below), [None] * len(beyond), {}

            def load_below(g, k, dj):
                c, z = below[levels * g + k], beyond[levels * g + k]
                if dj == 0:
                    return c
                if dj < 0:
                    return jnp.where(first_row, down(state[n, levels * g + k, under, :]), down(c))
                ghost = SIGN[g] * jnp.where(plain[g], z, down(turned(z, 1)))
                return jnp.where(last_row, jnp.where(top, ghost, up(z)), up(c))

            def load_beyond(g, k, dj):
                c, z = below[levels * g + k], beyond[levels * g + k]
                if dj == 0:
                    return z
                if dj < 0:
                    return jnp.where(first_row, down(c), down(z))
                ghost = SIGN[g] * jnp.where(plain[g], c, down(turned(c, N - 1)))
                return jnp.where(last_row, ghost, up(z))

            def keep_below(g, k, x):
                if g < 4:
                    new_below[levels * g + k] = x
                    return None
                fluxes[g, k] = down(x)
                return jnp.where(
                    first_row, down(flux[n, levels * (g - 4) + k, under, :]), fluxes[g, k]
                )

            def keep_beyond(g, k, x):
                if g < 4:
                    new_beyond[levels * g + k] = x
                    return None
                return jnp.where(first_row, fluxes[g, k], down(x))

            def masks(k):
                return [mask[levels * i + k, brim, :] for i in range(3)]

            def masks_beyond(k):
                return [mask_beyond[levels * i + k, strip, :] for i in range(3)]

            advance(load_below, lambda c: coef[c, brim, :], masks, keep_below, N - 1, 1, 8, levels)
            advance(
                load_beyond, lambda c: coef_beyond[c], masks_beyond, keep_beyond, east, west, 8, levels
            )
            if levels == 1:
                for i, x in enumerate(new_below):
                    state[n + 1, i, brim, :] = x
            after.append((tuple(new_below), tuple(new_beyond)))
        return tuple(after)

    start = tuple(
        (
            tuple(state[0, i, brim, :] for i in range(4 * levels)),
            tuple(beyond[i, strip, :] for i in range(4 * levels)),
        )
        for levels, state, beyond in ((LEVELS, main, top_main), (1, edge, top_edge))
    )
    done = lax.fori_loop(0, STEPS, outer, start)
    for i, x in enumerate(done[0][0]):
        main[STEPS, i, brim, :] = x

    inside = pl.ds(OFF, N)
    for i in range(4 * LEVELS):
        main_out[i, :, :] = main[STEPS, i, inside, :]
    for i in range(4):
        edge_out[i, :, :] = edge[STEPS, i, inside, :]

    for c in to_east + to_west:
        c.wait_send()

    @pl.when(inner)
    def _():
        for c in (to_north, to_ne, to_nw):
            c.wait_send()

    @pl.when(raised)
    def _():
        for c in (to_south, to_se, to_sw):
            c.wait_send()

    @pl.when(top)
    def _():
        to_fold.wait_send()

        @pl.when(fold_up != z)
        def _():
            to_fold_up.wait_send()

        @pl.when(fold_down != z)
        def _():
            to_fold_down.wait_send()


def deliver(main_ref, edge_ref, u_out, v_out, t_out, s_out, held, sem):
    lane = lanes((N, N))
    copies = []
    for g, out in enumerate((u_out, v_out, t_out, s_out)):
        x = edge_ref[g]
        for k in range(LEVELS):
            y = main_ref[3 * g + k]
            y = jnp.where(lane < WIDE, turned(x, -(GROUP * k + WEST_OWN)), y)
            sides = turned(x, N - SLIM - (GROUP * k + EAST_HALO - SLIM))
            held[3 * g + k, :, :] = jnp.where(lane >= N - SLIM, sides, y)
        c = pltpu.make_async_copy(held.at[pl.ds(3 * g, LEVELS)], out, sem.at[g])
        c.start()
        copies.append(c)
    for c in copies:
        c.wait()


def per_device(u, v, t, s, hx, hy, f, cell, zonal, merid, hinge):
    def buf(*shape):
        return pltpu.VMEM(shape + (N,), jnp.float32)

    vmem = pl.BlockSpec(memory_space=pltpu.VMEM)
    shape = jax.ShapeDtypeStruct((LEVELS, N, N), jnp.float32)
    results = pl.pallas_call(
        kernel,
        out_shape=(
            pltpu.VMEM((4 * LEVELS, N, N), jnp.float32),
            pltpu.VMEM((4, N, N), jnp.float32),
        ),
        in_specs=[pl.BlockSpec(memory_space=pltpu.HBM)] * 11,
        out_specs=(vmem,) * 2,
        scratch_shapes=[buf(LEVELS, N)] * 4
        + [buf(N)] * 3
        + [pltpu.VMEM((LEVELS, N, N), jnp.int32)] * 3
        + [pltpu.SMEM((4,), jnp.int32)]
        + [
            buf(5, 12, ROWS),
            buf(5, 4, ROWS),
            buf(12, 8),
            buf(4, 8),
            buf(4, 6, ROWS),
            buf(4, 2, ROWS),
            buf(9, ROWS),
            buf(3, ROWS),
            buf(9, 8),
            buf(3, 8),
            buf(3, 8),
            buf(3, 8),
            buf(3, ROWS),
            buf(11, ROWS),
            buf(11, ROWS),
            buf(11, 8),
            buf(11, 8),
            buf(N),
            buf(N),
            buf(96),
            buf(72),
            buf(18, 8),
            buf(8),
            buf(8),
            buf(N),
            buf(N),
            buf(96),
            buf(72),
            buf(96),
            buf(4, 8),
            pltpu.SemaphoreType.DMA((11 + 2 * PARTS,)),
            pltpu.SemaphoreType.DMA((11 + 2 * PARTS,)),
            pltpu.SemaphoreType.DMA((2,)),
            pltpu.SemaphoreType.DMA((11,)),
        ],
        compiler_params=pltpu.CompilerParams(
            collective_id=0, has_side_effects=True, vmem_limit_bytes=60 * 1024 * 1024
        ),
        name="halo_steps",
    )(u, v, t, s, hx, hy, f, cell, zonal, merid, hinge)


    return pl.pallas_call(
        deliver,
        out_shape=(shape,) * 4,
        in_specs=[vmem] * 2,
        out_specs=(pl.BlockSpec(memory_space=pl.ANY),) * 4,
        scratch_shapes=[buf(4 * LEVELS, N), pltpu.SemaphoreType.DMA((4,))],
        name="deliver",
    )(*(pltpu.with_memory_space_constraint(r, pltpu.VMEM) for r in results))


def solution(mesh):
    field, plain = P(None, "merid", "zonal"), P("merid", "zonal")
    return jax.shard_map(
        per_device,
        mesh=mesh,
        in_specs=(field,) * 4 + (plain,) * 3 + (field,) * 3 + (P(),),
        out_specs=(field,) * 4,
        check_vma=False,
    )
```

```python
import jax
import jax.numpy as jnp
from jax import lax
from jax.experimental import pallas as pl
from jax.experimental.pallas import tpu as pltpu
from jax.sharding import PartitionSpec as P

STEPS = 4
LEVELS = 3
TIME_STEP = 0.25
VISCOSITY = 0.25
DIFFUSIVITY = 0.25

MESH = pl.DeviceIdType.MESH

N = 128
OFF = 16
ROWS = 160
CHUNK = 128
FILL = PACK = PREPARE = UNPACK = READY = 128
PARTS = 1
PIECE = N // PARTS
WIDE = 5
SLIM = 4
GROUP = 42
WEST_OWN = WIDE
EAST_FIRST = WIDE + 9
EAST_HALO = EAST_FIRST + 9
CA, CB, CC, CF, CGX, CGY, CHX, CHY, CDX, CDY, CK = range(11)
SIGN = (-1.0, -1.0, 1.0, 1.0)


def sweep(body, size):
    def step(i, carry):
        first = pl.multiple_of(i * size, 8)
        body(first, pl.ds(first, size), pl.ds(pl.multiple_of(OFF + first, 8), size))
        return carry

    lax.fori_loop(0, N // size, step, 0)


def turned(x, shift):
    if isinstance(shift, int):
        shift %= N
        if shift == 0:
            return x
    return pltpu.roll(x, shift, 1)


def lanes(shape):
    return lax.broadcasted_iota(jnp.int32, shape, 1)


def coefficients(hx, hy, f):
    rx = 1.0 / hx
    ry = 1.0 / hy
    a = (TIME_STEP * VISCOSITY) * rx * rx
    b = (TIME_STEP * VISCOSITY) * ry * ry
    return (
        a,
        b,
        1.0 - 2.0 * (a + b),
        (0.5 * TIME_STEP) * f,
        TIME_STEP * rx,
        TIME_STEP * ry,
        0.5 * hx,
        0.5 * hy,
        DIFFUSIVITY * hy * rx,
        DIFFUSIVITY * hx * ry,
        TIME_STEP * rx * ry,
    )


def weights(t, s, lane):
    half = [0.25 * a - 0.2 * b for a, b in zip(t, s)]
    if len(half) == 1:
        one = jnp.where(lane >= GROUP, turned(half[0], GROUP), 0.0)
        two = jnp.where(lane >= 2 * GROUP, turned(half[0], 2 * GROUP), 0.0)
        return [half[0] + 2.0 * (one + two)]
    out = [half[0]]
    for k in range(1, LEVELS):
        out.append(out[-1] + (half[k - 1] + half[k]))
    return out


def advance(load, coef, masks, keep, east, west, rows, levels):
    lane = lanes((rows, N))
    span = range(levels)
    t = [load(2, k, 0) for k in span]
    s = [load(3, k, 0) for k in span]
    tn = [load(2, k, 1) for k in span]
    sn = [load(3, k, 1) for k in span]
    p = weights(t, s, lane)
    pn = weights(tn, sn, lane)
    te = [turned(x, east) for x in t]
    se = [turned(x, east) for x in s]
    if levels == 1:
        dp = [turned(p[0], east) - p[0]]
    else:
        dp = weights([a - b for a, b in zip(te, t)], [a - b for a, b in zip(se, s)], lane)
    for k in span:
        u, v = load(0, k, 0), load(1, k, 0)
        us, vs = load(0, k, -1), load(1, k, -1)
        uw = turned(u, west)
        mu, mv, mc = masks(k)
        un = mu * (
            coef(CC) * u
            + coef(CA) * (turned(u, east) + uw)
            + coef(CB) * (load(0, k, 1) + us)
            + coef(CF) * (v + vs)
            - coef(CGX) * dp[k]
        )
        vn = mv * (
            coef(CC) * v
            + coef(CA) * (turned(v, east) + turned(v, west))
            + coef(CB) * (load(1, k, 1) + vs)
            - coef(CF) * (u + uw)
            - coef(CGY) * (pn[k] - p[k])
        )
        keep(0, k, un)
        keep(1, k, vn)
        q, d = coef(CHY) * un, coef(CDX) * mu
        qp, qm = q + d, q - d
        r, e = coef(CHX) * vn, coef(CDY) * mv
        rp, rm = r + e, r - e
        scale = mc * coef(CK)
        for which, c, ce, cn in ((2, t[k], te[k], tn[k]), (3, s[k], se[k], sn[k])):
            fe = qp * c + qm * ce
            fn = rp * c + rm * cn
            below = keep(which + 2, k, fn)
            keep(which, k, c - scale * ((fe - turned(fe, west)) + (fn - below)))


def pack_wide(plane, rows):
    lane = lanes((rows, N))
    out = None
    for k in range(LEVELS):
        for g in range(8):
            first = GROUP * k + WIDE * g
            part = turned(plane(g, k), first - (N - WIDE))
            out = part if out is None else jnp.where(lane >= first, part, out)
    return out


def pack_slim(plane, rows):
    lane = lanes((rows, N))
    out = None
    for k in range(LEVELS):
        for g in range(8):
            first = GROUP * k + SLIM * g
            part = turned(plane(g, k), first)
            out = part if out is None else jnp.where(lane >= first, part, out)
    return out


def pack_own(plane, g, rows):
    lane = lanes((rows, N))
    out = None
    for k in range(LEVELS):
        x = plane(g, k)
        for first, column in ((GROUP * k + WEST_OWN, 0), (GROUP * k + EAST_FIRST, N - 9)):
            part = turned(x, first - column)
            out = part if out is None else jnp.where(lane >= first, part, out)
    return out


def merge_halo(own, wide, slim, g, rows):
    lane = lanes((rows, N))
    place = lane - jnp.where(lane >= 2 * GROUP, 2 * GROUP, jnp.where(lane >= GROUP, GROUP, 0))
    own = jnp.where(place < WIDE, turned(wide, -WIDE * g), own)
    east = (place >= EAST_HALO) & (place < EAST_HALO + SLIM)
    return jnp.where(east, turned(slim, EAST_HALO - SLIM * g), own)


def flipped(x):
    lane = lanes(x.shape)
    for bit in (64, 32, 16, 8, 4, 2, 1):
        if bit == 64:
            x = turned(x, 64)
        else:
            x = jnp.where((lane & bit) != 0, turned(x, bit), turned(x, -bit))
    return x


def kernel(
    u_hbm,
    v_hbm,
    t_hbm,
    s_hbm,
    hx_hbm,
    hy_hbm,
    f_hbm,
    cell_hbm,
    zonal_hbm,
    merid_hbm,
    hinge_hbm,
    main_out,
    edge_out,
    u_ref,
    v_ref,
    t_ref,
    s_ref,
    hx_ref,
    hy_ref,
    f_ref,
    cell_ref,
    zonal_ref,
    merid_ref,
    hinge,
    main,
    edge,
    top_main,
    top_edge,
    flux_main,
    flux_edge,
    mask_main,
    mask_edge,
    mask_top_main,
    mask_top_edge,
    metric_main,
    metric_top,
    metric_edge,
    coef_main,
    coef_edge,
    coef_top_main,
    coef_top_edge,
    east_buf,
    west_buf,
    north_buf,
    south_buf,
    fold_tile,
    fold_west,
    fold_east,
    from_west,
    from_east,
    from_south,
    from_north,
    from_fold,
    from_corner,
    send_sem,
    recv_sem,
    local_sem,
    load_sem,
):
    sources = (u_hbm, v_hbm, t_hbm, s_hbm, cell_hbm, zonal_hbm, merid_hbm, hx_hbm, hy_hbm, f_hbm, hinge_hbm)
    targets = (u_ref, v_ref, t_ref, s_ref, cell_ref, zonal_ref, merid_ref, hx_ref, hy_ref, f_ref, hinge)
    loads = [
        pltpu.make_async_copy(src, dst, load_sem.at[i])
        for i, (src, dst) in enumerate(zip(sources, targets))
    ]
    for c in loads:
        c.start()

    nz, nm = lax.axis_size("zonal"), lax.axis_size("merid")
    z, m = lax.axis_index("zonal"), lax.axis_index("merid")
    east_z, west_z = lax.rem(z + 1, nz), lax.rem(z + nz - 1, nz)
    fold_z = nz - 1 - z
    fold_up, fold_down = lax.rem(fold_z + 1, nz), lax.rem(fold_z + nz - 1, nz)
    top, bottom = m == nm - 1, m == 0
    inner = jnp.logical_not(top)
    raised = jnp.logical_not(bottom)

    def at(zz, mm):
        return {"zonal": zz, "merid": mm}

    barrier = pltpu.get_barrier_semaphore()

    def hail(zz, mm):
        pl.semaphore_signal(barrier, inc=1, device_id=at(zz, mm), device_id_type=MESH)

    hail(east_z, m)
    hail(west_z, m)

    @pl.when(raised)
    def _():
        for zz in (west_z, z, east_z):
            hail(zz, m - 1)

    @pl.when(inner)
    def _():
        for zz in (west_z, z, east_z):
            hail(zz, m + 1)

    @pl.when(top)
    def _():
        hail(fold_z, m)

        @pl.when(fold_up != z)
        def _():
            hail(fold_up, m)

        @pl.when(fold_down != z)
        def _():
            hail(fold_down, m)

    for c in loads:
        c.wait()
    fields = (u_ref, v_ref, t_ref, s_ref)

    def fill(first, here, there):
        for k in range(LEVELS):
            mu = zonal_ref[k, here, :].astype(jnp.float32)
            mv = merid_ref[k, here, :].astype(jnp.float32)
            mc = cell_ref[k, here, :].astype(jnp.float32)
            mask_main[k, there, :] = mu
            mask_main[3 + k, there, :] = mv
            mask_main[6 + k, there, :] = mc
            for g, ref in enumerate(fields):
                main[0, 3 * g + k, there, :] = ref[k, here, :] * (mu, mv, mc, mc)[g]

    sweep(fill, FILL)

    def plane_at(start, rows):
        def plane(g, k):
            if g < 4:
                return main[0, 3 * g + k, pl.ds(OFF + start, rows), :]
            if g == 4:
                return mask_main[6 + k, pl.ds(OFF + start, rows), :]
            return (hx_ref, hy_ref, f_ref)[g - 5][pl.ds(start, rows), :]

        return plane

    def number(g, k):
        return 3 * g + k if g < 5 else 15 + g - 5

    every = [(g, k) for g in range(5) for k in range(LEVELS)] + [(g, 0) for g in (5, 6, 7)]

    @pl.when(inner)
    def _():
        for g, k in every:
            i = number(g, k)
            north_buf[pl.ds(WIDE * i, WIDE), :] = plane_at(N - WIDE, WIDE)(g, k)

    @pl.when(top)
    def _():
        plane = plane_at(N - 8, 8)
        for g, k in every:
            i = number(g, k)
            tile = flipped(plane(g, k))
            fold_tile[i, :, :] = tile
            north_buf[pl.ds(WIDE * i, WIDE), :] = tile[8 - WIDE :, :]
            if g == 1:
                north_buf[pl.ds(90 + k, 1), :] = tile[2:3, :]

        def mirrored(g, k):
            return fold_tile[number(g, k)]

        fold_west[...] = pack_wide(mirrored, 8)
        fold_east[...] = pack_slim(mirrored, 8)

    def copy(src, dst, slot, zz, mm):
        return pltpu.make_async_remote_copy(
            src_ref=src,
            dst_ref=dst,
            send_sem=send_sem.at[slot],
            recv_sem=recv_sem.at[slot],
            device_id=at(zz, mm),
            device_id_type=MESH,
        )

    corner = lambda i: from_corner.at[i]
    low, high = pl.ds(0, 8), pl.ds(N - 8, 8)
    to_east, to_west = [], []
    for i in range(PARTS):
        piece = pl.ds(i * PIECE, PIECE)
        to_east.append(copy(east_buf.at[piece], from_west.at[piece], 11 + 2 * i, east_z, m))
        to_west.append(copy(west_buf.at[piece], from_east.at[piece], 12 + 2 * i, west_z, m))
    to_north = copy(north_buf, from_south, 2, z, m + 1)
    to_south = copy(south_buf, from_north, 3, z, m - 1)
    to_fold = copy(north_buf, from_fold, 4, fold_z, m)
    to_ne = copy(east_buf.at[high], corner(0), 5, east_z, m + 1)
    to_nw = copy(west_buf.at[high], corner(1), 6, west_z, m + 1)
    to_se = copy(east_buf.at[low], corner(2), 7, east_z, m - 1)
    to_sw = copy(west_buf.at[low], corner(3), 8, west_z, m - 1)
    to_fold_up = copy(fold_west, corner(2), 9, fold_up, m)
    to_fold_down = copy(fold_east, corner(3), 10, fold_down, m)
    keep_fold_up = pltpu.make_async_copy(fold_west, corner(2), local_sem.at[0])
    keep_fold_down = pltpu.make_async_copy(fold_east, corner(3), local_sem.at[1])

    same = jnp.where(fold_up == z, 1, 0) + jnp.where(fold_down == z, 1, 0)
    pl.semaphore_wait(barrier, 2 + jnp.where(bottom, 0, 3) + 3 - jnp.where(top, same, 0))

    @pl.when(top)
    def _():
        to_fold.start()

        @pl.when(fold_up != z)
        def _():
            to_fold_up.start()

        @pl.when(fold_up == z)
        def _():
            keep_fold_up.start()

        @pl.when(fold_down != z)
        def _():
            to_fold_down.start()

        @pl.when(fold_down == z)
        def _():
            keep_fold_down.start()

    @pl.when(inner)
    def _():
        to_north.start()

    for g, k in every:
        south_buf[pl.ds(SLIM * number(g, k), SLIM), :] = plane_at(0, SLIM)(g, k)

    @pl.when(raised)
    def _():
        to_south.start()

    for i in range(PARTS):
        plane = plane_at(i * PIECE, PIECE)
        east_buf[pl.ds(i * PIECE, PIECE), :] = pack_wide(plane, PIECE)
        to_east[i].start()
        west_buf[pl.ds(i * PIECE, PIECE), :] = pack_slim(plane, PIECE)
        to_west[i].start()

    @pl.when(inner)
    def _():
        to_ne.start()
        to_nw.start()

    @pl.when(raised)
    def _():
        to_se.start()
        to_sw.start()

    def prepare(first, here, there):
        for c, x in enumerate(coefficients(hx_ref[here, :], hy_ref[here, :], f_ref[here, :])):
            coef_main[c, there, :] = x
        plane = plane_at(first, PREPARE)
        for g in range(8):
            x = pack_own(plane, g, PREPARE)
            if g < 4:
                edge[0, g, there, :] = x
            elif g == 4:
                mask_edge[2, there, :] = x
            else:
                metric_edge[g - 5, there, :] = x

    sweep(prepare, PREPARE)

    def step_rows(n, start, rows, state, flux, mask, coef, levels, align=True):
        def at_row(dj):
            first = OFF + start + dj
            if dj == 0 and align:
                first = pl.multiple_of(first, 8)
            return pl.ds(first, rows)

        def load(g, k, dj):
            return state[n, levels * g + k, at_row(dj), :]

        def keep(g, k, x):
            if g < 4:
                state[n + 1, levels * g + k, at_row(0), :] = x
                return None
            flux[n, levels * (g - 4) + k, at_row(0), :] = x
            return flux[n, levels * (g - 4) + k, at_row(-1), :]

        def masks(k):
            return [mask[levels * i + k, at_row(0), :] for i in range(3)]

        advance(load, lambda c: coef[c, at_row(0), :], masks, keep, N - 1, 1, rows, levels)

    def interior(n, carry):
        def chunk(i, inside):
            step_rows(n, i * CHUNK, CHUNK, main, flux_main, mask_main, coef_main, LEVELS)
            return inside

        return lax.fori_loop(0, N // CHUNK, chunk, carry)

    lax.fori_loop(0, STEPS, interior, 0)

    halo = pl.ds(OFF - 8, 8)

    @pl.when(raised)
    def _():
        to_north.wait_recv()
        last = pl.ds(OFF - WIDE, WIDE)
        for g, k in every:
            x = from_south[pl.ds(WIDE * number(g, k), WIDE), :]
            if g < 4:
                main[0, 3 * g + k, last, :] = x
            elif g == 4:
                mask_main[6 + k, last, :] = x
            else:
                metric_main[g - 5, pl.ds(8 - WIDE, WIDE), :] = x

    @pl.when(bottom)
    def _():
        zero = jnp.zeros((8, N), jnp.float32)
        for g, k in every:
            if g < 4:
                main[0, 3 * g + k, halo, :] = zero
            elif g == 4:
                mask_main[6 + k, halo, :] = zero
            else:
                metric_main[g - 5, :, :] = zero + 1.0
        for i in (0, 1):
            from_corner[i, :, :] = zero

    for k in range(LEVELS):
        mc = mask_main[6 + k, halo, :]
        mask_main[k, halo, :] = mc * turned(mc, N - 1)
        mask_main[3 + k, halo, :] = mc * mask_main[6 + k, pl.ds(OFF - 7, 8), :]
    for c, x in enumerate(coefficients(metric_main[0], metric_main[1], metric_main[2])):
        coef_main[c, halo, :] = x

    strip = pl.ds(0, 8)
    for g, k in every:
        if g < 4:
            top_main[3 * g + k, strip, :] = jnp.zeros((8, N), jnp.float32)
        elif g == 4:
            mask_top_main[6 + k, strip, :] = jnp.zeros((8, N), jnp.float32)
        else:
            metric_top[g - 5, :, :] = jnp.ones((8, N), jnp.float32)

    def top_keep(g, k, first, x):
        rows = pl.ds(first, x.shape[0])
        if g < 4:
            top_main[3 * g + k, rows, :] = x
        elif g == 4:
            mask_top_main[6 + k, rows, :] = x
        else:
            metric_top[g - 5, pl.ds(first, x.shape[0]), :] = x

    @pl.when(inner)
    def _():
        to_south.wait_recv()
        for g, k in every:
            top_keep(g, k, 0, from_north[pl.ds(SLIM * number(g, k), SLIM), :])

    @pl.when(top)
    def _():
        to_fold.wait_recv()

        for g, k in every:
            top_keep(g, k, 8 - WIDE, from_fold[pl.ds(WIDE * number(g, k), WIDE), :])
        for k in range(LEVELS):
            top_keep(1, k, 2, from_fold[pl.ds(90 + k, 1), :])

    east = jnp.where(top, 1, N - 1)
    west = jnp.where(top, N - 1, 1)

    def top_plane(g, k):
        if g < 4:
            return top_main[3 * g + k, strip, :]
        if g == 4:
            return mask_top_main[6 + k, strip, :]
        return metric_top[g - 5, :, :]

    for c, x in enumerate(coefficients(metric_top[0], metric_top[1], metric_top[2])):
        coef_top_main[c, :, :] = x
    row = lax.broadcasted_iota(jnp.int32, (8, N), 0)

    def top_masks(mask, levels):
        for k in range(levels):
            mc = mask[2 * levels + k, strip, :]
            mask[k, strip, :] = mc * turned(mc, east)
            mask[levels + k, strip, :] = mc * jnp.where(row == 7, 1.0, pltpu.roll(mc, 7, 0))

    top_masks(mask_top_main, LEVELS)

    plain = [jnp.full((1, N), hinge[g], jnp.int32) == 0 for g in range(4)]

    first_row, last_row = row == 0, row == 7
    brim, under = pl.ds(OFF + N - 8, 8), pl.ds(OFF + N - 16, 8)

    def up(x):
        return pltpu.roll(x, 7, 0)

    def down(x):
        return pltpu.roll(x, 1, 0)

    def north_side(n, carry, levels, state, flux, mask, mask_beyond, coef, coef_beyond):
        below, beyond = carry
        new_below, new_beyond, fluxes = [None] * len(below), [None] * len(beyond), {}

        def load_below(g, k, dj):
            c, z = below[levels * g + k], beyond[levels * g + k]
            if dj == 0:
                return c
            if dj < 0:
                return jnp.where(first_row, down(state[n, levels * g + k, under, :]), down(c))
            ghost = SIGN[g] * jnp.where(plain[g], z, down(turned(z, 1)))
            return jnp.where(last_row, jnp.where(top, ghost, up(z)), up(c))

        def load_beyond(g, k, dj):
            c, z = below[levels * g + k], beyond[levels * g + k]
            if dj == 0:
                return z
            if dj < 0:
                return jnp.where(first_row, down(c), down(z))
            ghost = SIGN[g] * jnp.where(plain[g], c, down(turned(c, N - 1)))
            return jnp.where(last_row, ghost, up(z))

        def keep_below(g, k, x):
            if g < 4:
                new_below[levels * g + k] = x
                return None
            fluxes[g, k] = down(x)
            return jnp.where(
                first_row, down(flux[n, levels * (g - 4) + k, under, :]), fluxes[g, k]
            )

        def keep_beyond(g, k, x):
            if g < 4:
                new_beyond[levels * g + k] = x
                return None
            return jnp.where(first_row, fluxes[g, k], down(x))

        def masks(k):
            return [mask[levels * i + k, brim, :] for i in range(3)]

        def masks_beyond(k):
            return [mask_beyond[levels * i + k, strip, :] for i in range(3)]

        advance(load_below, lambda c: coef[c, brim, :], masks, keep_below, N - 1, 1, 8, levels)
        advance(
            load_beyond, lambda c: coef_beyond[c], masks_beyond, keep_beyond, east, west, 8, levels
        )
        if levels == 1:
            for i, x in enumerate(new_below):
                state[n + 1, i, brim, :] = x
        return tuple(new_below), tuple(new_beyond)

    def main_sides(n, carry):
        step_rows(n, n - WIDE, 8, main, flux_main, mask_main, coef_main, LEVELS, False)
        return north_side(
            n, carry, LEVELS, main, flux_main, mask_main, mask_top_main, coef_main, coef_top_main
        )

    def tiles(levels, state, beyond):
        return (
            tuple(state[0, i, brim, :] for i in range(4 * levels)),
            tuple(beyond[i, strip, :] for i in range(4 * levels)),
        )

    below, _ = lax.fori_loop(0, STEPS, main_sides, tiles(LEVELS, main, top_main))
    for i, x in enumerate(below):
        main[STEPS, i, brim, :] = x

    @pl.when(raised)
    def _():
        to_ne.wait_recv()
        to_nw.wait_recv()

    @pl.when(inner)
    def _():
        to_se.wait_recv()
        to_sw.wait_recv()

    @pl.when(top)
    def _():
        @pl.when(fold_up != z)
        def _():
            to_fold_up.wait_recv()

        @pl.when(fold_up == z)
        def _():
            keep_fold_up.wait()

        @pl.when(fold_down != z)
        def _():
            to_fold_down.wait_recv()

        @pl.when(fold_down == z)
        def _():
            keep_fold_down.wait()

    for c in to_east + to_west:
        c.wait_recv()

    def edge_keep(g, rows, x, offset=0):
        if g < 4:
            edge[0, g, rows, :] = x
        elif g == 4:
            mask_edge[2, rows, :] = x
        else:
            metric_edge[g - 5, rows, :] = x

    def south_plane(g, k):
        if g < 4:
            return main[0, 3 * g + k, halo, :]
        if g == 4:
            return mask_main[6 + k, halo, :]
        return metric_main[g - 5, :, :]

    for g in range(8):
        x = pack_own(south_plane, g, 8)
        x = merge_halo(x, from_corner[0], from_corner[1], g, 8)
        if g in (5, 6):
            x = jnp.where(bottom, 1.0, x)
        edge_keep(g, halo, x)

    def unpack(first, here, there):
        wide = from_west[here, :]
        slim = from_east[here, :]
        for g in range(8):
            if g < 4:
                x = edge[0, g, there, :]
            elif g == 4:
                x = mask_edge[2, there, :]
            else:
                x = metric_edge[g - 5, there, :]
            edge_keep(g, there, merge_halo(x, wide, slim, g, UNPACK))

    sweep(unpack, UNPACK)

    def edge_masks(start, rows):
        there = pl.ds(start, rows)
        mc = mask_edge[2, there, :]
        mask_edge[0, there, :] = mc * turned(mc, N - 1)
        mask_edge[1, there, :] = mc * mask_edge[2, pl.ds(start + 1, rows), :]

    def edge_ready(start, rows):
        there = pl.ds(start, rows)
        for c, x in enumerate(
            coefficients(metric_edge[0, there, :], metric_edge[1, there, :], metric_edge[2, there, :])
        ):
            coef_edge[c, there, :] = x

    edge_masks(OFF - 8, 8)
    edge_ready(OFF - 8, 8)

    def ready(first, here, there):
        edge_masks(OFF + first, READY)
        edge_ready(OFF + first, READY)

    sweep(ready, READY)

    edge_metric = []
    for g in range(8):
        x = merge_halo(pack_own(top_plane, g, 8), from_corner[2], from_corner[3], g, 8)
        if g < 4:
            top_edge[g, strip, :] = x
        elif g == 4:
            mask_top_edge[2, strip, :] = x
        else:
            edge_metric.append(x)
    for c, x in enumerate(coefficients(*edge_metric)):
        coef_top_edge[c, :, :] = x
    mc = mask_edge[2, pl.ds(OFF + N - 8, 8), :]
    over = jnp.where(top, 1.0, pltpu.roll(mask_top_edge[2, strip, :], 7, 0))
    mask_edge[1, pl.ds(OFF + N - 8, 8), :] = mc * jnp.where(row == 7, over, pltpu.roll(mc, 7, 0))

    top_masks(mask_top_edge, 1)

    def edge_sides(n, carry):
        step_rows(n, -8, 8, edge, flux_edge, mask_edge, coef_edge, 1)
        step_rows(n, 0, N - 8, edge, flux_edge, mask_edge, coef_edge, 1)
        return north_side(
            n, carry, 1, edge, flux_edge, mask_edge, mask_top_edge, coef_edge, coef_top_edge
        )

    lax.fori_loop(0, STEPS, edge_sides, tiles(1, edge, top_edge))

    inside = pl.ds(OFF, N)
    for i in range(4 * LEVELS):
        main_out[i, :, :] = main[STEPS, i, inside, :]
    for i in range(4):
        edge_out[i, :, :] = edge[STEPS, i, inside, :]

    for c in to_east + to_west:
        c.wait_send()

    @pl.when(inner)
    def _():
        for c in (to_north, to_ne, to_nw):
            c.wait_send()

    @pl.when(raised)
    def _():
        for c in (to_south, to_se, to_sw):
            c.wait_send()

    @pl.when(top)
    def _():
        to_fold.wait_send()

        @pl.when(fold_up != z)
        def _():
            to_fold_up.wait_send()

        @pl.when(fold_down != z)
        def _():
            to_fold_down.wait_send()


def deliver(main_ref, edge_ref, u_out, v_out, t_out, s_out, held, sem):
    lane = lanes((N, N))
    copies = []
    for g, out in enumerate((u_out, v_out, t_out, s_out)):
        x = edge_ref[g]
        for k in range(LEVELS):
            y = main_ref[3 * g + k]
            y = jnp.where(lane < WIDE, turned(x, -(GROUP * k + WEST_OWN)), y)
            sides = turned(x, N - SLIM - (GROUP * k + EAST_HALO - SLIM))
            held[3 * g + k, :, :] = jnp.where(lane >= N - SLIM, sides, y)
        c = pltpu.make_async_copy(held.at[pl.ds(3 * g, LEVELS)], out, sem.at[g])
        c.start()
        copies.append(c)
    for c in copies:
        c.wait()


def per_device(u, v, t, s, hx, hy, f, cell, zonal, merid, hinge):
    def buf(*shape):
        return pltpu.VMEM(shape + (N,), jnp.float32)

    vmem = pl.BlockSpec(memory_space=pltpu.VMEM)
    shape = jax.ShapeDtypeStruct((LEVELS, N, N), jnp.float32)
    results = pl.pallas_call(
        kernel,
        out_shape=(
            pltpu.VMEM((4 * LEVELS, N, N), jnp.float32),
            pltpu.VMEM((4, N, N), jnp.float32),
        ),
        in_specs=[pl.BlockSpec(memory_space=pltpu.HBM)] * 11,
        out_specs=(vmem,) * 2,
        scratch_shapes=[buf(LEVELS, N)] * 4
        + [buf(N)] * 3
        + [pltpu.VMEM((LEVELS, N, N), jnp.int32)] * 3
        + [pltpu.SMEM((4,), jnp.int32)]
        + [
            buf(5, 12, ROWS),
            buf(5, 4, ROWS),
            buf(12, 8),
            buf(4, 8),
            buf(4, 6, ROWS),
            buf(4, 2, ROWS),
            buf(9, ROWS),
            buf(3, ROWS),
            buf(9, 8),
            buf(3, 8),
            buf(3, 8),
            buf(3, 8),
            buf(3, ROWS),
            buf(11, ROWS),
            buf(11, ROWS),
            buf(11, 8),
            buf(11, 8),
            buf(N),
            buf(N),
            buf(96),
            buf(72),
            buf(18, 8),
            buf(8),
            buf(8),
            buf(N),
            buf(N),
            buf(96),
            buf(72),
            buf(96),
            buf(4, 8),
            pltpu.SemaphoreType.DMA((11 + 2 * PARTS,)),
            pltpu.SemaphoreType.DMA((11 + 2 * PARTS,)),
            pltpu.SemaphoreType.DMA((2,)),
            pltpu.SemaphoreType.DMA((11,)),
        ],
        compiler_params=pltpu.CompilerParams(
            collective_id=0, has_side_effects=True, vmem_limit_bytes=60 * 1024 * 1024
        ),
        name="halo_steps",
    )(u, v, t, s, hx, hy, f, cell, zonal, merid, hinge)


    return pl.pallas_call(
        deliver,
        out_shape=(shape,) * 4,
        in_specs=[vmem] * 2,
        out_specs=(pl.BlockSpec(memory_space=pl.ANY),) * 4,
        scratch_shapes=[buf(4 * LEVELS, N), pltpu.SemaphoreType.DMA((4,))],
        name="deliver",
    )(*(pltpu.with_memory_space_constraint(r, pltpu.VMEM) for r in results))


def solution(mesh):
    field, plain = P(None, "merid", "zonal"), P("merid", "zonal")
    return jax.shard_map(
        per_device,
        mesh=mesh,
        in_specs=(field,) * 4 + (plain,) * 3 + (field,) * 3 + (P(),),
        out_specs=(field,) * 4,
        check_vma=False,
    )
```

```python
import jax
import jax.numpy as jnp
from jax import lax
from jax.experimental import pallas as pl
from jax.experimental.pallas import tpu as pltpu
from jax.sharding import PartitionSpec as P

STEPS = 4
LEVELS = 3
TIME_STEP = 0.25
VISCOSITY = 0.25
DIFFUSIVITY = 0.25

MESH = pl.DeviceIdType.MESH

N = 128
OFF = 16
ROWS = 160
CHUNK = 128
FILL = PACK = PREPARE = UNPACK = READY = 128
PARTS = 1
PIECE = N // PARTS
WIDE = 5
SLIM = 4
GROUP = 42
WEST_OWN = WIDE
EAST_FIRST = WIDE + 9
EAST_HALO = EAST_FIRST + 9
CA, CB, CC, CF, CGX, CGY, CHX, CHY, CDX, CDY, CK = range(11)
SIGN = (-1.0, -1.0, 1.0, 1.0)


def sweep(body, size):
    def step(i, carry):
        first = pl.multiple_of(i * size, 8)
        body(first, pl.ds(first, size), pl.ds(pl.multiple_of(OFF + first, 8), size))
        return carry

    lax.fori_loop(0, N // size, step, 0)


def turned(x, shift):
    if isinstance(shift, int):
        shift %= N
        if shift == 0:
            return x
    return pltpu.roll(x, shift, 1)


def lanes(shape):
    return lax.broadcasted_iota(jnp.int32, shape, 1)


def coefficients(hx, hy, f):
    rx = 1.0 / hx
    ry = 1.0 / hy
    a = (TIME_STEP * VISCOSITY) * rx * rx
    b = (TIME_STEP * VISCOSITY) * ry * ry
    return (
        a,
        b,
        1.0 - 2.0 * (a + b),
        (0.5 * TIME_STEP) * f,
        TIME_STEP * rx,
        TIME_STEP * ry,
        0.5 * hx,
        0.5 * hy,
        DIFFUSIVITY * hy * rx,
        DIFFUSIVITY * hx * ry,
        TIME_STEP * rx * ry,
    )


def weights(t, s, lane):
    half = [0.25 * a - 0.2 * b for a, b in zip(t, s)]
    if len(half) == 1:
        one = jnp.where(lane >= GROUP, turned(half[0], GROUP), 0.0)
        two = jnp.where(lane >= 2 * GROUP, turned(half[0], 2 * GROUP), 0.0)
        return [half[0] + 2.0 * (one + two)]
    out = [half[0]]
    for k in range(1, LEVELS):
        out.append(out[-1] + (half[k - 1] + half[k]))
    return out


def advance(load, coef, masks, keep, east, west, rows, levels):
    lane = lanes((rows, N))
    span = range(levels)
    t = [load(2, k, 0) for k in span]
    s = [load(3, k, 0) for k in span]
    tn = [load(2, k, 1) for k in span]
    sn = [load(3, k, 1) for k in span]
    p = weights(t, s, lane)
    pn = weights(tn, sn, lane)
    te = [turned(x, east) for x in t]
    se = [turned(x, east) for x in s]
    if levels == 1:
        dp = [turned(p[0], east) - p[0]]
    else:
        dp = weights([a - b for a, b in zip(te, t)], [a - b for a, b in zip(se, s)], lane)
    for k in span:
        u, v = load(0, k, 0), load(1, k, 0)
        us, vs = load(0, k, -1), load(1, k, -1)
        uw = turned(u, west)
        mu, mv, mc = masks(k)
        un = mu * (
            coef(CC) * u
            + coef(CA) * (turned(u, east) + uw)
            + coef(CB) * (load(0, k, 1) + us)
            + coef(CF) * (v + vs)
            - coef(CGX) * dp[k]
        )
        vn = mv * (
            coef(CC) * v
            + coef(CA) * (turned(v, east) + turned(v, west))
            + coef(CB) * (load(1, k, 1) + vs)
            - coef(CF) * (u + uw)
            - coef(CGY) * (pn[k] - p[k])
        )
        keep(0, k, un)
        keep(1, k, vn)
        q, d = coef(CHY) * un, coef(CDX) * mu
        qp, qm = q + d, q - d
        r, e = coef(CHX) * vn, coef(CDY) * mv
        rp, rm = r + e, r - e
        scale = mc * coef(CK)
        for which, c, ce, cn in ((2, t[k], te[k], tn[k]), (3, s[k], se[k], sn[k])):
            fe = qp * c + qm * ce
            fn = rp * c + rm * cn
            below = keep(which + 2, k, fn)
            keep(which, k, c - scale * ((fe - turned(fe, west)) + (fn - below)))


def pack_wide(plane, rows):
    lane = lanes((rows, N))
    out = None
    for k in range(LEVELS):
        for g in range(8):
            first = GROUP * k + WIDE * g
            part = turned(plane(g, k), first - (N - WIDE))
            out = part if out is None else jnp.where(lane >= first, part, out)
    return out


def pack_slim(plane, rows):
    lane = lanes((rows, N))
    out = None
    for k in range(LEVELS):
        for g in range(8):
            first = GROUP * k + SLIM * g
            part = turned(plane(g, k), first)
            out = part if out is None else jnp.where(lane >= first, part, out)
    return out


def pack_own(plane, g, rows):
    lane = lanes((rows, N))
    out = None
    for k in range(LEVELS):
        x = plane(g, k)
        for first, column in ((GROUP * k + WEST_OWN, 0), (GROUP * k + EAST_FIRST, N - 9)):
            part = turned(x, first - column)
            out = part if out is None else jnp.where(lane >= first, part, out)
    return out


def merge_halo(own, wide, slim, g, rows):
    lane = lanes((rows, N))
    place = lane - jnp.where(lane >= 2 * GROUP, 2 * GROUP, jnp.where(lane >= GROUP, GROUP, 0))
    own = jnp.where(place < WIDE, turned(wide, -WIDE * g), own)
    east = (place >= EAST_HALO) & (place < EAST_HALO + SLIM)
    return jnp.where(east, turned(slim, EAST_HALO - SLIM * g), own)


def flipped(x):
    return jnp.take_along_axis(x, N - 1 - lanes(x.shape), axis=1)


def kernel(
    u_hbm,
    v_hbm,
    t_hbm,
    s_hbm,
    hx_hbm,
    hy_hbm,
    f_hbm,
    cell_hbm,
    zonal_hbm,
    merid_hbm,
    hinge_hbm,
    main_out,
    edge_out,
    u_ref,
    v_ref,
    t_ref,
    s_ref,
    hx_ref,
    hy_ref,
    f_ref,
    cell_ref,
    zonal_ref,
    merid_ref,
    hinge,
    main,
    edge,
    top_main,
    top_edge,
    flux_main,
    flux_edge,
    mask_main,
    mask_edge,
    mask_top_main,
    mask_top_edge,
    metric_main,
    metric_top,
    metric_edge,
    coef_main,
    coef_edge,
    coef_top_main,
    coef_top_edge,
    east_buf,
    west_buf,
    north_buf,
    south_buf,
    fold_tile,
    fold_west,
    fold_east,
    from_west,
    from_east,
    from_south,
    from_north,
    from_fold,
    from_corner,
    send_sem,
    recv_sem,
    local_sem,
    load_sem,
):
    sources = (u_hbm, v_hbm, t_hbm, s_hbm, cell_hbm, zonal_hbm, merid_hbm, hx_hbm, hy_hbm, f_hbm, hinge_hbm)
    targets = (u_ref, v_ref, t_ref, s_ref, cell_ref, zonal_ref, merid_ref, hx_ref, hy_ref, f_ref, hinge)
    loads = [
        pltpu.make_async_copy(src, dst, load_sem.at[i])
        for i, (src, dst) in enumerate(zip(sources, targets))
    ]
    for c in loads:
        c.start()

    nz, nm = lax.axis_size("zonal"), lax.axis_size("merid")
    z, m = lax.axis_index("zonal"), lax.axis_index("merid")
    east_z, west_z = lax.rem(z + 1, nz), lax.rem(z + nz - 1, nz)
    fold_z = nz - 1 - z
    fold_up, fold_down = lax.rem(fold_z + 1, nz), lax.rem(fold_z + nz - 1, nz)
    top, bottom = m == nm - 1, m == 0
    inner = jnp.logical_not(top)
    raised = jnp.logical_not(bottom)

    def at(zz, mm):
        return {"zonal": zz, "merid": mm}

    barrier = pltpu.get_barrier_semaphore()

    def hail(zz, mm):
        pl.semaphore_signal(barrier, inc=1, device_id=at(zz, mm), device_id_type=MESH)

    hail(east_z, m)
    hail(west_z, m)

    @pl.when(raised)
    def _():
        for zz in (west_z, z, east_z):
            hail(zz, m - 1)

    @pl.when(inner)
    def _():
        for zz in (west_z, z, east_z):
            hail(zz, m + 1)

    @pl.when(top)
    def _():
        hail(fold_z, m)

        @pl.when(fold_up != z)
        def _():
            hail(fold_up, m)

        @pl.when(fold_down != z)
        def _():
            hail(fold_down, m)

    for c in loads:
        c.wait()
    fields = (u_ref, v_ref, t_ref, s_ref)

    def fill(first, here, there):
        for k in range(LEVELS):
            mu = zonal_ref[k, here, :].astype(jnp.float32)
            mv = merid_ref[k, here, :].astype(jnp.float32)
            mc = cell_ref[k, here, :].astype(jnp.float32)
            mask_main[k, there, :] = mu
            mask_main[3 + k, there, :] = mv
            mask_main[6 + k, there, :] = mc
            for g, ref in enumerate(fields):
                main[0, 3 * g + k, there, :] = ref[k, here, :] * (mu, mv, mc, mc)[g]

    sweep(fill, FILL)

    def plane_at(start, rows):
        def plane(g, k):
            if g < 4:
                return main[0, 3 * g + k, pl.ds(OFF + start, rows), :]
            if g == 4:
                return mask_main[6 + k, pl.ds(OFF + start, rows), :]
            return (hx_ref, hy_ref, f_ref)[g - 5][pl.ds(start, rows), :]

        return plane

    def number(g, k):
        return 3 * g + k if g < 5 else 15 + g - 5

    every = [(g, k) for g in range(5) for k in range(LEVELS)] + [(g, 0) for g in (5, 6, 7)]

    @pl.when(inner)
    def _():
        for g, k in every:
            i = number(g, k)
            north_buf[pl.ds(WIDE * i, WIDE), :] = plane_at(N - WIDE, WIDE)(g, k)

    @pl.when(top)
    def _():
        plane = plane_at(N - 8, 8)
        for g, k in every:
            i = number(g, k)
            tile = flipped(plane(g, k))
            fold_tile[i, :, :] = tile
            north_buf[pl.ds(WIDE * i, WIDE), :] = tile[8 - WIDE :, :]
            if g == 1:
                north_buf[pl.ds(90 + k, 1), :] = tile[2:3, :]

        def mirrored(g, k):
            return fold_tile[number(g, k)]

        fold_west[...] = pack_wide(mirrored, 8)
        fold_east[...] = pack_slim(mirrored, 8)

    def copy(src, dst, slot, zz, mm):
        return pltpu.make_async_remote_copy(
            src_ref=src,
            dst_ref=dst,
            send_sem=send_sem.at[slot],
            recv_sem=recv_sem.at[slot],
            device_id=at(zz, mm),
            device_id_type=MESH,
        )

    corner = lambda i: from_corner.at[i]
    low, high = pl.ds(0, 8), pl.ds(N - 8, 8)
    to_east, to_west = [], []
    for i in range(PARTS):
        piece = pl.ds(i * PIECE, PIECE)
        to_east.append(copy(east_buf.at[piece], from_west.at[piece], 11 + 2 * i, east_z, m))
        to_west.append(copy(west_buf.at[piece], from_east.at[piece], 12 + 2 * i, west_z, m))
    to_north = copy(north_buf, from_south, 2, z, m + 1)
    to_south = copy(south_buf, from_north, 3, z, m - 1)
    to_fold = copy(north_buf, from_fold, 4, fold_z, m)
    to_ne = copy(east_buf.at[high], corner(0), 5, east_z, m + 1)
    to_nw = copy(west_buf.at[high], corner(1), 6, west_z, m + 1)
    to_se = copy(east_buf.at[low], corner(2), 7, east_z, m - 1)
    to_sw = copy(west_buf.at[low], corner(3), 8, west_z, m - 1)
    to_fold_up = copy(fold_west, corner(2), 9, fold_up, m)
    to_fold_down = copy(fold_east, corner(3), 10, fold_down, m)
    keep_fold_up = pltpu.make_async_copy(fold_west, corner(2), local_sem.at[0])
    keep_fold_down = pltpu.make_async_copy(fold_east, corner(3), local_sem.at[1])

    same = jnp.where(fold_up == z, 1, 0) + jnp.where(fold_down == z, 1, 0)
    pl.semaphore_wait(barrier, 2 + jnp.where(bottom, 0, 3) + 3 - jnp.where(top, same, 0))

    @pl.when(top)
    def _():
        to_fold.start()

        @pl.when(fold_up != z)
        def _():
            to_fold_up.start()

        @pl.when(fold_up == z)
        def _():
            keep_fold_up.start()

        @pl.when(fold_down != z)
        def _():
            to_fold_down.start()

        @pl.when(fold_down == z)
        def _():
            keep_fold_down.start()

    @pl.when(inner)
    def _():
        to_north.start()

    for g, k in every:
        south_buf[pl.ds(SLIM * number(g, k), SLIM), :] = plane_at(0, SLIM)(g, k)

    @pl.when(raised)
    def _():
        to_south.start()

    for i in range(PARTS):
        plane = plane_at(i * PIECE, PIECE)
        east_buf[pl.ds(i * PIECE, PIECE), :] = pack_wide(plane, PIECE)
        to_east[i].start()
        west_buf[pl.ds(i * PIECE, PIECE), :] = pack_slim(plane, PIECE)
        to_west[i].start()

    @pl.when(inner)
    def _():
        to_ne.start()
        to_nw.start()

    @pl.when(raised)
    def _():
        to_se.start()
        to_sw.start()

    def prepare(first, here, there):
        for c, x in enumerate(coefficients(hx_ref[here, :], hy_ref[here, :], f_ref[here, :])):
            coef_main[c, there, :] = x
        plane = plane_at(first, PREPARE)
        for g in range(8):
            x = pack_own(plane, g, PREPARE)
            if g < 4:
                edge[0, g, there, :] = x
            elif g == 4:
                mask_edge[2, there, :] = x
            else:
                metric_edge[g - 5, there, :] = x

    sweep(prepare, PREPARE)

    def step_rows(n, start, rows, state, flux, mask, coef, levels, align=True):
        def at_row(dj):
            first = OFF + start + dj
            if dj == 0 and align:
                first = pl.multiple_of(first, 8)
            return pl.ds(first, rows)

        def load(g, k, dj):
            return state[n, levels * g + k, at_row(dj), :]

        def keep(g, k, x):
            if g < 4:
                state[n + 1, levels * g + k, at_row(0), :] = x
                return None
            flux[n, levels * (g - 4) + k, at_row(0), :] = x
            return flux[n, levels * (g - 4) + k, at_row(-1), :]

        def masks(k):
            return [mask[levels * i + k, at_row(0), :] for i in range(3)]

        advance(load, lambda c: coef[c, at_row(0), :], masks, keep, N - 1, 1, rows, levels)

    def interior(n, carry):
        def chunk(i, inside):
            step_rows(n, i * CHUNK, CHUNK, main, flux_main, mask_main, coef_main, LEVELS)
            return inside

        return lax.fori_loop(0, N // CHUNK, chunk, carry)

    lax.fori_loop(0, STEPS, interior, 0)

    halo = pl.ds(OFF - 8, 8)

    @pl.when(raised)
    def _():
        to_north.wait_recv()
        to_ne.wait_recv()
        to_nw.wait_recv()
        last = pl.ds(OFF - WIDE, WIDE)
        for g, k in every:
            x = from_south[pl.ds(WIDE * number(g, k), WIDE), :]
            if g < 4:
                main[0, 3 * g + k, last, :] = x
            elif g == 4:
                mask_main[6 + k, last, :] = x
            else:
                metric_main[g - 5, pl.ds(8 - WIDE, WIDE), :] = x

    @pl.when(bottom)
    def _():
        zero = jnp.zeros((8, N), jnp.float32)
        for g, k in every:
            if g < 4:
                main[0, 3 * g + k, halo, :] = zero
            elif g == 4:
                mask_main[6 + k, halo, :] = zero
            else:
                metric_main[g - 5, :, :] = zero + 1.0
        for i in (0, 1):
            from_corner[i, :, :] = zero

    for k in range(LEVELS):
        mc = mask_main[6 + k, halo, :]
        mask_main[k, halo, :] = mc * turned(mc, N - 1)
        mask_main[3 + k, halo, :] = mc * mask_main[6 + k, pl.ds(OFF - 7, 8), :]
    for c, x in enumerate(coefficients(metric_main[0], metric_main[1], metric_main[2])):
        coef_main[c, halo, :] = x

    for c in to_east + to_west:
        c.wait_recv()

    def edge_keep(g, rows, x, offset=0):
        if g < 4:
            edge[0, g, rows, :] = x
        elif g == 4:
            mask_edge[2, rows, :] = x
        else:
            metric_edge[g - 5, rows, :] = x

    def south_plane(g, k):
        if g < 4:
            return main[0, 3 * g + k, halo, :]
        if g == 4:
            return mask_main[6 + k, halo, :]
        return metric_main[g - 5, :, :]

    for g in range(8):
        x = pack_own(south_plane, g, 8)
        x = merge_halo(x, from_corner[0], from_corner[1], g, 8)
        if g in (5, 6):
            x = jnp.where(bottom, 1.0, x)
        edge_keep(g, halo, x)

    def unpack(first, here, there):
        wide = from_west[here, :]
        slim = from_east[here, :]
        for g in range(8):
            if g < 4:
                x = edge[0, g, there, :]
            elif g == 4:
                x = mask_edge[2, there, :]
            else:
                x = metric_edge[g - 5, there, :]
            edge_keep(g, there, merge_halo(x, wide, slim, g, UNPACK))

    sweep(unpack, UNPACK)

    def edge_masks(start, rows):
        there = pl.ds(start, rows)
        mc = mask_edge[2, there, :]
        mask_edge[0, there, :] = mc * turned(mc, N - 1)
        mask_edge[1, there, :] = mc * mask_edge[2, pl.ds(start + 1, rows), :]

    def edge_ready(start, rows):
        there = pl.ds(start, rows)
        for c, x in enumerate(
            coefficients(metric_edge[0, there, :], metric_edge[1, there, :], metric_edge[2, there, :])
        ):
            coef_edge[c, there, :] = x

    edge_masks(OFF - 8, 8)
    edge_ready(OFF - 8, 8)

    def ready(first, here, there):
        edge_masks(OFF + first, READY)
        edge_ready(OFF + first, READY)

    sweep(ready, READY)

    strip = pl.ds(0, 8)
    for g, k in every:
        if g < 4:
            top_main[3 * g + k, strip, :] = jnp.zeros((8, N), jnp.float32)
        elif g == 4:
            mask_top_main[6 + k, strip, :] = jnp.zeros((8, N), jnp.float32)
        else:
            metric_top[g - 5, :, :] = jnp.ones((8, N), jnp.float32)

    def top_keep(g, k, first, x):
        rows = pl.ds(first, x.shape[0])
        if g < 4:
            top_main[3 * g + k, rows, :] = x
        elif g == 4:
            mask_top_main[6 + k, rows, :] = x
        else:
            metric_top[g - 5, pl.ds(first, x.shape[0]), :] = x

    @pl.when(inner)
    def _():
        to_south.wait_recv()
        to_se.wait_recv()
        to_sw.wait_recv()
        for g, k in every:
            top_keep(g, k, 0, from_north[pl.ds(SLIM * number(g, k), SLIM), :])

    @pl.when(top)
    def _():
        to_fold.wait_recv()

        @pl.when(fold_up != z)
        def _():
            to_fold_up.wait_recv()

        @pl.when(fold_up == z)
        def _():
            keep_fold_up.wait()

        @pl.when(fold_down != z)
        def _():
            to_fold_down.wait_recv()

        @pl.when(fold_down == z)
        def _():
            keep_fold_down.wait()

        for g, k in every:
            top_keep(g, k, 8 - WIDE, from_fold[pl.ds(WIDE * number(g, k), WIDE), :])
        for k in range(LEVELS):
            top_keep(1, k, 2, from_fold[pl.ds(90 + k, 1), :])

    east = jnp.where(top, 1, N - 1)
    west = jnp.where(top, N - 1, 1)

    def top_plane(g, k):
        if g < 4:
            return top_main[3 * g + k, strip, :]
        if g == 4:
            return mask_top_main[6 + k, strip, :]
        return metric_top[g - 5, :, :]

    edge_metric = []
    for g in range(8):
        x = merge_halo(pack_own(top_plane, g, 8), from_corner[2], from_corner[3], g, 8)
        if g < 4:
            top_edge[g, strip, :] = x
        elif g == 4:
            mask_top_edge[2, strip, :] = x
        else:
            edge_metric.append(x)
    for c, x in enumerate(coefficients(*edge_metric)):
        coef_top_edge[c, :, :] = x
    for c, x in enumerate(coefficients(metric_top[0], metric_top[1], metric_top[2])):
        coef_top_main[c, :, :] = x
    row = lax.broadcasted_iota(jnp.int32, (8, N), 0)
    mc = mask_edge[2, pl.ds(OFF + N - 8, 8), :]
    over = jnp.where(top, 1.0, pltpu.roll(mask_top_edge[2, strip, :], 7, 0))
    mask_edge[1, pl.ds(OFF + N - 8, 8), :] = mc * jnp.where(row == 7, over, pltpu.roll(mc, 7, 0))
    for mask, levels in ((mask_top_main, LEVELS), (mask_top_edge, 1)):
        for k in range(levels):
            mc = mask[2 * levels + k, strip, :]
            mask[k, strip, :] = mc * turned(mc, east)
            mask[levels + k, strip, :] = mc * jnp.where(row == 7, 1.0, pltpu.roll(mc, 7, 0))

    plain = [jnp.full((1, N), hinge[g], jnp.int32) == 0 for g in range(4)]

    first_row, last_row = row == 0, row == 7
    brim, under = pl.ds(OFF + N - 8, 8), pl.ds(OFF + N - 16, 8)

    def up(x):
        return pltpu.roll(x, 7, 0)

    def down(x):
        return pltpu.roll(x, 1, 0)

    kinds = (
        (LEVELS, main, flux_main, mask_main, mask_top_main, coef_main, coef_top_main),
        (1, edge, flux_edge, mask_edge, mask_top_edge, coef_edge, coef_top_edge),
    )

    def outer(n, carry):
        step_rows(n, n - WIDE, 8, main, flux_main, mask_main, coef_main, LEVELS, False)
        step_rows(n, -8, 8, edge, flux_edge, mask_edge, coef_edge, 1)
        step_rows(n, 0, N - 8, edge, flux_edge, mask_edge, coef_edge, 1)
        after = []
        for (levels, state, flux, mask, mask_beyond, coef, coef_beyond), (below, beyond) in zip(
            kinds, carry
        ):
            new_below, new_beyond, fluxes = [None] * len(below), [None] * len(beyond), {}

            def load_below(g, k, dj):
                c, z = below[levels * g + k], beyond[levels * g + k]
                if dj == 0:
                    return c
                if dj < 0:
                    return jnp.where(first_row, down(state[n, levels * g + k, under, :]), down(c))
                ghost = SIGN[g] * jnp.where(plain[g], z, down(turned(z, 1)))
                return jnp.where(last_row, jnp.where(top, ghost, up(z)), up(c))

            def load_beyond(g, k, dj):
                c, z = below[levels * g + k], beyond[levels * g + k]
                if dj == 0:
                    return z
                if dj < 0:
                    return jnp.where(first_row, down(c), down(z))
                ghost = SIGN[g] * jnp.where(plain[g], c, down(turned(c, N - 1)))
                return jnp.where(last_row, ghost, up(z))

            def keep_below(g, k, x):
                if g < 4:
                    new_below[levels * g + k] = x
                    return None
                fluxes[g, k] = down(x)
                return jnp.where(
                    first_row, down(flux[n, levels * (g - 4) + k, under, :]), fluxes[g, k]
                )

            def keep_beyond(g, k, x):
                if g < 4:
                    new_beyond[levels * g + k] = x
                    return None
                return jnp.where(first_row, fluxes[g, k], down(x))

            def masks(k):
                return [mask[levels * i + k, brim, :] for i in range(3)]

            def masks_beyond(k):
                return [mask_beyond[levels * i + k, strip, :] for i in range(3)]

            advance(load_below, lambda c: coef[c, brim, :], masks, keep_below, N - 1, 1, 8, levels)
            advance(
                load_beyond, lambda c: coef_beyond[c], masks_beyond, keep_beyond, east, west, 8, levels
            )
            if levels == 1:
                for i, x in enumerate(new_below):
                    state[n + 1, i, brim, :] = x
            after.append((tuple(new_below), tuple(new_beyond)))
        return tuple(after)

    start = tuple(
        (
            tuple(state[0, i, brim, :] for i in range(4 * levels)),
            tuple(beyond[i, strip, :] for i in range(4 * levels)),
        )
        for levels, state, beyond in ((LEVELS, main, top_main), (1, edge, top_edge))
    )
    done = lax.fori_loop(0, STEPS, outer, start)
    for i, x in enumerate(done[0][0]):
        main[STEPS, i, brim, :] = x

    inside = pl.ds(OFF, N)
    for i in range(4 * LEVELS):
        main_out[i, :, :] = main[STEPS, i, inside, :]
    for i in range(4):
        edge_out[i, :, :] = edge[STEPS, i, inside, :]

    for c in to_east + to_west:
        c.wait_send()

    @pl.when(inner)
    def _():
        for c in (to_north, to_ne, to_nw):
            c.wait_send()

    @pl.when(raised)
    def _():
        for c in (to_south, to_se, to_sw):
            c.wait_send()

    @pl.when(top)
    def _():
        to_fold.wait_send()

        @pl.when(fold_up != z)
        def _():
            to_fold_up.wait_send()

        @pl.when(fold_down != z)
        def _():
            to_fold_down.wait_send()


def deliver(main_ref, edge_ref, u_out, v_out, t_out, s_out, held, sem):
    lane = lanes((N, N))
    copies = []
    for g, out in enumerate((u_out, v_out, t_out, s_out)):
        x = edge_ref[g]
        for k in range(LEVELS):
            y = main_ref[3 * g + k]
            y = jnp.where(lane < WIDE, turned(x, -(GROUP * k + WEST_OWN)), y)
            sides = turned(x, N - SLIM - (GROUP * k + EAST_HALO - SLIM))
            held[3 * g + k, :, :] = jnp.where(lane >= N - SLIM, sides, y)
        c = pltpu.make_async_copy(held.at[pl.ds(3 * g, LEVELS)], out, sem.at[g])
        c.start()
        copies.append(c)
    for c in copies:
        c.wait()


def per_device(u, v, t, s, hx, hy, f, cell, zonal, merid, hinge):
    def buf(*shape):
        return pltpu.VMEM(shape + (N,), jnp.float32)

    vmem = pl.BlockSpec(memory_space=pltpu.VMEM)
    shape = jax.ShapeDtypeStruct((LEVELS, N, N), jnp.float32)
    results = pl.pallas_call(
        kernel,
        out_shape=(
            pltpu.VMEM((4 * LEVELS, N, N), jnp.float32),
            pltpu.VMEM((4, N, N), jnp.float32),
        ),
        in_specs=[pl.BlockSpec(memory_space=pltpu.HBM)] * 11,
        out_specs=(vmem,) * 2,
        scratch_shapes=[buf(LEVELS, N)] * 4
        + [buf(N)] * 3
        + [pltpu.VMEM((LEVELS, N, N), jnp.int32)] * 3
        + [pltpu.SMEM((4,), jnp.int32)]
        + [
            buf(5, 12, ROWS),
            buf(5, 4, ROWS),
            buf(12, 8),
            buf(4, 8),
            buf(4, 6, ROWS),
            buf(4, 2, ROWS),
            buf(9, ROWS),
            buf(3, ROWS),
            buf(9, 8),
            buf(3, 8),
            buf(3, 8),
            buf(3, 8),
            buf(3, ROWS),
            buf(11, ROWS),
            buf(11, ROWS),
            buf(11, 8),
            buf(11, 8),
            buf(N),
            buf(N),
            buf(96),
            buf(72),
            buf(18, 8),
            buf(8),
            buf(8),
            buf(N),
            buf(N),
            buf(96),
            buf(72),
            buf(96),
            buf(4, 8),
            pltpu.SemaphoreType.DMA((11 + 2 * PARTS,)),
            pltpu.SemaphoreType.DMA((11 + 2 * PARTS,)),
            pltpu.SemaphoreType.DMA((2,)),
            pltpu.SemaphoreType.DMA((11,)),
        ],
        compiler_params=pltpu.CompilerParams(
            collective_id=0, has_side_effects=True, vmem_limit_bytes=60 * 1024 * 1024
        ),
        name="halo_steps",
    )(u, v, t, s, hx, hy, f, cell, zonal, merid, hinge)


    return pl.pallas_call(
        deliver,
        out_shape=(shape,) * 4,
        in_specs=[vmem] * 2,
        out_specs=(pl.BlockSpec(memory_space=pl.ANY),) * 4,
        scratch_shapes=[buf(4 * LEVELS, N), pltpu.SemaphoreType.DMA((4,))],
        name="deliver",
    )(*(pltpu.with_memory_space_constraint(r, pltpu.VMEM) for r in results))


def solution(mesh):
    field, plain = P(None, "merid", "zonal"), P("merid", "zonal")
    return jax.shard_map(
        per_device,
        mesh=mesh,
        in_specs=(field,) * 4 + (plain,) * 3 + (field,) * 3 + (P(),),
        out_specs=(field,) * 4,
        check_vma=False,
    )
```

```python
import jax
import jax.numpy as jnp
from jax import lax
from jax.experimental import pallas as pl
from jax.experimental.pallas import tpu as pltpu
from jax.sharding import PartitionSpec as P

STEPS = 4
LEVELS = 3
TIME_STEP = 0.25
VISCOSITY = 0.25
DIFFUSIVITY = 0.25

MESH = pl.DeviceIdType.MESH

N = 128
OFF = 16
ROWS = 160
CHUNK = 128
FILL = PACK = PREPARE = UNPACK = READY = 128
PARTS = 1
PIECE = N // PARTS
WIDE = 5
SLIM = 4
GROUP = 42
WEST_OWN = WIDE
EAST_FIRST = WIDE + 9
EAST_HALO = EAST_FIRST + 9
CA, CB, CC, CF, CGX, CGY, CHX, CHY, CDX, CDY, CK = range(11)
SIGN = (-1.0, -1.0, 1.0, 1.0)


def sweep(body, size):
    def step(i, carry):
        first = pl.multiple_of(i * size, 8)
        body(first, pl.ds(first, size), pl.ds(pl.multiple_of(OFF + first, 8), size))
        return carry

    lax.fori_loop(0, N // size, step, 0)


def turned(x, shift):
    if isinstance(shift, int):
        shift %= N
        if shift == 0:
            return x
    return pltpu.roll(x, shift, 1)


def lanes(shape):
    return lax.broadcasted_iota(jnp.int32, shape, 1)


def coefficients(hx, hy, f):
    rx = 1.0 / hx
    ry = 1.0 / hy
    a = (TIME_STEP * VISCOSITY) * rx * rx
    b = (TIME_STEP * VISCOSITY) * ry * ry
    return (
        a,
        b,
        1.0 - 2.0 * (a + b),
        (0.5 * TIME_STEP) * f,
        TIME_STEP * rx,
        TIME_STEP * ry,
        0.5 * hx,
        0.5 * hy,
        DIFFUSIVITY * hy * rx,
        DIFFUSIVITY * hx * ry,
        TIME_STEP * rx * ry,
    )


def weights(t, s, lane):
    half = [0.25 * a - 0.2 * b for a, b in zip(t, s)]
    if len(half) == 1:
        one = jnp.where(lane >= GROUP, turned(half[0], GROUP), 0.0)
        two = jnp.where(lane >= 2 * GROUP, turned(half[0], 2 * GROUP), 0.0)
        return [half[0] + 2.0 * (one + two)]
    out = [half[0]]
    for k in range(1, LEVELS):
        out.append(out[-1] + (half[k - 1] + half[k]))
    return out


def advance(load, coef, masks, keep, east, west, rows, levels):
    lane = lanes((rows, N))
    span = range(levels)
    t = [load(2, k, 0) for k in span]
    s = [load(3, k, 0) for k in span]
    tn = [load(2, k, 1) for k in span]
    sn = [load(3, k, 1) for k in span]
    p = weights(t, s, lane)
    pn = weights(tn, sn, lane)
    te = [turned(x, east) for x in t]
    se = [turned(x, east) for x in s]
    if levels == 1:
        dp = [turned(p[0], east) - p[0]]
    else:
        dp = weights([a - b for a, b in zip(te, t)], [a - b for a, b in zip(se, s)], lane)
    for k in span:
        u, v = load(0, k, 0), load(1, k, 0)
        us, vs = load(0, k, -1), load(1, k, -1)
        uw = turned(u, west)
        mu, mv, mc = masks(k)
        un = mu * (
            coef(CC) * u
            + coef(CA) * (turned(u, east) + uw)
            + coef(CB) * (load(0, k, 1) + us)
            + coef(CF) * (v + vs)
            - coef(CGX) * dp[k]
        )
        vn = mv * (
            coef(CC) * v
            + coef(CA) * (turned(v, east) + turned(v, west))
            + coef(CB) * (load(1, k, 1) + vs)
            - coef(CF) * (u + uw)
            - coef(CGY) * (pn[k] - p[k])
        )
        keep(0, k, un)
        keep(1, k, vn)
        q, d = coef(CHY) * un, coef(CDX) * mu
        qp, qm = q + d, q - d
        r, e = coef(CHX) * vn, coef(CDY) * mv
        rp, rm = r + e, r - e
        scale = mc * coef(CK)
        for which, c, ce, cn in ((2, t[k], te[k], tn[k]), (3, s[k], se[k], sn[k])):
            fe = qp * c + qm * ce
            fn = rp * c + rm * cn
            below = keep(which + 2, k, fn)
            keep(which, k, c - scale * ((fe - turned(fe, west)) + (fn - below)))


def pack_wide(plane, rows):
    lane = lanes((rows, N))
    out = None
    for k in range(LEVELS):
        for g in range(8):
            first = GROUP * k + WIDE * g
            part = turned(plane(g, k), first - (N - WIDE))
            out = part if out is None else jnp.where(lane >= first, part, out)
    return out


def pack_slim(plane, rows):
    lane = lanes((rows, N))
    out = None
    for k in range(LEVELS):
        for g in range(8):
            first = GROUP * k + SLIM * g
            part = turned(plane(g, k), first)
            out = part if out is None else jnp.where(lane >= first, part, out)
    return out


def pack_own(plane, g, rows):
    lane = lanes((rows, N))
    out = None
    for k in range(LEVELS):
        x = plane(g, k)
        for first, column in ((GROUP * k + WEST_OWN, 0), (GROUP * k + EAST_FIRST, N - 9)):
            part = turned(x, first - column)
            out = part if out is None else jnp.where(lane >= first, part, out)
    return out


def merge_halo(own, wide, slim, g, rows):
    lane = lanes((rows, N))
    place = lane - jnp.where(lane >= 2 * GROUP, 2 * GROUP, jnp.where(lane >= GROUP, GROUP, 0))
    own = jnp.where(place < WIDE, turned(wide, -WIDE * g), own)
    east = (place >= EAST_HALO) & (place < EAST_HALO + SLIM)
    return jnp.where(east, turned(slim, EAST_HALO - SLIM * g), own)


def flipped(x):
    return jnp.take_along_axis(x, N - 1 - lanes(x.shape), axis=1)


def kernel(
    u_hbm,
    v_hbm,
    t_hbm,
    s_hbm,
    hx_hbm,
    hy_hbm,
    f_hbm,
    cell_hbm,
    zonal_hbm,
    merid_hbm,
    hinge_hbm,
    main_out,
    edge_out,
    u_ref,
    v_ref,
    t_ref,
    s_ref,
    hx_ref,
    hy_ref,
    f_ref,
    cell_ref,
    zonal_ref,
    merid_ref,
    hinge,
    main,
    edge,
    top_main,
    top_edge,
    flux_main,
    flux_edge,
    mask_main,
    mask_edge,
    mask_top_main,
    mask_top_edge,
    metric_main,
    metric_top,
    metric_edge,
    coef_main,
    coef_edge,
    coef_top_main,
    coef_top_edge,
    east_buf,
    west_buf,
    north_buf,
    south_buf,
    fold_tile,
    fold_west,
    fold_east,
    from_west,
    from_east,
    from_south,
    from_north,
    from_fold,
    from_corner,
    send_sem,
    recv_sem,
    local_sem,
    load_sem,
):
    sources = (u_hbm, v_hbm, t_hbm, s_hbm, cell_hbm, zonal_hbm, merid_hbm, hx_hbm, hy_hbm, f_hbm, hinge_hbm)
    targets = (u_ref, v_ref, t_ref, s_ref, cell_ref, zonal_ref, merid_ref, hx_ref, hy_ref, f_ref, hinge)
    loads = [
        pltpu.make_async_copy(src, dst, load_sem.at[i])
        for i, (src, dst) in enumerate(zip(sources, targets))
    ]
    for c in loads:
        c.start()

    nz, nm = lax.axis_size("zonal"), lax.axis_size("merid")
    z, m = lax.axis_index("zonal"), lax.axis_index("merid")
    east_z, west_z = lax.rem(z + 1, nz), lax.rem(z + nz - 1, nz)
    fold_z = nz - 1 - z
    fold_up, fold_down = lax.rem(fold_z + 1, nz), lax.rem(fold_z + nz - 1, nz)
    top, bottom = m == nm - 1, m == 0
    inner = jnp.logical_not(top)
    raised = jnp.logical_not(bottom)

    def at(zz, mm):
        return {"zonal": zz, "merid": mm}

    barrier = pltpu.get_barrier_semaphore()

    def hail(zz, mm):
        pl.semaphore_signal(barrier, inc=1, device_id=at(zz, mm), device_id_type=MESH)

    hail(east_z, m)
    hail(west_z, m)

    @pl.when(raised)
    def _():
        for zz in (west_z, z, east_z):
            hail(zz, m - 1)

    @pl.when(inner)
    def _():
        for zz in (west_z, z, east_z):
            hail(zz, m + 1)

    @pl.when(top)
    def _():
        hail(fold_z, m)

        @pl.when(fold_up != z)
        def _():
            hail(fold_up, m)

        @pl.when(fold_down != z)
        def _():
            hail(fold_down, m)

    for c in loads:
        c.wait()
    fields = (u_ref, v_ref, t_ref, s_ref)

    def fill(first, here, there):
        for k in range(LEVELS):
            mu = zonal_ref[k, here, :].astype(jnp.float32)
            mv = merid_ref[k, here, :].astype(jnp.float32)
            mc = cell_ref[k, here, :].astype(jnp.float32)
            mask_main[k, there, :] = mu
            mask_main[3 + k, there, :] = mv
            mask_main[6 + k, there, :] = mc
            for g, ref in enumerate(fields):
                main[0, 3 * g + k, there, :] = ref[k, here, :] * (mu, mv, mc, mc)[g]

    sweep(fill, FILL)

    def plane_at(start, rows):
        def plane(g, k):
            if g < 4:
                return main[0, 3 * g + k, pl.ds(OFF + start, rows), :]
            if g == 4:
                return mask_main[6 + k, pl.ds(OFF + start, rows), :]
            return (hx_ref, hy_ref, f_ref)[g - 5][pl.ds(start, rows), :]

        return plane

    def number(g, k):
        return 3 * g + k if g < 5 else 15 + g - 5

    every = [(g, k) for g in range(5) for k in range(LEVELS)] + [(g, 0) for g in (5, 6, 7)]

    @pl.when(inner)
    def _():
        for g, k in every:
            i = number(g, k)
            north_buf[pl.ds(WIDE * i, WIDE), :] = plane_at(N - WIDE, WIDE)(g, k)

    @pl.when(top)
    def _():
        plane = plane_at(N - 8, 8)
        for g, k in every:
            i = number(g, k)
            tile = flipped(plane(g, k))
            fold_tile[i, :, :] = tile
            north_buf[pl.ds(WIDE * i, WIDE), :] = tile[8 - WIDE :, :]
            if g == 1:
                north_buf[pl.ds(90 + k, 1), :] = tile[2:3, :]

        def mirrored(g, k):
            return fold_tile[number(g, k)]

        fold_west[...] = pack_wide(mirrored, 8)
        fold_east[...] = pack_slim(mirrored, 8)

    def copy(src, dst, slot, zz, mm):
        return pltpu.make_async_remote_copy(
            src_ref=src,
            dst_ref=dst,
            send_sem=send_sem.at[slot],
            recv_sem=recv_sem.at[slot],
            device_id=at(zz, mm),
            device_id_type=MESH,
        )

    corner = lambda i: from_corner.at[i]
    low, high = pl.ds(0, 8), pl.ds(N - 8, 8)
    to_east, to_west = [], []
    for i in range(PARTS):
        piece = pl.ds(i * PIECE, PIECE)
        to_east.append(copy(east_buf.at[piece], from_west.at[piece], 11 + 2 * i, east_z, m))
        to_west.append(copy(west_buf.at[piece], from_east.at[piece], 12 + 2 * i, west_z, m))
    to_north = copy(north_buf, from_south, 2, z, m + 1)
    to_south = copy(south_buf, from_north, 3, z, m - 1)
    to_fold = copy(north_buf, from_fold, 4, fold_z, m)
    to_ne = copy(east_buf.at[high], corner(0), 5, east_z, m + 1)
    to_nw = copy(west_buf.at[high], corner(1), 6, west_z, m + 1)
    to_se = copy(east_buf.at[low], corner(2), 7, east_z, m - 1)
    to_sw = copy(west_buf.at[low], corner(3), 8, west_z, m - 1)
    to_fold_up = copy(fold_west, corner(2), 9, fold_up, m)
    to_fold_down = copy(fold_east, corner(3), 10, fold_down, m)
    keep_fold_up = pltpu.make_async_copy(fold_west, corner(2), local_sem.at[0])
    keep_fold_down = pltpu.make_async_copy(fold_east, corner(3), local_sem.at[1])

    same = jnp.where(fold_up == z, 1, 0) + jnp.where(fold_down == z, 1, 0)
    pl.semaphore_wait(barrier, 2 + jnp.where(bottom, 0, 3) + 3 - jnp.where(top, same, 0))

    @pl.when(inner)
    def _():
        to_north.start()

    for g, k in every:
        south_buf[pl.ds(SLIM * number(g, k), SLIM), :] = plane_at(0, SLIM)(g, k)

    @pl.when(raised)
    def _():
        to_south.start()

    for i in range(PARTS):
        plane = plane_at(i * PIECE, PIECE)
        east_buf[pl.ds(i * PIECE, PIECE), :] = pack_wide(plane, PIECE)
        to_east[i].start()
        west_buf[pl.ds(i * PIECE, PIECE), :] = pack_slim(plane, PIECE)
        to_west[i].start()

    @pl.when(inner)
    def _():
        to_ne.start()
        to_nw.start()

    @pl.when(raised)
    def _():
        to_se.start()
        to_sw.start()

    @pl.when(top)
    def _():
        to_fold.start()

        @pl.when(fold_up != z)
        def _():
            to_fold_up.start()

        @pl.when(fold_up == z)
        def _():
            keep_fold_up.start()

        @pl.when(fold_down != z)
        def _():
            to_fold_down.start()

        @pl.when(fold_down == z)
        def _():
            keep_fold_down.start()

    def prepare(first, here, there):
        for c, x in enumerate(coefficients(hx_ref[here, :], hy_ref[here, :], f_ref[here, :])):
            coef_main[c, there, :] = x
        plane = plane_at(first, PREPARE)
        for g in range(8):
            x = pack_own(plane, g, PREPARE)
            if g < 4:
                edge[0, g, there, :] = x
            elif g == 4:
                mask_edge[2, there, :] = x
            else:
                metric_edge[g - 5, there, :] = x

    sweep(prepare, PREPARE)

    def step_rows(n, start, rows, state, flux, mask, coef, levels, align=True):
        def at_row(dj):
            first = OFF + start + dj
            if dj == 0 and align:
                first = pl.multiple_of(first, 8)
            return pl.ds(first, rows)

        def load(g, k, dj):
            return state[n, levels * g + k, at_row(dj), :]

        def keep(g, k, x):
            if g < 4:
                state[n + 1, levels * g + k, at_row(0), :] = x
                return None
            flux[n, levels * (g - 4) + k, at_row(0), :] = x
            return flux[n, levels * (g - 4) + k, at_row(-1), :]

        def masks(k):
            return [mask[levels * i + k, at_row(0), :] for i in range(3)]

        advance(load, lambda c: coef[c, at_row(0), :], masks, keep, N - 1, 1, rows, levels)

    def interior(n, carry):
        def chunk(i, inside):
            step_rows(n, i * CHUNK, CHUNK, main, flux_main, mask_main, coef_main, LEVELS)
            return inside

        return lax.fori_loop(0, N // CHUNK, chunk, carry)

    lax.fori_loop(0, STEPS, interior, 0)

    halo = pl.ds(OFF - 8, 8)

    @pl.when(raised)
    def _():
        to_north.wait_recv()
        to_ne.wait_recv()
        to_nw.wait_recv()
        last = pl.ds(OFF - WIDE, WIDE)
        for g, k in every:
            x = from_south[pl.ds(WIDE * number(g, k), WIDE), :]
            if g < 4:
                main[0, 3 * g + k, last, :] = x
            elif g == 4:
                mask_main[6 + k, last, :] = x
            else:
                metric_main[g - 5, pl.ds(8 - WIDE, WIDE), :] = x

    @pl.when(bottom)
    def _():
        zero = jnp.zeros((8, N), jnp.float32)
        for g, k in every:
            if g < 4:
                main[0, 3 * g + k, halo, :] = zero
            elif g == 4:
                mask_main[6 + k, halo, :] = zero
            else:
                metric_main[g - 5, :, :] = zero + 1.0
        for i in (0, 1):
            from_corner[i, :, :] = zero

    for k in range(LEVELS):
        mc = mask_main[6 + k, halo, :]
        mask_main[k, halo, :] = mc * turned(mc, N - 1)
        mask_main[3 + k, halo, :] = mc * mask_main[6 + k, pl.ds(OFF - 7, 8), :]
    for c, x in enumerate(coefficients(metric_main[0], metric_main[1], metric_main[2])):
        coef_main[c, halo, :] = x

    for c in to_east + to_west:
        c.wait_recv()

    def edge_keep(g, rows, x, offset=0):
        if g < 4:
            edge[0, g, rows, :] = x
        elif g == 4:
            mask_edge[2, rows, :] = x
        else:
            metric_edge[g - 5, rows, :] = x

    def south_plane(g, k):
        if g < 4:
            return main[0, 3 * g + k, halo, :]
        if g == 4:
            return mask_main[6 + k, halo, :]
        return metric_main[g - 5, :, :]

    for g in range(8):
        x = pack_own(south_plane, g, 8)
        x = merge_halo(x, from_corner[0], from_corner[1], g, 8)
        if g in (5, 6):
            x = jnp.where(bottom, 1.0, x)
        edge_keep(g, halo, x)

    def unpack(first, here, there):
        wide = from_west[here, :]
        slim = from_east[here, :]
        for g in range(8):
            if g < 4:
                x = edge[0, g, there, :]
            elif g == 4:
                x = mask_edge[2, there, :]
            else:
                x = metric_edge[g - 5, there, :]
            edge_keep(g, there, merge_halo(x, wide, slim, g, UNPACK))

    sweep(unpack, UNPACK)

    def edge_masks(start, rows):
        there = pl.ds(start, rows)
        mc = mask_edge[2, there, :]
        mask_edge[0, there, :] = mc * turned(mc, N - 1)
        mask_edge[1, there, :] = mc * mask_edge[2, pl.ds(start + 1, rows), :]

    def edge_ready(start, rows):
        there = pl.ds(start, rows)
        for c, x in enumerate(
            coefficients(metric_edge[0, there, :], metric_edge[1, there, :], metric_edge[2, there, :])
        ):
            coef_edge[c, there, :] = x

    edge_masks(OFF - 8, 8)
    edge_ready(OFF - 8, 8)

    def ready(first, here, there):
        edge_masks(OFF + first, READY)
        edge_ready(OFF + first, READY)

    sweep(ready, READY)

    strip = pl.ds(0, 8)
    for g, k in every:
        if g < 4:
            top_main[3 * g + k, strip, :] = jnp.zeros((8, N), jnp.float32)
        elif g == 4:
            mask_top_main[6 + k, strip, :] = jnp.zeros((8, N), jnp.float32)
        else:
            metric_top[g - 5, :, :] = jnp.ones((8, N), jnp.float32)

    def top_keep(g, k, first, x):
        rows = pl.ds(first, x.shape[0])
        if g < 4:
            top_main[3 * g + k, rows, :] = x
        elif g == 4:
            mask_top_main[6 + k, rows, :] = x
        else:
            metric_top[g - 5, pl.ds(first, x.shape[0]), :] = x

    @pl.when(inner)
    def _():
        to_south.wait_recv()
        to_se.wait_recv()
        to_sw.wait_recv()
        for g, k in every:
            top_keep(g, k, 0, from_north[pl.ds(SLIM * number(g, k), SLIM), :])

    @pl.when(top)
    def _():
        to_fold.wait_recv()

        @pl.when(fold_up != z)
        def _():
            to_fold_up.wait_recv()

        @pl.when(fold_up == z)
        def _():
            keep_fold_up.wait()

        @pl.when(fold_down != z)
        def _():
            to_fold_down.wait_recv()

        @pl.when(fold_down == z)
        def _():
            keep_fold_down.wait()

        for g, k in every:
            top_keep(g, k, 8 - WIDE, from_fold[pl.ds(WIDE * number(g, k), WIDE), :])
        for k in range(LEVELS):
            top_keep(1, k, 2, from_fold[pl.ds(90 + k, 1), :])

    east = jnp.where(top, 1, N - 1)
    west = jnp.where(top, N - 1, 1)

    def top_plane(g, k):
        if g < 4:
            return top_main[3 * g + k, strip, :]
        if g == 4:
            return mask_top_main[6 + k, strip, :]
        return metric_top[g - 5, :, :]

    edge_metric = []
    for g in range(8):
        x = merge_halo(pack_own(top_plane, g, 8), from_corner[2], from_corner[3], g, 8)
        if g < 4:
            top_edge[g, strip, :] = x
        elif g == 4:
            mask_top_edge[2, strip, :] = x
        else:
            edge_metric.append(x)
    for c, x in enumerate(coefficients(*edge_metric)):
        coef_top_edge[c, :, :] = x
    for c, x in enumerate(coefficients(metric_top[0], metric_top[1], metric_top[2])):
        coef_top_main[c, :, :] = x
    row = lax.broadcasted_iota(jnp.int32, (8, N), 0)
    mc = mask_edge[2, pl.ds(OFF + N - 8, 8), :]
    over = jnp.where(top, 1.0, pltpu.roll(mask_top_edge[2, strip, :], 7, 0))
    mask_edge[1, pl.ds(OFF + N - 8, 8), :] = mc * jnp.where(row == 7, over, pltpu.roll(mc, 7, 0))
    for mask, levels in ((mask_top_main, LEVELS), (mask_top_edge, 1)):
        for k in range(levels):
            mc = mask[2 * levels + k, strip, :]
            mask[k, strip, :] = mc * turned(mc, east)
            mask[levels + k, strip, :] = mc * jnp.where(row == 7, 1.0, pltpu.roll(mc, 7, 0))

    plain = [jnp.full((1, N), hinge[g], jnp.int32) == 0 for g in range(4)]

    first_row, last_row = row == 0, row == 7
    brim, under = pl.ds(OFF + N - 8, 8), pl.ds(OFF + N - 16, 8)

    def up(x):
        return pltpu.roll(x, 7, 0)

    def down(x):
        return pltpu.roll(x, 1, 0)

    kinds = (
        (LEVELS, main, flux_main, mask_main, mask_top_main, coef_main, coef_top_main),
        (1, edge, flux_edge, mask_edge, mask_top_edge, coef_edge, coef_top_edge),
    )

    def outer(n, carry):
        step_rows(n, n - WIDE, 8, main, flux_main, mask_main, coef_main, LEVELS, False)
        step_rows(n, -8, 8, edge, flux_edge, mask_edge, coef_edge, 1)
        step_rows(n, 0, N - 8, edge, flux_edge, mask_edge, coef_edge, 1)
        after = []
        for (levels, state, flux, mask, mask_beyond, coef, coef_beyond), (below, beyond) in zip(
            kinds, carry
        ):
            new_below, new_beyond, fluxes = [None] * len(below), [None] * len(beyond), {}

            def load_below(g, k, dj):
                c, z = below[levels * g + k], beyond[levels * g + k]
                if dj == 0:
                    return c
                if dj < 0:
                    return jnp.where(first_row, down(state[n, levels * g + k, under, :]), down(c))
                ghost = SIGN[g] * jnp.where(plain[g], z, down(turned(z, 1)))
                return jnp.where(last_row, jnp.where(top, ghost, up(z)), up(c))

            def load_beyond(g, k, dj):
                c, z = below[levels * g + k], beyond[levels * g + k]
                if dj == 0:
                    return z
                if dj < 0:
                    return jnp.where(first_row, down(c), down(z))
                ghost = SIGN[g] * jnp.where(plain[g], c, down(turned(c, N - 1)))
                return jnp.where(last_row, ghost, up(z))

            def keep_below(g, k, x):
                if g < 4:
                    new_below[levels * g + k] = x
                    return None
                fluxes[g, k] = down(x)
                return jnp.where(
                    first_row, down(flux[n, levels * (g - 4) + k, under, :]), fluxes[g, k]
                )

            def keep_beyond(g, k, x):
                if g < 4:
                    new_beyond[levels * g + k] = x
                    return None
                return jnp.where(first_row, fluxes[g, k], down(x))

            def masks(k):
                return [mask[levels * i + k, brim, :] for i in range(3)]

            def masks_beyond(k):
                return [mask_beyond[levels * i + k, strip, :] for i in range(3)]

            advance(load_below, lambda c: coef[c, brim, :], masks, keep_below, N - 1, 1, 8, levels)
            advance(
                load_beyond, lambda c: coef_beyond[c], masks_beyond, keep_beyond, east, west, 8, levels
            )
            if levels == 1:
                for i, x in enumerate(new_below):
                    state[n + 1, i, brim, :] = x
            after.append((tuple(new_below), tuple(new_beyond)))
        return tuple(after)

    start = tuple(
        (
            tuple(state[0, i, brim, :] for i in range(4 * levels)),
            tuple(beyond[i, strip, :] for i in range(4 * levels)),
        )
        for levels, state, beyond in ((LEVELS, main, top_main), (1, edge, top_edge))
    )
    done = lax.fori_loop(0, STEPS, outer, start)
    for i, x in enumerate(done[0][0]):
        main[STEPS, i, brim, :] = x

    inside = pl.ds(OFF, N)
    for i in range(4 * LEVELS):
        main_out[i, :, :] = main[STEPS, i, inside, :]
    for i in range(4):
        edge_out[i, :, :] = edge[STEPS, i, inside, :]

    for c in to_east + to_west:
        c.wait_send()

    @pl.when(inner)
    def _():
        for c in (to_north, to_ne, to_nw):
            c.wait_send()

    @pl.when(raised)
    def _():
        for c in (to_south, to_se, to_sw):
            c.wait_send()

    @pl.when(top)
    def _():
        to_fold.wait_send()

        @pl.when(fold_up != z)
        def _():
            to_fold_up.wait_send()

        @pl.when(fold_down != z)
        def _():
            to_fold_down.wait_send()


def deliver(main_ref, edge_ref, u_out, v_out, t_out, s_out, held, sem):
    lane = lanes((N, N))
    copies = []
    for g, out in enumerate((u_out, v_out, t_out, s_out)):
        x = edge_ref[g]
        for k in range(LEVELS):
            y = main_ref[3 * g + k]
            y = jnp.where(lane < WIDE, turned(x, -(GROUP * k + WEST_OWN)), y)
            sides = turned(x, N - SLIM - (GROUP * k + EAST_HALO - SLIM))
            held[3 * g + k, :, :] = jnp.where(lane >= N - SLIM, sides, y)
        c = pltpu.make_async_copy(held.at[pl.ds(3 * g, LEVELS)], out, sem.at[g])
        c.start()
        copies.append(c)
    for c in copies:
        c.wait()


def per_device(u, v, t, s, hx, hy, f, cell, zonal, merid, hinge):
    def buf(*shape):
        return pltpu.VMEM(shape + (N,), jnp.float32)

    vmem = pl.BlockSpec(memory_space=pltpu.VMEM)
    shape = jax.ShapeDtypeStruct((LEVELS, N, N), jnp.float32)
    results = pl.pallas_call(
        kernel,
        out_shape=(
            pltpu.VMEM((4 * LEVELS, N, N), jnp.float32),
            pltpu.VMEM((4, N, N), jnp.float32),
        ),
        in_specs=[pl.BlockSpec(memory_space=pltpu.HBM)] * 11,
        out_specs=(vmem,) * 2,
        scratch_shapes=[buf(LEVELS, N)] * 4
        + [buf(N)] * 3
        + [pltpu.VMEM((LEVELS, N, N), jnp.int32)] * 3
        + [pltpu.SMEM((4,), jnp.int32)]
        + [
            buf(5, 12, ROWS),
            buf(5, 4, ROWS),
            buf(12, 8),
            buf(4, 8),
            buf(4, 6, ROWS),
            buf(4, 2, ROWS),
            buf(9, ROWS),
            buf(3, ROWS),
            buf(9, 8),
            buf(3, 8),
            buf(3, 8),
            buf(3, 8),
            buf(3, ROWS),
            buf(11, ROWS),
            buf(11, ROWS),
            buf(11, 8),
            buf(11, 8),
            buf(N),
            buf(N),
            buf(96),
            buf(72),
            buf(18, 8),
            buf(8),
            buf(8),
            buf(N),
            buf(N),
            buf(96),
            buf(72),
            buf(96),
            buf(4, 8),
            pltpu.SemaphoreType.DMA((11 + 2 * PARTS,)),
            pltpu.SemaphoreType.DMA((11 + 2 * PARTS,)),
            pltpu.SemaphoreType.DMA((2,)),
            pltpu.SemaphoreType.DMA((11,)),
        ],
        compiler_params=pltpu.CompilerParams(
            collective_id=0, has_side_effects=True, vmem_limit_bytes=60 * 1024 * 1024
        ),
        name="halo_steps",
    )(u, v, t, s, hx, hy, f, cell, zonal, merid, hinge)


    return pl.pallas_call(
        deliver,
        out_shape=(shape,) * 4,
        in_specs=[vmem] * 2,
        out_specs=(pl.BlockSpec(memory_space=pl.ANY),) * 4,
        scratch_shapes=[buf(4 * LEVELS, N), pltpu.SemaphoreType.DMA((4,))],
        name="deliver",
    )(*(pltpu.with_memory_space_constraint(r, pltpu.VMEM) for r in results))


def solution(mesh):
    field, plain = P(None, "merid", "zonal"), P("merid", "zonal")
    return jax.shard_map(
        per_device,
        mesh=mesh,
        in_specs=(field,) * 4 + (plain,) * 3 + (field,) * 3 + (P(),),
        out_specs=(field,) * 4,
        check_vma=False,
    )
```
